32 devices in a mesh: groups: 2 (over x), gy: 16 (over z, y, core).
Axes of the slice: x: 2, y: 2, z: 4, core: 2. Of those that a mesh axis runs over, the one named last changes fastest.
Arguments:
- observed: float32 [2048, 16, 256], P(('groups', 'gy')), parts along dimension 0, may hold values from -6 to 6
- tf_table: float32 [16], replicated, may hold values from 0.2 to 2
- tilt_index: int32 [513, 129], replicated, may hold values from 0 to 15
- wedge: int32 [513, 129], replicated, may hold values 0 or 1
Outputs:
- restored: float32 [2048, 16, 256], P(('groups', 'gy')), parts along dimension 0
The draws below stay inside these ranges and needn't reach their ends.
There are 2 independent parts, one for each index of `groups`. The reference program is written for one: setup_inputs(seed, part) draws one part's arguments, and reference() takes and returns one part's arrays. A program takes and returns all parts, laid end to end along the dimension named above; an argument that names none is the same for every part. Nothing has to cross between parts.
All inputs are finite; a program needn't handle non-finite values.
Results may differ from the reference program's by a relative error of at most 0.00011.
Values sent between devices are 32-bit elements; how exact they have to be, the bound alone decides.
No kernel may reach another device: no remote copies, remote signals or barrier semaphores. Data moves between devices by JAX's collectives and lax.ppermute only.
A program may use at most 64 MiB of HBM per device.

```python
import math
import jax
import jax.numpy as jnp
from jax import lax

NX = 1024
NZ = 256
LEVELS = 16
OUTER = 2
PASSES = 2
NY = 16
NXH = 513
NZH = 129


def with_ends(values, own_key, smallest, top_value):
    shape = values.shape
    place = [jax.random.randint(jax.random.fold_in(own_key, axis), (), 0, shape[axis]) for axis in range(len(shape))]
    values = values.at[tuple(place)].set(smallest)
    longest = shape.index(max(shape))
    place[longest] = (place[longest] + 1) % shape[longest]
    return values.at[tuple(place)].set(top_value)


def block_levels(key, extent, cuts, least, top_value):
    loudness, own = 1.0, jax.random.fold_in(key, 6)
    for dim, shards_of in cuts:
        draws = jnp.exp(jax.random.uniform(jax.random.fold_in(own, dim), (shards_of,), jnp.float32, least / len(cuts), top_value / len(cuts)))
        loudness = loudness * jnp.repeat(draws, extent[dim] // shards_of).reshape([-1 if axis == dim else 1 for axis in range(len(extent))])
    return loudness


def bell_draw(own_key, extent, scale, reach, cuts=(), kind=jnp.bfloat16):
    level = block_levels(own_key, extent, cuts, -0.22, 0.18) if cuts else 1.0
    array = jax.random.normal(own_key, extent, jnp.float32) * scale * level
    return jnp.minimum(jnp.maximum(array, -reach), reach).astype(kind)


def setup_inputs(seed: int = 0, part: int = 0) -> dict:
    splits = jax.random.split(jax.random.key(seed), 5)
    part_keys = jax.random.split(jax.random.fold_in(splits[4], part), 5)
    return {
        "observed": bell_draw(part_keys[0], (NX, NY, NZ), 1.0, 6.0, ((0, 16),), jnp.float32),
        "tf_table": jnp.clip(jnp.exp(jax.random.uniform(splits[1], (LEVELS,), jnp.float32, math.log(0.2), math.log(2.0))), 0.2, 2.0),
        "tilt_index": with_ends(jax.random.randint(splits[2], (NXH, NZH), 0, LEVELS), jax.random.fold_in(splits[2], 1), 0, LEVELS - 1).astype(jnp.int32),
        "wedge": with_ends((jax.random.randint(splits[3], (NXH, NZH), 0, 4) < 3).astype(jnp.int32), jax.random.fold_in(splits[3], 1), 0, 1),
    }


step_dual = 0.14
step_primal = 0.14
huber_eps = 0.05
bound_dual = 0.5

def curvature(field, axis):
    widths = [(0, 0), (0, 0), (0, 0)]
    widths[axis] = (1, 1)
    padded = jnp.pad(field, widths)
    upper = lax.slice_in_dim(padded, 2, padded.shape[axis], axis=axis)
    lower = lax.slice_in_dim(padded, 0, padded.shape[axis] - 2, axis=axis)
    return upper + lower - 2.0 * field

def denoise(target, duals):
    field = target
    lead = target
    for sweep in range(PASSES):
        raised = [(duals[axis] + step_dual * curvature(lead, axis)) / (1.0 + step_dual * huber_eps / bound_dual) for axis in range(3)]
        total = raised[0] * raised[0] + raised[1] * raised[1] + raised[2] * raised[2]
        shrink = jnp.sqrt(jnp.maximum(1.0, total / (bound_dual * bound_dual)))
        duals = (raised[0] / shrink, raised[1] / shrink, raised[2] / shrink)
        adjoint = curvature(duals[0], 0) + curvature(duals[1], 1) + curvature(duals[2], 2)
        updated = (field - step_primal * adjoint + step_primal * target) / (1.0 + step_primal)
        lead = 2.0 * updated - field
        field = updated
    return (field, duals)

def reference(observed, tf_table, tilt_index, wedge):
    half_rows = tf_table[tilt_index] * wedge.astype(tf_table.dtype)
    response = jnp.concatenate([half_rows, half_rows[NX // 2 - 1:0:-1]], 0)
    denom = response * response + 1.0
    g_data = (response / denom)[:, None, :]
    g_prior = (1.0 / denom)[:, None, :]
    spectrum = jnp.fft.rfft2(observed, axes=(0, 2))
    current = observed
    duals = (jnp.zeros_like(observed), jnp.zeros_like(observed), jnp.zeros_like(observed))
    for outer in range(OUTER):
        mixed = g_data * spectrum + g_prior * jnp.fft.rfft2(current, axes=(0, 2))
        target = jnp.fft.irfft2(mixed, s=(NX, NZ), axes=(0, 2)).astype(observed.dtype)
        current, duals = denoise(target, duals)
    return current
```

```python
import functools

import jax
import jax.numpy as jnp
import ml_dtypes
import numpy as np
from jax import lax
from jax.experimental import pallas as pl
from jax.experimental.pallas import tpu as pltpu
from jax.sharding import PartitionSpec as P

OUTER = 2
PASSES = 2

step_dual = 0.14
step_primal = 0.14
huber_eps = 0.05
bound_dual = 0.5

SUB = 8
LANE = 128
HALO_LAST = 4
HALO_FIRST = 8
VMEM_LIMIT = 48 * 1024 * 1024

f32 = jnp.float32
bf16 = jnp.bfloat16


def halves(table):
    high = table.astype(ml_dtypes.bfloat16)
    low = (table - high.astype(np.float64)).astype(ml_dtypes.bfloat16)
    return np.stack([high, low])


def cas(rows, columns, length):
    phase = (rows[:, None] * columns[None, :]) % length
    angle = phase * (2.0 * np.pi / length)
    return np.cos(angle) + np.sin(angle)


def z_table(length):
    index = np.arange(length)
    return halves(cas(index, index, length))


def x_tables(length):
    half = length // 2
    place = np.arange(half)
    even = cas(2 * place, place, length)
    odd = cas(2 * place + 1, place, length)
    return np.stack([halves(even), halves(odd), halves(odd.T)])


def kx_order(length):
    full = np.concatenate([np.arange(0, length, 2), np.arange(1, length, 2)])
    return np.minimum(full, length - full)


def kz_order(length):
    full = np.arange(length)
    return np.minimum(full, length - full)


def filters(tf_table, tilt_index, wedge, nx, nz):
    levels = tf_table.shape[0]
    code = jnp.where(wedge > 0, tilt_index + 1, 0).astype(bf16)
    pick_x = np.zeros((nx, tilt_index.shape[0]), ml_dtypes.bfloat16)
    pick_x[np.arange(nx), kx_order(nx)] = 1
    pick_z = np.zeros((tilt_index.shape[1], nz), ml_dtypes.bfloat16)
    pick_z[kz_order(nz), np.arange(nz)] = 1
    wide = jnp.dot(code, pick_z, preferred_element_type=f32).astype(bf16)
    spread = jnp.dot(pick_x, wide, preferred_element_type=f32)
    response = jnp.zeros_like(spread)
    for level in range(levels):
        response = jnp.where(spread == level + 1.0, tf_table[level], response)
    scale = 1.0 / (nx * nz)
    prior = scale / (response * response + 1.0)
    data = response * prior
    return data + prior, data, prior


def split(value):
    high = value.astype(bf16)
    return high, (value - high.astype(f32)).astype(bf16)


def dot3(a, b):
    dot = functools.partial(jnp.dot, preferred_element_type=f32)
    return dot(a[0], b[0]) + (dot(a[0], b[1]) + dot(a[1], b[0]))


def filter_kernel(first, halo, *refs):
    if first:
        (cells, ztab, xtab, both, data, windows, kept, waves, high, low, padded) = refs
    else:
        (cells, ztab, xtab, kept, prior, windows, waves, high, low, padded) = refs
    devices, _, slab, nz = cells.shape
    nx = devices * slab
    half = nx // 2
    tile = min(256, half)
    ztable = (ztab[0], ztab[1])
    flat = cells[:, 0].reshape(nx, nz)
    for top in range(0, half, tile):
        a = dot3(split(flat[top : top + tile]), ztable)
        b = dot3(split(flat[half + top : half + top + tile]), ztable)
        for spot, value in ((top, a + b), (half + top, a - b)):
            high[spot : spot + tile], low[spot : spot + tile] = split(value)
    for part in range(2):
        base = part * half
        folded = (high[base : base + half], low[base : base + half])
        for top in range(0, half, tile):
            rows = slice(base + top, base + top + tile)
            table = (xtab[part, 0, top : top + tile], xtab[part, 1, top : top + tile])
            wave = dot3(table, folded)
            if first:
                waves[rows] = wave * both[rows]
                kept[0, rows] = wave * data[rows]
            else:
                waves[rows] = kept[0, rows] + wave * prior[rows]
    for top in range(0, nx, tile):
        rows = slice(top, top + tile)
        high[rows], low[rows] = split(waves[rows])
    even = (high[:half], low[:half])
    odd = (high[half:], low[half:])
    padded[:SUB] = jnp.zeros((SUB, nz), f32)
    padded[halo + nx - halo % SUB : halo + nx - halo % SUB + SUB] = jnp.zeros((SUB, nz), f32)
    for top in range(0, half, tile):
        e = dot3((xtab[0, 0, top : top + tile], xtab[0, 1, top : top + tile]), even)
        o = dot3((xtab[2, 0, top : top + tile], xtab[2, 1, top : top + tile]), odd)
        padded[halo + top : halo + top + tile] = dot3(split(e + o), ztable)
        padded[halo + half + top : halo + half + top + tile] = dot3(split(e - o), ztable)
    width = slab + 2 * halo
    for device in range(devices):
        windows[device, 0] = padded[device * slab : device * slab + width]


def run_filter(first, halo, cells, tables, weights):
    devices, rows, slab, nz = cells.shape
    nx = devices * slab
    width = slab + 2 * halo
    ztab, xtab = tables

    def whole(array):
        return pl.BlockSpec(array.shape, lambda r: (0,) * array.ndim)

    def per_row(planes):
        return pl.BlockSpec((devices, 1, planes, nz), lambda r: (0, r, 0, 0))

    kept_spec = pl.BlockSpec((1, nx, nz), lambda r: (r, 0, 0))
    windows_shape = jax.ShapeDtypeStruct((devices, rows, width, nz), f32)
    kept_shape = jax.ShapeDtypeStruct((rows, nx, nz), f32)
    in_specs = [per_row(slab), whole(ztab), whole(xtab)]
    if first:
        in_specs += [whole(weights[0]), whole(weights[1])]
        out_specs, out_shape = [per_row(width), kept_spec], [windows_shape, kept_shape]
    else:
        in_specs += [kept_spec, whole(weights[1])]
        out_specs, out_shape = per_row(width), windows_shape
    flops = 3 * 2 * rows * (2 * nx * nz * nz + nx * nx * nz)
    return pl.pallas_call(
        functools.partial(filter_kernel, first, halo),
        grid=(rows,),
        in_specs=in_specs,
        out_specs=out_specs,
        out_shape=out_shape,
        scratch_shapes=[
            pltpu.VMEM((nx, nz), f32),
            pltpu.VMEM((nx, nz), bf16),
            pltpu.VMEM((nx, nz), bf16),
            pltpu.VMEM((nx + 2 * SUB, nz), f32),
        ],
        compiler_params=pltpu.CompilerParams(vmem_limit_bytes=VMEM_LIMIT),
        cost_estimate=pl.CostEstimate(
            flops=flops, bytes_accessed=8 * 1024 * 1024, transcendentals=0
        ),
    )(cells, ztab, xtab, *weights)


def lane_bends(pieces):
    lane = lax.broadcasted_iota(jnp.int32, pieces[0].shape, 1)
    up = [pltpu.roll(piece, LANE - 1, 1) for piece in pieces]
    down = [pltpu.roll(piece, 1, 1) for piece in pieces]
    bends = []
    for k, piece in enumerate(pieces):
        above = up[k + 1] if k + 1 < len(pieces) else 0.0
        below = down[k - 1] if k > 0 else 0.0
        upper = jnp.where(lane == LANE - 1, above, up[k])
        lower = jnp.where(lane == 0, below, down[k])
        bends.append(upper + lower - 2.0 * piece)
    return bends


def row_bends(groups):
    row = lax.broadcasted_iota(jnp.int32, groups[0].shape, 0)
    up = [pltpu.roll(group, SUB - 1, 0) for group in groups]
    down = [pltpu.roll(group, 1, 0) for group in groups]
    count = len(groups)
    bends = []
    for g, group in enumerate(groups):
        upper = jnp.where(row == SUB - 1, up[(g + 1) % count], up[g])
        lower = jnp.where(row == 0, down[g - 1], down[g])
        bends.append(upper + lower - 2.0 * group)
    return bends


def passes_kernel(first, last, halo, slab, nx, start_ref, target, *refs):
    if first:
        duals_in, refs = None, refs
    else:
        duals_in, refs = refs[:3], refs[3:]
    if last:
        restored, refs = refs[0], refs[1:]
    else:
        current, duals_out, refs = refs[0], refs[1:4], refs[4:]
    lead, field, dual_x, dual_y, dual_z = refs[:5]
    turned = refs[5:]
    ny, width, nz = target.shape
    groups = width // SUB
    blocks = nz // LANE
    decay = 1.0 / (1.0 + step_dual * huber_eps / bound_dual)
    gain = step_dual * decay
    origin = start_ref[0] - halo

    def inside(g):
        if SUB * g >= halo and SUB * (g + 1) <= width - halo:
            return None
        place = origin + SUB * g + lax.broadcasted_iota(jnp.int32, (SUB, LANE), 0)
        return (place >= 0) & (place < nx)

    def masked(value, g):
        mask = inside(g)
        return value if mask is None else jnp.where(mask, value, 0.0)

    def at(g, k):
        return pl.ds(SUB * g, SUB), pl.ds(LANE * k, LANE)

    empty = jnp.zeros((width, nz), f32)
    for plane in (0, ny + 1):
        lead[plane] = empty
        dual_y[plane] = empty

    @pl.loop(0, ny)
    def _(y):
        lead[y + 1] = target[y]

    for sweep in range(PASSES):
        if sweep > 0:
            before = (lambda y: (dual_x, y)), (lambda y: (dual_y, y + 1)), (lambda y: (dual_z, y))
        elif duals_in is not None:
            before = tuple((lambda y, ref=ref: (ref, y)) for ref in duals_in)
        else:
            before = None
        final = sweep == PASSES - 1

        @pl.loop(0, ny)
        def _(y):
            here = [[lead[(y + 1,) + at(g, k)] for k in range(blocks)] for g in range(groups)]
            columns = [row_bends([here[g][k] for g in range(groups)]) for k in range(blocks)]
            for g in range(groups):
                along_z = lane_bends(here[g])
                for k in range(blocks):
                    spot = at(g, k)
                    along_y = lead[(y,) + spot] + lead[(y + 2,) + spot] - 2.0 * here[g][k]
                    raised = [gain * columns[k][g], gain * along_y, gain * along_z[k]]
                    if before is not None:
                        for a in range(3):
                            ref, plane = before[a](y)
                            raised[a] = raised[a] + decay * ref[(plane,) + spot]
                    total = (
                        raised[0] * raised[0] + raised[1] * raised[1] + raised[2] * raised[2]
                    )
                    shrink = lax.rsqrt(
                        jnp.maximum(1.0, total * (1.0 / (bound_dual * bound_dual)))
                    )
                    made = [raised[0] * masked(shrink, g), raised[1] * shrink, raised[2] * shrink]
                    dual_x[(y,) + spot] = made[0]
                    dual_y[(y + 1,) + spot] = made[1]
                    dual_z[(y,) + spot] = made[2]
                    if final and not last:
                        shift = halo - HALO_LAST
                        kept_rows = slab + 2 * HALO_LAST
                        lo = max(0, shift - SUB * g)
                        hi = min(SUB, kept_rows + shift - SUB * g)
                        if lo < hi:
                            rows = pl.ds(SUB * g + lo - shift, hi - lo)
                            for a in range(3):
                                duals_out[a][y, rows, spot[1]] = made[a][lo:hi]

        @pl.loop(0, ny)
        def _(y):
            wanted = range(groups)
            if final:
                wanted = [
                    g for g in wanted if SUB * (g + 1) > halo and SUB * g < width - halo
                ]
            near = [[dual_x[(y,) + at(g, k)] for k in range(blocks)] for g in range(groups)]
            columns = [row_bends([near[g][k] for g in range(groups)]) for k in range(blocks)]
            for g in wanted:
                along_z = lane_bends([dual_z[(y,) + at(g, k)] for k in range(blocks)])
                for k in range(blocks):
                    spot = at(g, k)
                    along_y = (
                        dual_y[(y,) + spot]
                        + dual_y[(y + 2,) + spot]
                        - 2.0 * dual_y[(y + 1,) + spot]
                    )
                    adjoint = columns[k][g] + along_y + along_z[k]
                    goal = target[(y,) + spot]
                    if sweep == 0:
                        old = goal
                        updated = goal - (step_primal / (1.0 + step_primal)) * adjoint
                    else:
                        old = field[(y,) + spot]
                        updated = (old + step_primal * (goal - adjoint)) * (
                            1.0 / (1.0 + step_primal)
                        )
                    if not final:
                        field[(y,) + spot] = updated
                        lead[(y + 1,) + spot] = masked(2.0 * updated - old, g)
                        continue
                    lo = max(0, halo - SUB * g)
                    hi = min(SUB, slab + halo - SUB * g)
                    x = SUB * g + lo - halo
                    if last:
                        turned[k][pl.ds(x * ny + y, hi - lo, stride=ny), :] = updated[lo:hi]
                    else:
                        current[y, pl.ds(x, hi - lo), spot[1]] = updated[lo:hi]

    for k, block in enumerate(turned):
        restored[:, LANE * k : LANE * (k + 1)] = block[:]


def run_passes(first, last, halo, slab, start, target, duals):
    ny, width, nz = target.shape
    nx = slab * lax.axis_size("gy")
    vmem = pl.BlockSpec(memory_space=pltpu.VMEM)
    if last:
        out_shape = jax.ShapeDtypeStruct((slab * ny, nz), f32)
        out_specs = vmem
    else:
        kept = jax.ShapeDtypeStruct((ny, slab + 2 * HALO_LAST, nz), f32)
        out_shape = [jax.ShapeDtypeStruct((ny, slab, nz), f32), kept, kept, kept]
        out_specs = [vmem] * 4
    return pl.pallas_call(
        functools.partial(passes_kernel, first, last, halo, slab, nx),
        in_specs=[pl.BlockSpec(memory_space=pltpu.SMEM)] + [vmem] * (1 + len(duals)),
        out_specs=out_specs,
        out_shape=out_shape,
        scratch_shapes=[
            pltpu.VMEM((ny + 2, width, nz), f32),
            pltpu.VMEM((ny, width, nz), f32),
            pltpu.VMEM((ny, width, nz), f32),
            pltpu.VMEM((ny + 2, width, nz), f32),
            pltpu.VMEM((ny, width, nz), f32),
        ]
        + [pltpu.VMEM((slab * ny, LANE), f32)] * (nz // LANE if last else 0),
        compiler_params=pltpu.CompilerParams(vmem_limit_bytes=VMEM_LIMIT),
        cost_estimate=pl.CostEstimate(
            flops=120 * ny * width * nz,
            bytes_accessed=8 * 4 * ny * width * nz,
            transcendentals=PASSES * ny * width * nz,
        ),
    )(start, target, *duals)


def exchange(blocks):
    return lax.all_to_all(blocks, "gy", split_axis=0, concat_axis=0, tiled=True)


def local(observed, tf_table, tilt_index, wedge):
    slab, ny, nz = observed.shape
    devices = lax.axis_size("gy")
    rows = ny // devices
    nx = slab * devices
    start = (lax.axis_index("gy") * slab).astype(jnp.int32).reshape(1)
    tables = (jnp.asarray(z_table(nz)), jnp.asarray(x_tables(nx)))
    cells = exchange(observed.transpose(1, 0, 2).reshape(devices, rows, slab, nz))
    both, data, prior = filters(tf_table, tilt_index, wedge, nx, nz)
    duals = ()
    for outer in range(OUTER):
        first, last = outer == 0, outer == OUTER - 1
        halo = HALO_LAST if last else HALO_FIRST
        if first:
            windows, kept = run_filter(True, halo, cells, tables, (both, data))
        else:
            windows = run_filter(False, halo, cells, tables, (kept, prior))
        target = exchange(windows).reshape(ny, slab + 2 * halo, nz)
        made = run_passes(first, last, halo, slab, start, target, duals)
        if last:
            return made.reshape(slab, ny, nz)
        duals = tuple(made[1:])
        cells = exchange(made[0].reshape(devices, rows, slab, nz))


def solution(mesh):
    in_specs = (P(("groups", "gy"), None, None), P(), P(), P())
    out_specs = P(("groups", "gy"), None, None)
    return jax.shard_map(local, mesh=mesh, in_specs=in_specs, out_specs=out_specs, check_vma=False)
```

```python
import functools

import jax
import jax.numpy as jnp
import ml_dtypes
import numpy as np
from jax import lax
from jax.experimental import pallas as pl
from jax.experimental.pallas import tpu as pltpu
from jax.sharding import PartitionSpec as P

OUTER = 2
PASSES = 2

step_dual = 0.14
step_primal = 0.14
huber_eps = 0.05
bound_dual = 0.5

SUB = 8
LANE = 128
HALO_LAST = 4
HALO_FIRST = 8
MIB = 1024 * 1024

f32 = jnp.float32
bf16 = jnp.bfloat16


def halves(table):
    high = table.astype(ml_dtypes.bfloat16)
    low = (table - high.astype(np.float64)).astype(ml_dtypes.bfloat16)
    return np.stack([high, low])


def cas(rows, columns, length):
    phase = (rows[:, None] * columns[None, :]) % length
    angle = phase * (2.0 * np.pi / length)
    return np.cos(angle) + np.sin(angle)


def z_table(length):
    index = np.arange(length)
    return halves(cas(index, index, length))


def x_tables(length, slab, chunks):
    half = length // 2
    place = np.arange(half)
    forward = []
    for chunk in range(chunks):
        cells = place[place % slab // (slab // chunks) == chunk]
        forward.append(
            np.stack(
                [halves(cas(2 * place, cells, length)), halves(cas(2 * place + 1, cells, length))]
            )
        )
    inverse = np.stack(
        [halves(cas(place, 2 * place, length)), halves(cas(place, 2 * place + 1, length))]
    )
    return forward, inverse


def padded_to(length, unit):
    return -(-length // unit) * unit


def weights_kernel(nx, nz, levels, table_ref, code_ref, both, data, prior):
    half = nx // 2
    tile = min(256, half)
    heights, widths = code_ref.shape
    scale = 1.0 / (nx * nz)
    kz = lax.broadcasted_iota(jnp.int32, (heights, nz), 1)
    kz = jnp.minimum(kz, nz - kz)
    pick_z = jnp.where(kz == lax.broadcasted_iota(jnp.int32, (heights, nz), 0), 1.0, 0.0)
    pick_z = pick_z.astype(bf16)
    for part in range(2):
        for top in range(0, half, tile):
            kx = 2 * (top + lax.broadcasted_iota(jnp.int32, (tile, widths), 0)) + part
            kx = jnp.minimum(kx, nx - kx)
            pick_x = jnp.where(kx == lax.broadcasted_iota(jnp.int32, (tile, widths), 1), 1.0, 0.0)
            tall = lax.dot_general(
                pick_x.astype(bf16),
                code_ref[...],
                (((1,), (1,)), ((), ())),
                preferred_element_type=f32,
            )
            spread = jnp.dot(tall.astype(bf16), pick_z, preferred_element_type=f32)
            response = jnp.zeros_like(spread)
            for level in range(levels):
                response = jnp.where(spread == level + 1.0, table_ref[level], response)
            gain = scale / (response * response + 1.0)
            rows = slice(part * half + top, part * half + top + tile)
            prior[rows] = gain
            data[rows] = response * gain
            both[rows] = response * gain + gain


def make_weights(tf_table, tilt_index, wedge, nx, nz):
    levels = tf_table.shape[0]
    code = jnp.where(wedge > 0, tilt_index + 1, 0).T
    extra = [(0, padded_to(size, LANE) - size) for size in code.shape]
    code = jnp.pad(code, extra).astype(bf16)
    grid = jax.ShapeDtypeStruct((nx, nz), f32)
    vmem = pl.BlockSpec(memory_space=pltpu.VMEM)
    return pl.pallas_call(
        functools.partial(weights_kernel, nx, nz, levels),
        in_specs=[pl.BlockSpec(memory_space=pltpu.SMEM), vmem],
        out_specs=[vmem] * 3,
        out_shape=[grid] * 3,
        compiler_params=pltpu.CompilerParams(vmem_limit_bytes=16 * MIB),
        cost_estimate=pl.CostEstimate(
            flops=60 * nx * nz, bytes_accessed=12 * nx * nz, transcendentals=0
        ),
    )(tf_table, code)


def split(value):
    high = value.astype(bf16)
    return high, (value - high.astype(f32)).astype(bf16)


def dot3(a, b):
    dot = functools.partial(jnp.dot, preferred_element_type=f32)
    return dot(a[0], b[0]) + (dot(a[0], b[1]) + dot(a[1], b[0]))


def filter_kernel(first, opens, closes, halo, slab, *refs):
    cells, ztab, forward, refs = refs[0], refs[1], refs[2], refs[3:]
    if not opens:
        so_far, refs = refs[0], refs[1:]
    if closes:
        inverse, refs = refs[0], refs[1:]
        if first:
            both, data, refs = refs[0], refs[1], refs[2:]
        else:
            kept, prior, refs = refs[0], refs[1], refs[2:]
        count = len(refs) - (6 if first else 5)
        windows, refs = refs[:count], refs[count:]
        if first:
            kept, refs = refs[0], refs[1:]
        high, low, wave_high, wave_low, padded = refs
    else:
        sums, high, low = refs
    devices, rows, chunk, nz = cells.shape
    nx = devices * slab
    half = nx // 2
    folds = devices * chunk // 2
    ztable = (ztab[0], ztab[1])
    for r in range(rows):
        flat = cells[:, r].reshape(2 * folds, nz)
        tile = min(256, folds)
        for top in range(0, folds, tile):
            a = dot3(split(flat[top : top + tile]), ztable)
            b = dot3(split(flat[folds + top : folds + top + tile]), ztable)
            for spot, value in ((top, a + b), (folds + top, a - b)):
                high[spot : spot + tile], low[spot : spot + tile] = split(value)
        tile = min(256, half)
        for part in range(2):
            base = part * folds
            folded = (high[base : base + folds], low[base : base + folds])
            for top in range(0, half, tile):
                spot = slice(part * half + top, part * half + top + tile)
                table = (forward[part, 0, top : top + tile], forward[part, 1, top : top + tile])
                wave = dot3(table, folded)
                if not opens:
                    wave = so_far[r, spot] + wave
                if not closes:
                    sums[r, spot] = wave
                    continue
                if first:
                    mixed = wave * both[spot]
                    kept[r, spot] = wave * data[spot]
                else:
                    mixed = kept[r, spot] + wave * prior[spot]
                wave_high[spot], wave_low[spot] = split(mixed)
        if not closes:
            continue
        even = (wave_high[:half], wave_low[:half])
        odd = (wave_high[half:], wave_low[half:])
        after = halo + nx - halo % SUB
        padded[:SUB] = jnp.zeros((SUB, nz), f32)
        padded[after : after + SUB] = jnp.zeros((SUB, nz), f32)
        for top in range(0, half, tile):
            e = dot3((inverse[0, 0, top : top + tile], inverse[0, 1, top : top + tile]), even)
            o = dot3((inverse[1, 0, top : top + tile], inverse[1, 1, top : top + tile]), odd)
            padded[halo + top : halo + top + tile] = dot3(split(e + o), ztable)
            padded[halo + half + top : halo + half + top + tile] = dot3(split(e - o), ztable)
        for device in range(devices):
            spot = device * slab
            for window in windows:
                width = window.shape[2]
                window[device, r] = padded[spot : spot + width]
                spot += width


def start_filter(cells, tables, chunk, slab):
    devices, rows, size, nz = cells.shape
    nx = devices * slab
    ztab, forward, _ = tables
    vmem = pl.BlockSpec(memory_space=pltpu.VMEM)
    folds = devices * size
    return pl.pallas_call(
        functools.partial(filter_kernel, False, True, False, 0, slab),
        in_specs=[vmem] * 3,
        out_specs=vmem,
        out_shape=jax.ShapeDtypeStruct((rows, nx, nz), f32),
        scratch_shapes=[pltpu.VMEM((folds, nz), bf16), pltpu.VMEM((folds, nz), bf16)],
        compiler_params=pltpu.CompilerParams(vmem_limit_bytes=16 * MIB),
        cost_estimate=pl.CostEstimate(
            flops=6 * rows * folds * nz * (nz + nx // 2),
            bytes_accessed=4 * rows * nx * nz,
            transcendentals=0,
        ),
    )(cells, ztab, forward[chunk])


def finish_filter(first, halo, cells, so_far, tables, weights, chunk, slab, widths):
    devices, rows, size, nz = cells.shape
    nx = devices * slab
    ztab, forward, inverse = tables
    vmem = pl.BlockSpec(memory_space=pltpu.VMEM)
    folds = devices * size
    operands = [cells, ztab, forward[chunk]] + so_far + [inverse] + list(weights)
    out_shape = [jax.ShapeDtypeStruct((devices, rows, width, nz), f32) for width in widths]
    if first:
        out_shape.append(jax.ShapeDtypeStruct((rows, nx, nz), f32))
    return pl.pallas_call(
        functools.partial(filter_kernel, first, not so_far, True, halo, slab),
        in_specs=[vmem] * len(operands),
        out_specs=[vmem] * len(out_shape),
        out_shape=out_shape,
        scratch_shapes=[
            pltpu.VMEM((folds, nz), bf16),
            pltpu.VMEM((folds, nz), bf16),
            pltpu.VMEM((nx, nz), bf16),
            pltpu.VMEM((nx, nz), bf16),
            pltpu.VMEM((nx + 2 * SUB, nz), f32),
        ],
        compiler_params=pltpu.CompilerParams(vmem_limit_bytes=24 * MIB),
        cost_estimate=pl.CostEstimate(
            flops=6 * rows * nx * nz * (2 * nz + nx),
            bytes_accessed=8 * rows * nx * nz,
            transcendentals=0,
        ),
    )(*operands)


def lane_bends(pieces):
    lane = lax.broadcasted_iota(jnp.int32, pieces[0].shape, 1)
    up = [pltpu.roll(piece, LANE - 1, 1) for piece in pieces]
    down = [pltpu.roll(piece, 1, 1) for piece in pieces]
    bends = []
    for k, piece in enumerate(pieces):
        above = up[k + 1] if k + 1 < len(pieces) else 0.0
        below = down[k - 1] if k > 0 else 0.0
        upper = jnp.where(lane == LANE - 1, above, up[k])
        lower = jnp.where(lane == 0, below, down[k])
        bends.append(upper + lower - 2.0 * piece)
    return bends


def row_bends(groups):
    row = lax.broadcasted_iota(jnp.int32, groups[0].shape, 0)
    up = [pltpu.roll(group, SUB - 1, 0) for group in groups]
    down = [pltpu.roll(group, 1, 0) for group in groups]
    count = len(groups)
    bends = []
    for g, group in enumerate(groups):
        upper = jnp.where(row == SUB - 1, up[(g + 1) % count], up[g])
        lower = jnp.where(row == 0, down[g - 1], down[g])
        bends.append(upper + lower - 2.0 * group)
    return bends


def passes_kernel(first, last, chunk, halo, slab, nx, start_ref, *refs):
    pieces, refs = refs[: min(chunk, 1) + 1], refs[min(chunk, 1) + 1 :]
    if first:
        duals_in, refs = None, refs
    else:
        duals_in, refs = refs[:3], refs[3:]
    if last and chunk:
        before_this, refs = refs[:chunk], refs[chunk:]
    if last:
        restored, refs = refs[0], refs[1:]
    else:
        current, duals_out, refs = refs[0], refs[1:4], refs[4:]
    lead, field, dual_x, dual_y, dual_z = refs[:5]
    turned = refs[5:]
    ny, _, nz = pieces[0].shape
    width = slab + 2 * halo
    groups = width // SUB
    blocks = nz // LANE
    decay = 1.0 / (1.0 + step_dual * huber_eps / bound_dual)
    gain = step_dual * decay
    origin = start_ref[0] + chunk * slab - halo
    shared = 2 * halo if chunk else 0

    def goal_of(y, g, k):
        lanes = pl.ds(LANE * k, LANE)
        if SUB * g < shared:
            return pieces[0][y, pl.ds(pieces[0].shape[1] - shared + SUB * g, SUB), lanes]
        return pieces[-1][y, pl.ds(SUB * g - shared, SUB), lanes]

    def inside(g):
        if SUB * g >= halo and SUB * (g + 1) <= width - halo:
            return None
        place = origin + SUB * g + lax.broadcasted_iota(jnp.int32, (SUB, LANE), 0)
        return (place >= 0) & (place < nx)

    def masked(value, g):
        mask = inside(g)
        return value if mask is None else jnp.where(mask, value, 0.0)

    def at(g, k):
        return pl.ds(SUB * g, SUB), pl.ds(LANE * k, LANE)

    empty = jnp.zeros((width, nz), f32)
    for plane in (0, ny + 1):
        lead[plane] = empty
        dual_y[plane] = empty

    @pl.loop(0, ny)
    def _(y):
        if shared:
            lead[y + 1, :shared] = pieces[0][y, pieces[0].shape[1] - shared :]
        lead[y + 1, shared:] = pieces[-1][y]

    for sweep in range(PASSES):
        if sweep > 0:
            before = (lambda y: (dual_x, y)), (lambda y: (dual_y, y + 1)), (lambda y: (dual_z, y))
        elif duals_in is not None:
            before = tuple((lambda y, ref=ref: (ref, y)) for ref in duals_in)
        else:
            before = None
        final = sweep == PASSES - 1

        @pl.loop(0, ny)
        def _(y):
            here = [[lead[(y + 1,) + at(g, k)] for k in range(blocks)] for g in range(groups)]
            columns = [row_bends([here[g][k] for g in range(groups)]) for k in range(blocks)]
            for g in range(groups):
                along_z = lane_bends(here[g])
                for k in range(blocks):
                    spot = at(g, k)
                    along_y = lead[(y,) + spot] + lead[(y + 2,) + spot] - 2.0 * here[g][k]
                    raised = [gain * columns[k][g], gain * along_y, gain * along_z[k]]
                    if before is not None:
                        for a in range(3):
                            ref, plane = before[a](y)
                            raised[a] = raised[a] + decay * ref[(plane,) + spot]
                    total = (
                        raised[0] * raised[0] + raised[1] * raised[1] + raised[2] * raised[2]
                    )
                    shrink = lax.rsqrt(
                        jnp.maximum(1.0, total * (1.0 / (bound_dual * bound_dual)))
                    )
                    made = [raised[0] * masked(shrink, g), raised[1] * shrink, raised[2] * shrink]
                    dual_x[(y,) + spot] = made[0]
                    dual_y[(y + 1,) + spot] = made[1]
                    dual_z[(y,) + spot] = made[2]
                    if final and not last:
                        shift = halo - HALO_LAST
                        kept_rows = slab + 2 * HALO_LAST
                        lo = max(0, shift - SUB * g)
                        hi = min(SUB, kept_rows + shift - SUB * g)
                        if lo < hi:
                            rows = pl.ds(SUB * g + lo - shift, hi - lo)
                            for a in range(3):
                                duals_out[a][y, rows, spot[1]] = made[a][lo:hi]

        @pl.loop(0, ny)
        def _(y):
            wanted = range(groups)
            if final:
                wanted = [
                    g for g in wanted if SUB * (g + 1) > halo and SUB * g < width - halo
                ]
            near = [[dual_x[(y,) + at(g, k)] for k in range(blocks)] for g in range(groups)]
            columns = [row_bends([near[g][k] for g in range(groups)]) for k in range(blocks)]
            for g in wanted:
                along_z = lane_bends([dual_z[(y,) + at(g, k)] for k in range(blocks)])
                for k in range(blocks):
                    spot = at(g, k)
                    along_y = (
                        dual_y[(y,) + spot]
                        + dual_y[(y + 2,) + spot]
                        - 2.0 * dual_y[(y + 1,) + spot]
                    )
                    adjoint = columns[k][g] + along_y + along_z[k]
                    goal = goal_of(y, g, k)
                    if sweep == 0:
                        old = goal
                        updated = goal - (step_primal / (1.0 + step_primal)) * adjoint
                    else:
                        old = field[(y,) + spot]
                        updated = (old + step_primal * (goal - adjoint)) * (
                            1.0 / (1.0 + step_primal)
                        )
                    if not final:
                        field[(y,) + spot] = updated
                        lead[(y + 1,) + spot] = masked(2.0 * updated - old, g)
                        continue
                    lo = max(0, halo - SUB * g)
                    hi = min(SUB, slab + halo - SUB * g)
                    x = SUB * g + lo - halo
                    if last:
                        turned[k][pl.ds(x * ny + y, hi - lo, stride=ny), :] = updated[lo:hi]
                    else:
                        current[y, pl.ds(x, hi - lo), spot[1]] = updated[lo:hi]

    if last:
        for c in range(chunk):
            restored[c * slab * ny : (c + 1) * slab * ny] = before_this[c][:]
        base = chunk * slab * ny
        for k, block in enumerate(turned):
            restored[base:, LANE * k : LANE * (k + 1)] = block[:]


def run_passes(first, last, chunk, halo, slab, nx, start, pieces, duals, done):
    ny, _, nz = pieces[0].shape
    width = slab + 2 * halo
    vmem = pl.BlockSpec(memory_space=pltpu.VMEM)
    if last:
        out_shape = jax.ShapeDtypeStruct(((chunk + 1) * slab * ny, nz), f32)
        out_specs = vmem
    else:
        kept = jax.ShapeDtypeStruct((ny, slab + 2 * HALO_LAST, nz), f32)
        out_shape = [jax.ShapeDtypeStruct((ny, slab, nz), f32), kept, kept, kept]
        out_specs = [vmem] * 4
    operands = list(pieces) + list(duals) + list(done)
    field = ny * padded_to(width, SUB) * nz * 4
    return pl.pallas_call(
        functools.partial(passes_kernel, first, last, chunk, halo, slab, nx),
        in_specs=[pl.BlockSpec(memory_space=pltpu.SMEM)] + [vmem] * len(operands),
        out_specs=out_specs,
        out_shape=out_shape,
        scratch_shapes=[
            pltpu.VMEM((ny + 2, width, nz), f32),
            pltpu.VMEM((ny, width, nz), f32),
            pltpu.VMEM((ny, width, nz), f32),
            pltpu.VMEM((ny + 2, width, nz), f32),
            pltpu.VMEM((ny, width, nz), f32),
        ]
        + [pltpu.VMEM((slab * ny, LANE), f32)] * (nz // LANE if last else 0),
        compiler_params=pltpu.CompilerParams(vmem_limit_bytes=12 * field + 8 * MIB),
        cost_estimate=pl.CostEstimate(
            flops=60 * PASSES * ny * width * nz,
            bytes_accessed=8 * 4 * ny * width * nz,
            transcendentals=PASSES * ny * width * nz,
        ),
    )(start, *operands)


def exchange(blocks):
    return lax.all_to_all(blocks, "gy", split_axis=0, concat_axis=0, tiled=True)


def local(observed, tf_table, tilt_index, wedge):
    slab, ny, nz = observed.shape
    devices = lax.axis_size("gy")
    rows = ny // devices
    nx = slab * devices
    chunks = 2 if slab % (2 * SUB) == 0 and slab >= 4 * HALO_FIRST else 1
    size = slab // chunks
    start = (lax.axis_index("gy") * slab).astype(jnp.int32).reshape(1)
    forward, inverse = x_tables(nx, slab, chunks)
    tables = (
        jnp.asarray(z_table(nz)),
        [jnp.asarray(table) for table in forward],
        jnp.asarray(inverse),
    )
    cells = []
    for chunk in range(chunks):
        part = lax.slice_in_dim(observed, chunk * size, (chunk + 1) * size, axis=0)
        cells.append(exchange(part.transpose(1, 0, 2).reshape(devices, rows, size, nz)))
    both, data, prior = make_weights(tf_table, tilt_index, wedge, nx, nz)
    duals = [()] * chunks
    for outer in range(OUTER):
        first, last = outer == 0, outer == OUTER - 1
        halo = HALO_LAST if last else HALO_FIRST
        so_far = [start_filter(cells[0], tables, 0, slab)] if chunks > 1 else []
        weights = (both, data) if first else (kept, prior)
        widths = [size + 2 * halo] + [size] * (chunks - 1)
        made = finish_filter(
            first, halo, cells[-1], so_far, tables, weights, chunks - 1, slab, widths
        )
        if first:
            kept = made[chunks]
        pieces = [
            exchange(made[chunk]).reshape(ny, widths[chunk], nz) for chunk in range(chunks)
        ]
        cells, done = [], []
        for chunk in range(chunks):
            used = pieces[max(chunk - 1, 0) : chunk + 1]
            out = run_passes(
                first, last, chunk, halo, size, nx, start, used, duals[chunk], done
            )
            if last:
                done = [out]
                continue
            duals[chunk] = tuple(out[1:])
            cells.append(exchange(out[0].reshape(devices, rows, size, nz)))
    return done[0].reshape(slab, ny, nz)


def solution(mesh):
    in_specs = (P(("groups", "gy"), None, None), P(), P(), P())
    out_specs = P(("groups", "gy"), None, None)
    return jax.shard_map(local, mesh=mesh, in_specs=in_specs, out_specs=out_specs, check_vma=False)
```

```python
import functools

import jax
import jax.numpy as jnp
import ml_dtypes
import numpy as np
from jax import lax
from jax.experimental import pallas as pl
from jax.experimental.pallas import tpu as pltpu
from jax.sharding import PartitionSpec as P

OUTER = 2
PASSES = 2

step_dual = 0.14
step_primal = 0.14
huber_eps = 0.05
bound_dual = 0.5

SUB = 8
LANE = 128
HALO_LAST = 2 * PASSES
HALO_FIRST = HALO_LAST + 2 * PASSES - 2
UNROLL = 4
MIB = 1024 * 1024

f32 = jnp.float32
bf16 = jnp.bfloat16


def halves(table):
    high = table.astype(ml_dtypes.bfloat16)
    low = (table - high.astype(np.float64)).astype(ml_dtypes.bfloat16)
    return np.stack([high, low])


def cas(rows, columns, length):
    phase = (rows[:, None] * columns[None, :]) % length
    angle = phase * (2.0 * np.pi / length)
    return np.cos(angle) + np.sin(angle)


def z_table(length):
    index = np.arange(length)
    return halves(cas(index, index, length))


def x_tables(length):
    half = length // 2
    place = np.arange(half)
    even = cas(2 * place, place, length)
    odd = cas(2 * place + 1, place, length)
    return np.stack([halves(even), halves(odd), halves(odd.T)])


def padded_to(length, unit):
    return -(-length // unit) * unit


def weights_kernel(nx, nz, levels, table_ref, code_ref, both, data, prior):
    half = nx // 2
    tile = min(256, half)
    heights, widths = code_ref.shape
    scale = 1.0 / (nx * nz)
    kz = lax.broadcasted_iota(jnp.int32, (heights, nz), 1)
    kz = jnp.minimum(kz, nz - kz)
    pick_z = jnp.where(kz == lax.broadcasted_iota(jnp.int32, (heights, nz), 0), 1.0, 0.0)
    pick_z = pick_z.astype(bf16)
    for part in range(2):
        for top in range(0, half, tile):
            kx = 2 * (top + lax.broadcasted_iota(jnp.int32, (tile, widths), 0)) + part
            kx = jnp.minimum(kx, nx - kx)
            pick_x = jnp.where(kx == lax.broadcasted_iota(jnp.int32, (tile, widths), 1), 1.0, 0.0)
            tall = lax.dot_general(
                pick_x.astype(bf16),
                code_ref[...],
                (((1,), (1,)), ((), ())),
                preferred_element_type=f32,
            )
            spread = jnp.dot(tall.astype(bf16), pick_z, preferred_element_type=f32)
            response = jnp.zeros_like(spread)
            for level in range(levels):
                response = jnp.where(spread == level + 1.0, table_ref[level], response)
            gain = scale / (response * response + 1.0)
            rows = slice(part * half + top, part * half + top + tile)
            prior[rows] = gain
            data[rows] = response * gain
            both[rows] = response * gain + gain


def make_weights(tf_table, tilt_index, wedge, nx, nz):
    levels = tf_table.shape[0]
    code = jnp.where(wedge > 0, tilt_index + 1, 0).T
    extra = [(0, padded_to(size, LANE) - size) for size in code.shape]
    code = jnp.pad(code, extra).astype(bf16)
    grid = jax.ShapeDtypeStruct((nx, nz), f32)
    vmem = pl.BlockSpec(memory_space=pltpu.VMEM)
    return pl.pallas_call(
        functools.partial(weights_kernel, nx, nz, levels),
        in_specs=[pl.BlockSpec(memory_space=pltpu.SMEM), vmem],
        out_specs=[vmem] * 3,
        out_shape=[grid] * 3,
        compiler_params=pltpu.CompilerParams(vmem_limit_bytes=16 * MIB),
        cost_estimate=pl.CostEstimate(
            flops=60 * nx * nz, bytes_accessed=12 * nx * nz, transcendentals=0
        ),
    )(tf_table, code)


def split(value):
    high = value.astype(bf16)
    return high, (value - high.astype(f32)).astype(bf16)


def dot3(a, b):
    dot = functools.partial(jnp.dot, preferred_element_type=f32)
    return dot(a[0], b[0]) + (dot(a[0], b[1]) + dot(a[1], b[0]))


def turn_kernel(ny, planes, cells, turned, staged, placed, semaphores):
    blocks = len(staged)
    steps = placed.shape[1] // planes
    rows = planes * ny
    incoming = [
        [
            pltpu.make_async_copy(
                cells.at[pl.ds(step * rows, rows), pl.ds(LANE * k, LANE)],
                staged[k].at[pl.ds(step * rows, rows), :],
                semaphores.at[0, step, k],
            )
            for k in range(blocks)
        ]
        for step in range(steps)
    ]
    outgoing = [
        pltpu.make_async_copy(
            placed.at[:, pl.ds(step * planes, planes), :],
            turned.at[:, pl.ds(step * planes, planes), :],
            semaphores.at[1, step, 0],
        )
        for step in range(steps)
    ]
    for step in range(steps):
        for copy in incoming[step]:
            copy.start()
    for step in range(steps):
        for copy in incoming[step]:
            copy.wait()
        for y in range(ny):
            for x in range(step * planes, (step + 1) * planes, SUB):
                for k in range(blocks):
                    placed[y, x : x + SUB, LANE * k : LANE * (k + 1)] = staged[k][
                        pl.ds(x * ny + y, SUB, stride=ny), :
                    ]
        outgoing[step].start()
    for copy in outgoing:
        copy.wait()


def turn(observed):
    slab, ny, nz = observed.shape
    planes = 2 * SUB if slab % (2 * SUB) == 0 else SUB
    anywhere = pl.BlockSpec(memory_space=pl.ANY)
    return pl.pallas_call(
        functools.partial(turn_kernel, ny, planes),
        in_specs=[anywhere],
        out_specs=anywhere,
        out_shape=jax.ShapeDtypeStruct((ny, slab, nz), f32),
        scratch_shapes=[
            [pltpu.VMEM((slab * ny, LANE), f32)] * (nz // LANE),
            pltpu.VMEM((ny, slab, nz), f32),
            pltpu.SemaphoreType.DMA((2, slab // planes, nz // LANE)),
        ],
        compiler_params=pltpu.CompilerParams(vmem_limit_bytes=16 * MIB),
        cost_estimate=pl.CostEstimate(
            flops=0, bytes_accessed=8 * slab * ny * nz, transcendentals=0
        ),
    )(observed.reshape(slab * ny, nz))


def window_tiles(width, nz):
    return width * nz // (SUB * LANE)


def filter_kernel(first, halo, slab, *refs):
    cells, ztab, xtab_far, refs = refs[0], refs[1], refs[2], refs[3:]
    if first:
        both_far, data_far, windows, kept_far, refs = refs[0], refs[1], refs[2], refs[3], refs[4:]
    else:
        kept_far, prior_far, windows, refs = refs[0], refs[1], refs[2], refs[3:]
    xtab, scale, other, high, low, padded, semaphores = refs
    devices, rows, _, nz = cells.shape
    nx = devices * slab
    half = nx // 2
    tile = min(256, half)
    width = slab + 2 * halo
    blocks = nz // LANE
    ztable = (ztab[0], ztab[1])
    arrivals = [
        pltpu.make_async_copy(xtab_far.at[0], xtab.at[0], semaphores.at[0]),
        pltpu.make_async_copy(xtab_far.at[1], xtab.at[1], semaphores.at[1]),
        pltpu.make_async_copy(both_far if first else prior_far, scale, semaphores.at[2]),
        pltpu.make_async_copy(xtab_far.at[2], xtab.at[2], semaphores.at[3]),
    ]
    if first:
        arrivals.append(pltpu.make_async_copy(data_far, other.at[0], semaphores.at[4]))
    for copy in arrivals:
        copy.start()
    for r in range(rows):
        if not first:
            kept_copy = pltpu.make_async_copy(kept_far.at[r], other.at[0], semaphores.at[4])
            kept_copy.start()
        flat = cells[:, r].reshape(nx, nz)
        for top in range(0, half, tile):
            a = dot3(split(flat[top : top + tile]), ztable)
            b = dot3(split(flat[half + top : half + top + tile]), ztable)
            for spot, value in ((top, a + b), (half + top, a - b)):
                high[spot : spot + tile], low[spot : spot + tile] = split(value)
        folded = [
            (high[part * half : (part + 1) * half], low[part * half : (part + 1) * half])
            for part in range(2)
        ]
        waves = []
        for part in range(2):
            if r == 0:
                arrivals[part].wait()
            for top in range(0, half, tile):
                table = (xtab[part, 0, top : top + tile], xtab[part, 1, top : top + tile])
                waves.append(dot3(table, folded[part]))
        if r == 0:
            arrivals[2].wait()
            if first:
                arrivals[4].wait()
        if not first:
            kept_copy.wait()
        for i, wave in enumerate(waves):
            spot = slice(i * tile, (i + 1) * tile)
            if first:
                mixed = wave * scale[spot]
                other[1, spot] = wave * other[0, spot]
            else:
                mixed = other[0, spot] + wave * scale[spot]
            high[spot], low[spot] = split(mixed)
        if first:
            kept_copy = pltpu.make_async_copy(other.at[1], kept_far.at[r], semaphores.at[5])
            kept_copy.start()
        if r == 0:
            arrivals[3].wait()
        even = (high[:half], low[:half])
        odd = (high[half:], low[half:])
        after = (halo + nx) // SUB * SUB
        padded[:SUB] = jnp.zeros((SUB, nz), f32)
        padded[after : after + 2 * SUB] = jnp.zeros((2 * SUB, nz), f32)
        for top in range(0, half, tile):
            e = dot3((xtab[0, 0, top : top + tile], xtab[0, 1, top : top + tile]), even)
            o = dot3((xtab[2, 0, top : top + tile], xtab[2, 1, top : top + tile]), odd)
            padded[halo + top : halo + top + tile] = dot3(split(e + o), ztable)
            padded[halo + half + top : halo + half + top + tile] = dot3(split(e - o), ztable)
        for device in range(devices):
            for g in range(width // SUB):
                spot = device * slab + SUB * g
                for k in range(blocks):
                    windows[device, r, g * blocks + k] = padded[
                        spot : spot + SUB, LANE * k : LANE * (k + 1)
                    ]
            spot = device * slab + width // SUB * SUB
            rest = width % SUB
            for k in range(blocks if rest else 0):
                windows[
                    device, r, width // SUB * blocks + k * rest // SUB, k * rest % SUB : k * rest % SUB + rest
                ] = padded[spot : spot + rest, LANE * k : LANE * (k + 1)]
        if first:
            kept_copy.wait()


def run_filter(first, halo, cells, tables, far):
    devices, rows, slab, nz = cells.shape
    nx = devices * slab
    ztab, xtab = tables
    vmem = pl.BlockSpec(memory_space=pltpu.VMEM)
    anywhere = pl.BlockSpec(memory_space=pl.ANY)
    tiles = window_tiles(slab + 2 * halo, nz)
    out_shape = [jax.ShapeDtypeStruct((devices, rows, tiles, SUB, LANE), f32)]
    out_specs = [vmem]
    if first:
        out_shape.append(jax.ShapeDtypeStruct((rows, nx, nz), f32))
        out_specs.append(anywhere)
    return pl.pallas_call(
        functools.partial(filter_kernel, first, halo, slab),
        in_specs=[vmem, vmem, anywhere, anywhere, anywhere],
        out_specs=out_specs,
        out_shape=out_shape,
        scratch_shapes=[
            pltpu.VMEM(xtab.shape, bf16),
            pltpu.VMEM((nx, nz), f32),
            pltpu.VMEM((2, nx, nz), f32),
            pltpu.VMEM((nx, nz), bf16),
            pltpu.VMEM((nx, nz), bf16),
            pltpu.VMEM((nx + 3 * SUB, nz), f32),
            pltpu.SemaphoreType.DMA((6,)),
        ],
        compiler_params=pltpu.CompilerParams(vmem_limit_bytes=32 * MIB),
        cost_estimate=pl.CostEstimate(
            flops=6 * rows * nx * nz * (2 * nz + nx),
            bytes_accessed=8 * rows * nx * nz,
            transcendentals=0,
        ),
    )(cells, ztab, xtab, *far)


def lane_sums(pieces):
    lane = lax.broadcasted_iota(jnp.int32, pieces[0].shape, 1)
    up = [pltpu.roll(piece, LANE - 1, 1) for piece in pieces]
    down = [pltpu.roll(piece, 1, 1) for piece in pieces]
    sums = []
    for k in range(len(pieces)):
        above = up[k + 1] if k + 1 < len(pieces) else 0.0
        below = down[k - 1] if k > 0 else 0.0
        sums.append(
            jnp.where(lane == LANE - 1, above, up[k]) + jnp.where(lane == 0, below, down[k])
        )
    return sums


def row_sums(groups):
    row = lax.broadcasted_iota(jnp.int32, groups[0].shape, 0)
    up = [pltpu.roll(group, SUB - 1, 0) for group in groups]
    down = [pltpu.roll(group, 1, 0) for group in groups]
    count = len(groups)
    return [
        jnp.where(row == SUB - 1, up[(g + 1) % count], up[g])
        + jnp.where(row == 0, down[g - 1], down[g])
        for g in range(count)
    ]


def passes_kernel(first, last, halo, slab, nx, start_ref, target, *refs):
    if first:
        duals_in, refs = None, refs
    else:
        duals_in, refs = refs[:3], refs[3:]
    if last:
        restored, refs = refs[0], refs[1:]
    else:
        current, duals_out, refs = refs[0], refs[1:4], refs[4:]
    lead, field, dual_x, dual_y, dual_z = refs[:5]
    turned = refs[5:]
    ny, _, nz = field.shape
    width = slab + 2 * halo
    groups = padded_to(width, SUB) // SUB
    blocks = nz // LANE
    decay = 1.0 / (1.0 + step_dual * huber_eps / bound_dual)
    gain = step_dual * decay
    floor = 1.0 / (decay * decay)
    slope = (gain / (decay * bound_dual)) ** 2
    keep = 1.0 / (1.0 + step_primal)
    pull = step_primal * keep
    push = pull * gain / decay
    origin = start_ref[0] - halo

    def goal_of(y, g, k):
        if SUB * (g + 1) <= width:
            return target[y, g * blocks + k]
        rest = width % SUB
        tail = target[y, g * blocks + k * rest // SUB]
        shift = k * rest % SUB
        return pltpu.roll(tail, SUB - shift, 0) if shift else tail

    def masked(value, g):
        if SUB * g >= halo and SUB * (g + 1) <= width - halo:
            return value
        place = origin + SUB * g + lax.broadcasted_iota(jnp.int32, (SUB, LANE), 0)
        return jnp.where((place >= 0) & (place < nx), value, 0.0)

    def at(g, k):
        return pl.ds(SUB * g, SUB), pl.ds(LANE * k, LANE)

    empty = jnp.zeros(lead.shape[1:], f32)
    for plane in (0, ny + 1):
        lead[plane] = empty
        dual_y[plane] = empty

    @pl.loop(0, ny, unroll=UNROLL)
    def _(y):
        for g in range(groups):
            for k in range(blocks):
                lead[(y + 1,) + at(g, k)] = goal_of(y, g, k)

    for sweep in range(PASSES):
        final = sweep == PASSES - 1

        @pl.loop(0, ny, unroll=UNROLL)
        def _(y):
            here = [[lead[(y + 1,) + at(g, k)] for k in range(blocks)] for g in range(groups)]
            columns = [row_sums([here[g][k] for g in range(groups)]) for k in range(blocks)]
            for g in range(groups):
                along_z = lane_sums(here[g])
                for k in range(blocks):
                    spot = at(g, k)
                    twice = here[g][k] + here[g][k]
                    along_y = lead[(y,) + spot] + lead[(y + 2,) + spot]
                    raised = [columns[k][g] - twice, along_y - twice, along_z[k] - twice]
                    if sweep > 0:
                        before = [dual_x[(y,) + spot], dual_y[(y + 1,) + spot], dual_z[(y,) + spot]]
                    elif duals_in is not None:
                        before = [ref[(y,) + spot] for ref in duals_in]
                    else:
                        before = None
                    if before is not None:
                        raised = [old + new for old, new in zip(before, raised)]
                    total = (
                        raised[0] * raised[0] + raised[1] * raised[1] + raised[2] * raised[2]
                    )
                    shrink = lax.rsqrt(jnp.maximum(floor, total * slope))
                    made = [raised[0] * masked(shrink, g), raised[1] * shrink, raised[2] * shrink]
                    dual_x[(y,) + spot] = made[0]
                    dual_y[(y + 1,) + spot] = made[1]
                    dual_z[(y,) + spot] = made[2]
                    if final and not last:
                        shift = halo - HALO_LAST
                        lo = max(0, shift - SUB * g)
                        hi = min(SUB, slab + 2 * HALO_LAST + shift - SUB * g)
                        if lo < hi:
                            rows = pl.ds(SUB * g + lo - shift, hi - lo)
                            for a in range(3):
                                duals_out[a][y, rows, spot[1]] = made[a][lo:hi]

        @pl.loop(0, ny, unroll=UNROLL)
        def _(y):
            wanted = range(groups)
            if final:
                wanted = [
                    g for g in wanted if SUB * (g + 1) > halo and SUB * g < width - halo
                ]
            near = [[dual_x[(y,) + at(g, k)] for k in range(blocks)] for g in range(groups)]
            columns = [row_sums([near[g][k] for g in range(groups)]) for k in range(blocks)]
            for g in wanted:
                here = [dual_z[(y,) + at(g, k)] for k in range(blocks)]
                along_z = lane_sums(here)
                for k in range(blocks):
                    spot = at(g, k)
                    along_y = dual_y[(y,) + spot] + dual_y[(y + 2,) + spot]
                    centre = near[g][k] + dual_y[(y + 1,) + spot] + here[k]
                    adjoint = columns[k][g] + along_y + along_z[k] - (centre + centre)
                    move = push * adjoint
                    goal = goal_of(y, g, k)
                    if sweep == 0:
                        updated = goal - move
                        ahead = updated - move
                    else:
                        old = field[(y,) + spot]
                        updated = keep * old + pull * goal - move
                        ahead = updated + updated - old
                    if not final:
                        field[(y,) + spot] = updated
                        lead[(y + 1,) + spot] = masked(ahead, g)
                        continue
                    lo = max(0, halo - SUB * g)
                    hi = min(SUB, slab + halo - SUB * g)
                    x = SUB * g + lo - halo
                    if last:
                        turned[k][pl.ds(x * ny + y, hi - lo, stride=ny), :] = updated[lo:hi]
                    else:
                        current[y, pl.ds(x, hi - lo), spot[1]] = updated[lo:hi]

    for k, block in enumerate(turned):
        restored[:, LANE * k : LANE * (k + 1)] = block[:]


def run_passes(first, last, halo, slab, nx, start, target, duals):
    ny = target.shape[0]
    nz = target.shape[1] * SUB * LANE // (slab + 2 * halo)
    width = padded_to(slab + 2 * halo, SUB)
    vmem = pl.BlockSpec(memory_space=pltpu.VMEM)
    if last:
        out_shape = jax.ShapeDtypeStruct((slab * ny, nz), f32)
        out_specs = vmem
    else:
        kept = jax.ShapeDtypeStruct((ny, slab + 2 * HALO_LAST, nz), f32)
        out_shape = [jax.ShapeDtypeStruct((ny, slab, nz), f32), kept, kept, kept]
        out_specs = [vmem] * 4
    return pl.pallas_call(
        functools.partial(passes_kernel, first, last, halo, slab, nx),
        in_specs=[pl.BlockSpec(memory_space=pltpu.SMEM)] + [vmem] * (1 + len(duals)),
        out_specs=out_specs,
        out_shape=out_shape,
        scratch_shapes=[
            pltpu.VMEM((ny + 2, width, nz), f32),
            pltpu.VMEM((ny, width, nz), f32),
            pltpu.VMEM((ny, width, nz), f32),
            pltpu.VMEM((ny + 2, width, nz), f32),
            pltpu.VMEM((ny, width, nz), f32),
        ]
        + [pltpu.VMEM((slab * ny, LANE), f32)] * (nz // LANE if last else 0),
        compiler_params=pltpu.CompilerParams(vmem_limit_bytes=40 * MIB),
        cost_estimate=pl.CostEstimate(
            flops=60 * PASSES * ny * width * nz,
            bytes_accessed=8 * 4 * ny * width * nz,
            transcendentals=PASSES * ny * width * nz,
        ),
    )(start, target, *duals)


def exchange(blocks):
    return lax.all_to_all(blocks, "gy", split_axis=0, concat_axis=0, tiled=True)


def local(observed, tf_table, tilt_index, wedge):
    slab, ny, nz = observed.shape
    devices = lax.axis_size("gy")
    rows = ny // devices
    nx = slab * devices
    start = (lax.axis_index("gy") * slab).astype(jnp.int32).reshape(1)
    tables = (jnp.asarray(z_table(nz)), jnp.asarray(x_tables(nx)))
    cells = exchange(turn(observed).reshape(devices, rows, slab, nz))
    both, data, prior = make_weights(tf_table, tilt_index, wedge, nx, nz)
    duals = ()
    for outer in range(OUTER):
        first, last = outer == 0, outer == OUTER - 1
        halo = HALO_LAST if last else HALO_FIRST
        made = run_filter(first, halo, cells, tables, (both, data) if first else (kept, prior))
        if first:
            kept = made[1]
        windows = exchange(made[0])
        target = windows.reshape((ny,) + windows.shape[2:])
        made = run_passes(first, last, halo, slab, nx, start, target, duals)
        if last:
            return made.reshape(slab, ny, nz)
        duals = tuple(made[1:])
        cells = exchange(made[0].reshape(devices, rows, slab, nz))


def solution(mesh):
    in_specs = (P(("groups", "gy"), None, None), P(), P(), P())
    out_specs = P(("groups", "gy"), None, None)
    return jax.shard_map(local, mesh=mesh, in_specs=in_specs, out_specs=out_specs, check_vma=False)
```

```python
import functools

import jax
import jax.numpy as jnp
import ml_dtypes
import numpy as np
from jax import lax
from jax.experimental import pallas as pl
from jax.experimental.pallas import tpu as pltpu
from jax.sharding import PartitionSpec as P

OUTER = 2
PASSES = 2

step_dual = 0.14
step_primal = 0.14
huber_eps = 0.05
bound_dual = 0.5

SUB = 8
LANE = 128
HALO_LAST = 2 * PASSES
HALO_FIRST = HALO_LAST + 2 * PASSES - 2
UNROLL = 4
MIB = 1024 * 1024

f32 = jnp.float32
bf16 = jnp.bfloat16

UNIT = step_dual / bound_dual


def halves(table):
    high = table.astype(ml_dtypes.bfloat16)
    low = (table - high.astype(np.float64)).astype(ml_dtypes.bfloat16)
    return np.stack([high, low])


def cas(rows, columns, length):
    phase = (rows[:, None] * columns[None, :]) % length
    angle = phase * (2.0 * np.pi / length)
    return np.cos(angle) + np.sin(angle)


def z_table(length):
    index = np.arange(length)
    return halves(cas(index, index, length))


def x_tables(length):
    half, quarter = length // 2, length // 4
    place = np.arange(half)
    fourth = cas(4 * place[:quarter], place[:quarter], length)
    second = cas(4 * place[:quarter] + 2, place[:quarter], length)
    odd = cas(2 * place + 1, place, length)
    small = np.stack([halves(fourth), halves(second), halves(second.T)])
    return small, np.stack([halves(odd), halves(odd.T)])


def kx_rows(length):
    half, quarter = length // 2, length // 4
    return ((0, quarter, 4, 0), (quarter, quarter, 4, 2), (half, half, 2, 1))


def padded_to(length, unit):
    return -(-length // unit) * unit


def weights_kernel(nx, nz, levels, table_ref, code_ref, both, data, prior):
    heights, widths = code_ref.shape
    scale = 1.0 / (nx * nz)
    kz = lax.broadcasted_iota(jnp.int32, (heights, nz), 1)
    kz = jnp.minimum(kz, nz - kz)
    pick_z = jnp.where(kz == lax.broadcasted_iota(jnp.int32, (heights, nz), 0), 1.0, 0.0)
    pick_z = pick_z.astype(bf16)
    for base, count, step, least in kx_rows(nx):
        tile = min(256, count)
        for top in range(0, count, tile):
            kx = step * (top + lax.broadcasted_iota(jnp.int32, (tile, widths), 0)) + least
            kx = jnp.minimum(kx, nx - kx)
            pick_x = jnp.where(kx == lax.broadcasted_iota(jnp.int32, (tile, widths), 1), 1.0, 0.0)
            tall = lax.dot_general(
                pick_x.astype(bf16),
                code_ref[...],
                (((1,), (1,)), ((), ())),
                preferred_element_type=f32,
            )
            spread = jnp.dot(tall.astype(bf16), pick_z, preferred_element_type=f32)
            response = jnp.zeros_like(spread)
            for level in range(levels):
                response = jnp.where(spread == level + 1.0, table_ref[level], response)
            gain = scale / (response * response + 1.0)
            rows = slice(base + top, base + top + tile)
            prior[rows] = gain
            data[rows] = (UNIT * response) * gain
            both[rows] = UNIT * (response * gain + gain)


def make_weights(tf_table, tilt_index, wedge, nx, nz):
    levels = tf_table.shape[0]
    code = jnp.where(wedge > 0, tilt_index + 1, 0).T
    extra = [(0, padded_to(size, LANE) - size) for size in code.shape]
    code = jnp.pad(code, extra).astype(bf16)
    grid = jax.ShapeDtypeStruct((nx, nz), f32)
    vmem = pl.BlockSpec(memory_space=pltpu.VMEM)
    return pl.pallas_call(
        functools.partial(weights_kernel, nx, nz, levels),
        in_specs=[pl.BlockSpec(memory_space=pltpu.SMEM), vmem],
        out_specs=[vmem] * 3,
        out_shape=[grid] * 3,
        compiler_params=pltpu.CompilerParams(vmem_limit_bytes=16 * MIB),
        cost_estimate=pl.CostEstimate(
            flops=60 * nx * nz, bytes_accessed=12 * nx * nz, transcendentals=0
        ),
    )(tf_table, code)


def split(value):
    high = value.astype(bf16)
    return high, (value - high.astype(f32)).astype(bf16)


def dot3(a, b):
    dot = functools.partial(jnp.dot, preferred_element_type=f32)
    return dot(a[0], b[0]) + (dot(a[0], b[1]) + dot(a[1], b[0]))


def turn_kernel(ny, planes, cells, turned, staged, placed, semaphores):
    blocks = len(staged)
    steps = placed.shape[1] // planes
    rows = planes * ny
    incoming = [
        [
            pltpu.make_async_copy(
                cells.at[pl.ds(step * rows, rows), pl.ds(LANE * k, LANE)],
                staged[k].at[pl.ds(step * rows, rows), :],
                semaphores.at[0, step, k],
            )
            for k in range(blocks)
        ]
        for step in range(steps)
    ]
    outgoing = [
        pltpu.make_async_copy(
            placed.at[:, pl.ds(step * planes, planes), :],
            turned.at[:, pl.ds(step * planes, planes), :],
            semaphores.at[1, step, 0],
        )
        for step in range(steps)
    ]
    for step in range(steps):
        for copy in incoming[step]:
            copy.start()
    for step in range(steps):
        for copy in incoming[step]:
            copy.wait()
        for y in range(ny):
            for x in range(step * planes, (step + 1) * planes, SUB):
                for k in range(blocks):
                    placed[y, x : x + SUB, LANE * k : LANE * (k + 1)] = staged[k][
                        pl.ds(x * ny + y, SUB, stride=ny), :
                    ]
        outgoing[step].start()
    for copy in outgoing:
        copy.wait()


def turn(observed):
    slab, ny, nz = observed.shape
    planes = 2 * SUB if slab % (2 * SUB) == 0 else SUB
    anywhere = pl.BlockSpec(memory_space=pltpu.HBM)
    return pl.pallas_call(
        functools.partial(turn_kernel, ny, planes),
        in_specs=[anywhere],
        out_specs=anywhere,
        out_shape=jax.ShapeDtypeStruct((ny, slab, nz), f32),
        scratch_shapes=[
            [pltpu.VMEM((slab * ny, LANE), f32)] * (nz // LANE),
            pltpu.VMEM((ny, slab, nz), f32),
            pltpu.SemaphoreType.DMA((2, slab // planes, nz // LANE)),
        ],
        compiler_params=pltpu.CompilerParams(vmem_limit_bytes=16 * MIB),
        cost_estimate=pl.CostEstimate(
            flops=0, bytes_accessed=8 * slab * ny * nz, transcendentals=0
        ),
    )(observed.reshape(slab * ny, nz))


def window_tiles(width, nz):
    return width * nz // (SUB * LANE)


def filter_kernel(first, halo, slab, *refs):
    cells, ztab_far, small_far, odd_far, refs = refs[0], refs[1], refs[2], refs[3], refs[4:]
    if first:
        both_far, data_far, windows_far, kept_far, refs = refs[0], refs[1], refs[2], refs[3], refs[4:]
    else:
        kept_far, prior_far, windows, refs = refs[0], refs[1], refs[2], refs[3:]
    ztab, small, odd, scale, other, high, low, padded, semaphores, refs = refs[:9] + (refs[9:],)
    if first:
        windows, window_semaphores = refs
    devices, rows, _, nz = cells.shape
    nx = devices * slab
    half, quarter = nx // 2, nx // 4
    width = slab + 2 * halo
    blocks = nz // LANE
    arrivals = [
        pltpu.make_async_copy(ztab_far, ztab, semaphores.at[0]),
        pltpu.make_async_copy(small_far, small, semaphores.at[1]),
        pltpu.make_async_copy(odd_far.at[0], odd.at[0], semaphores.at[2]),
        pltpu.make_async_copy(both_far if first else prior_far, scale, semaphores.at[3]),
    ]
    if first:
        arrivals.append(pltpu.make_async_copy(data_far, other.at[0], semaphores.at[4]))
    last_arrival = pltpu.make_async_copy(odd_far.at[1], odd.at[1], semaphores.at[5])
    for copy in arrivals:
        copy.start()

    def table(ref, i, rows=slice(None)):
        return ref[i, 0, rows], ref[i, 1, rows]

    def store(spot, value):
        high[spot], low[spot] = split(value)

    def load(spot):
        return high[spot], low[spot]

    parts = [slice(i * quarter, (i + 1) * quarter) for i in range(4)]
    folds = [parts[0], parts[1], slice(half, nx)]
    for r in range(rows):
        if not first:
            kept_copy = pltpu.make_async_copy(kept_far.at[r], other.at[0], semaphores.at[4])
            kept_copy.start()
        if r == 0:
            last_arrival.start()
        q = [
            cells[i * devices // 4 : (i + 1) * devices // 4, r].reshape(quarter, nz)
            for i in range(4)
        ]
        even = (q[0] + q[2], q[1] + q[3])
        folded = (even[0] + even[1], even[0] - even[1], q[0] - q[2], q[1] - q[3])
        if r == 0:
            arrivals[0].wait()
        ztable = (ztab[0], ztab[1])
        for spot, value in zip(parts, folded):
            store(spot, dot3(split(value), ztable))
        if r == 0:
            arrivals[1].wait()
        waves = [dot3(table(small, i), load(folds[i])) for i in range(2)]
        if r == 0:
            arrivals[2].wait()
        for i in range(2):
            waves.append(dot3(table(odd, 0, parts[i]), load(folds[2])))
        if r == 0:
            for copy in arrivals[3:]:
                copy.wait()
        if not first:
            kept_copy.wait()
        for spot, wave in zip(parts, waves):
            if first:
                other[1, spot] = wave * other[0, spot]
                store(spot, wave * scale[spot])
            else:
                store(spot, other[0, spot] + wave * scale[spot])
        if first:
            kept_copy = pltpu.make_async_copy(other.at[1], kept_far.at[r], semaphores.at[6])
            kept_copy.start()
        after = (halo + nx) // SUB * SUB
        padded[:SUB] = jnp.zeros((SUB, nz), f32)
        padded[after : after + 2 * SUB] = jnp.zeros((2 * SUB, nz), f32)
        plus, minus = dot3(table(small, 0), load(folds[0])), dot3(table(small, 2), load(folds[1]))
        if r == 0:
            last_arrival.wait()
        leaving = []
        written, sent = set(), set()
        for i, e in enumerate((plus + minus, plus - minus)):
            o = dot3(table(odd, 1, parts[i]), load(folds[2]))
            for j, value in ((i, e + o), (i + 2, e - o)):
                place = halo + j * quarter
                padded[place : place + quarter] = dot3(split(value), ztable)
                written |= set(range(j * quarter, (j + 1) * quarter))
            for device in range(devices):
                needed = range(device * slab - halo, (device + 1) * slab + halo)
                if device in sent or not written.issuperset(x for x in needed if 0 <= x < nx):
                    continue
                sent.add(device)
                for g in range(width // SUB):
                    spot = device * slab + SUB * g
                    for k in range(blocks):
                        windows[device, r, g * blocks + k] = padded[
                            spot : spot + SUB, LANE * k : LANE * (k + 1)
                        ]
                rest = width % SUB
                spot = device * slab + width - rest
                for k in range(blocks if rest else 0):
                    tile, row = width // SUB * blocks + k * rest // SUB, k * rest % SUB
                    windows[device, r, tile, row : row + rest] = padded[
                        spot : spot + rest, LANE * k : LANE * (k + 1)
                    ]
                if first:
                    copy = pltpu.make_async_copy(
                        windows.at[device, r], windows_far.at[device, r], window_semaphores.at[device]
                    )
                    copy.start()
                    leaving.append(copy)
        if first:
            for copy in leaving:
                copy.wait()
            kept_copy.wait()


def run_filter(first, halo, cells, tables, far):
    devices, rows, slab, nz = cells.shape
    nx = devices * slab
    ztab, small, odd = tables
    vmem = pl.BlockSpec(memory_space=pltpu.VMEM)
    hbm = pl.BlockSpec(memory_space=pltpu.HBM)
    windows = (devices, rows, window_tiles(slab + 2 * halo, nz), SUB, LANE)
    out_shape, out_specs = [jax.ShapeDtypeStruct(windows, f32)], [hbm if first else vmem]
    if first:
        out_shape.append(jax.ShapeDtypeStruct((rows, nx, nz), f32))
        out_specs.append(hbm)
    scratch_shapes = [
        pltpu.VMEM(ztab.shape, bf16),
        pltpu.VMEM(small.shape, bf16),
        pltpu.VMEM(odd.shape, bf16),
        pltpu.VMEM((nx, nz), f32),
        pltpu.VMEM((2, nx, nz), f32),
        pltpu.VMEM((nx, nz), bf16),
        pltpu.VMEM((nx, nz), bf16),
        pltpu.VMEM((nx + 3 * SUB, nz), f32),
        pltpu.SemaphoreType.DMA((7,)),
    ]
    if first:
        scratch_shapes += [pltpu.VMEM(windows, f32), pltpu.SemaphoreType.DMA((devices,))]
    return pl.pallas_call(
        functools.partial(filter_kernel, first, halo, slab),
        in_specs=[vmem] + [hbm] * (3 + len(far)),
        out_specs=out_specs,
        out_shape=out_shape,
        scratch_shapes=scratch_shapes,
        compiler_params=pltpu.CompilerParams(vmem_limit_bytes=32 * MIB),
        cost_estimate=pl.CostEstimate(
            flops=6 * rows * nx * nz * (2 * nz + nx),
            bytes_accessed=8 * rows * nx * nz,
            transcendentals=0,
        ),
    )(cells, ztab, small, odd, *far)


def lane_sums(pieces):
    lane = lax.broadcasted_iota(jnp.int32, pieces[0].shape, 1)
    up = [pltpu.roll(piece, LANE - 1, 1) for piece in pieces]
    down = [pltpu.roll(piece, 1, 1) for piece in pieces]
    sums = []
    for k in range(len(pieces)):
        above = up[k + 1] if k + 1 < len(pieces) else 0.0
        below = down[k - 1] if k > 0 else 0.0
        sums.append(
            jnp.where(lane == LANE - 1, above, up[k]) + jnp.where(lane == 0, below, down[k])
        )
    return sums


def row_sums(groups):
    row = lax.broadcasted_iota(jnp.int32, groups[0].shape, 0)
    up = [pltpu.roll(group, SUB - 1, 0) for group in groups]
    down = [pltpu.roll(group, 1, 0) for group in groups]
    count = len(groups)
    return [
        jnp.where(row == SUB - 1, up[(g + 1) % count], up[g])
        + jnp.where(row == 0, down[g - 1], down[g])
        for g in range(count)
    ]


def passes_kernel(first, last, halo, slab, nx, start_ref, target, *refs):
    if first:
        duals_in, refs = None, refs
    else:
        duals_in, refs = refs[:3], refs[3:]
    if last:
        restored, refs = refs[0], refs[1:]
    else:
        current, duals_out, refs = refs[0], refs[1:4], refs[4:]
    lead, field, dual_x, dual_y, dual_z = refs[:5]
    turned = refs[5:-1] if last else ()
    ny, _, nz = field.shape
    width = slab + 2 * halo
    groups = padded_to(width, SUB) // SUB
    blocks = nz // LANE
    decay = 1.0 / (1.0 + step_dual * huber_eps / bound_dual)
    gain = step_dual * decay
    floor = 1.0 / (decay * decay)
    keep = 1.0 / (1.0 + step_primal)
    pull = step_primal * keep
    push = pull * gain / decay
    origin = start_ref[0] - halo

    def goal_of(y, g, k):
        if SUB * (g + 1) <= width:
            return target[y, g * blocks + k]
        rest = width % SUB
        tail = target[y, g * blocks + k * rest // SUB]
        shift = k * rest % SUB
        return pltpu.roll(tail, SUB - shift, 0) if shift else tail

    def masked(value, g):
        if SUB * g >= halo and SUB * (g + 1) <= width - halo:
            return value
        place = origin + SUB * g + lax.broadcasted_iota(jnp.int32, (SUB, LANE), 0)
        return jnp.where((place >= 0) & (place < nx), value, 0.0)

    def at(g, k):
        return pl.ds(SUB * g, SUB), pl.ds(LANE * k, LANE)

    empty = jnp.zeros(lead.shape[1:], f32)
    for plane in (0, ny + 1):
        lead[plane] = empty
        dual_y[plane] = empty

    @pl.loop(0, ny, unroll=UNROLL)
    def _(y):
        for g in range(groups):
            for k in range(blocks):
                lead[(y + 1,) + at(g, k)] = goal_of(y, g, k)

    for sweep in range(PASSES):
        final = sweep == PASSES - 1

        @pl.loop(0, ny, unroll=UNROLL)
        def _(y):
            here = [[lead[(y + 1,) + at(g, k)] for k in range(blocks)] for g in range(groups)]
            columns = [row_sums([here[g][k] for g in range(groups)]) for k in range(blocks)]
            for g in range(groups):
                along_z = lane_sums(here[g])
                for k in range(blocks):
                    spot = at(g, k)
                    twice = here[g][k] + here[g][k]
                    along_y = lead[(y,) + spot] + lead[(y + 2,) + spot]
                    raised = [columns[k][g] - twice, along_y - twice, along_z[k] - twice]
                    if sweep > 0:
                        before = [dual_x[(y,) + spot], dual_y[(y + 1,) + spot], dual_z[(y,) + spot]]
                    elif duals_in is not None:
                        before = [ref[(y,) + spot] for ref in duals_in]
                    else:
                        before = None
                    if before is not None:
                        raised = [old + new for old, new in zip(before, raised)]
                    total = (
                        raised[0] * raised[0] + raised[1] * raised[1] + raised[2] * raised[2]
                    )
                    shrink = lax.rsqrt(jnp.maximum(floor, total))
                    made = [raised[0] * masked(shrink, g), raised[1] * shrink, raised[2] * shrink]
                    dual_x[(y,) + spot] = made[0]
                    dual_y[(y + 1,) + spot] = made[1]
                    dual_z[(y,) + spot] = made[2]
                    if final and not last:
                        shift = halo - HALO_LAST
                        lo = max(0, shift - SUB * g)
                        hi = min(SUB, slab + 2 * HALO_LAST + shift - SUB * g)
                        if lo < hi:
                            rows = pl.ds(SUB * g + lo - shift, hi - lo)
                            for a in range(3):
                                duals_out[a][y, rows, spot[1]] = made[a][lo:hi]

        @pl.loop(0, ny, unroll=UNROLL)
        def _(y):
            wanted = range(groups)
            if final:
                wanted = [
                    g for g in wanted if SUB * (g + 1) > halo and SUB * g < width - halo
                ]
            near = [[dual_x[(y,) + at(g, k)] for k in range(blocks)] for g in range(groups)]
            columns = [row_sums([near[g][k] for g in range(groups)]) for k in range(blocks)]
            for g in wanted:
                here = [dual_z[(y,) + at(g, k)] for k in range(blocks)]
                along_z = lane_sums(here)
                for k in range(blocks):
                    spot = at(g, k)
                    along_y = dual_y[(y,) + spot] + dual_y[(y + 2,) + spot]
                    centre = near[g][k] + dual_y[(y + 1,) + spot] + here[k]
                    adjoint = columns[k][g] + along_y + along_z[k] - (centre + centre)
                    goal = goal_of(y, g, k)
                    if sweep == 0:
                        move = push * adjoint
                        updated = goal - move
                        ahead = updated - move
                    else:
                        old = field[(y,) + spot]
                        whole = UNIT if final and last else 1.0
                        updated = (keep / whole) * old + (pull / whole) * goal
                        updated = updated - (push / whole) * adjoint
                        ahead = updated + updated - old
                    if not final:
                        field[(y,) + spot] = updated
                        lead[(y + 1,) + spot] = masked(ahead, g)
                        continue
                    lo = max(0, halo - SUB * g)
                    hi = min(SUB, slab + halo - SUB * g)
                    x = SUB * g + lo - halo
                    if last:
                        turned[k][pl.ds(x * ny + y, hi - lo, stride=ny), :] = updated[lo:hi]
                    else:
                        current[y, pl.ds(x, hi - lo), spot[1]] = updated[lo:hi]

    copies = [
        pltpu.make_async_copy(
            block, restored.at[:, pl.ds(LANE * k, LANE)], refs[-1].at[k]
        )
        for k, block in enumerate(turned)
    ]
    for copy in copies:
        copy.start()
    for copy in copies:
        copy.wait()


def run_passes(first, last, halo, slab, nx, start, target, duals):
    ny = target.shape[0]
    nz = target.shape[1] * SUB * LANE // (slab + 2 * halo)
    width = padded_to(slab + 2 * halo, SUB)
    vmem = pl.BlockSpec(memory_space=pltpu.VMEM)
    if last:
        out_shape = jax.ShapeDtypeStruct((slab * ny, nz), f32)
        out_specs = pl.BlockSpec(memory_space=pltpu.HBM)
    else:
        kept = jax.ShapeDtypeStruct((ny, slab + 2 * HALO_LAST, nz), f32)
        out_shape = [jax.ShapeDtypeStruct((ny, slab, nz), f32), kept, kept, kept]
        out_specs = [vmem] * 4
    return pl.pallas_call(
        functools.partial(passes_kernel, first, last, halo, slab, nx),
        in_specs=[pl.BlockSpec(memory_space=pltpu.SMEM)] + [vmem] * (1 + len(duals)),
        out_specs=out_specs,
        out_shape=out_shape,
        scratch_shapes=[
            pltpu.VMEM((ny + 2, width, nz), f32),
            pltpu.VMEM((ny, width, nz), f32),
            pltpu.VMEM((ny, width, nz), f32),
            pltpu.VMEM((ny + 2, width, nz), f32),
            pltpu.VMEM((ny, width, nz), f32),
        ]
        + [pltpu.VMEM((slab * ny, LANE), f32)] * (nz // LANE if last else 0)
        + [pltpu.SemaphoreType.DMA((nz // LANE,))] * last,
        compiler_params=pltpu.CompilerParams(vmem_limit_bytes=40 * MIB),
        cost_estimate=pl.CostEstimate(
            flops=60 * PASSES * ny * width * nz,
            bytes_accessed=8 * 4 * ny * width * nz,
            transcendentals=PASSES * ny * width * nz,
        ),
    )(start, target, *duals)


def exchange(blocks):
    return lax.all_to_all(blocks, "gy", split_axis=0, concat_axis=0, tiled=True)


def local(observed, tf_table, tilt_index, wedge):
    slab, ny, nz = observed.shape
    devices = lax.axis_size("gy")
    rows = ny // devices
    nx = slab * devices
    start = (lax.axis_index("gy") * slab).astype(jnp.int32).reshape(1)
    tables = [jnp.asarray(table) for table in (z_table(nz),) + x_tables(nx)]
    cells = exchange(turn(observed).reshape(devices, rows, slab, nz))
    both, data, prior = make_weights(tf_table, tilt_index, wedge, nx, nz)
    duals = ()
    for outer in range(OUTER):
        first, last = outer == 0, outer == OUTER - 1
        halo = HALO_LAST if last else HALO_FIRST
        made = run_filter(first, halo, cells, tables, (both, data) if first else (kept, prior))
        if first:
            kept = made[1]
        windows = exchange(made[0])
        target = windows.reshape((ny,) + windows.shape[2:])
        made = run_passes(first, last, halo, slab, nx, start, target, duals)
        if last:
            return made.reshape(slab, ny, nz)
        duals = tuple(made[1:])
        cells = exchange(made[0].reshape(devices, rows, slab, nz))


def solution(mesh):
    in_specs = (P(("groups", "gy"), None, None), P(), P(), P())
    out_specs = P(("groups", "gy"), None, None)
    return jax.shard_map(local, mesh=mesh, in_specs=in_specs, out_specs=out_specs, check_vma=False)
```

```python
import functools

import jax
import jax.numpy as jnp
import ml_dtypes
import numpy as np
from jax import lax
from jax.experimental import pallas as pl
from jax.experimental.pallas import tpu as pltpu
from jax.sharding import PartitionSpec as P

OUTER = 2
PASSES = 2

step_dual = 0.14
step_primal = 0.14
huber_eps = 0.05
bound_dual = 0.5

SUB = 8
LANE = 128
HALO_LAST = 2 * PASSES
HALO_FIRST = HALO_LAST + 2 * PASSES - 2
UNROLL = 4
MIB = 1024 * 1024
MOST_VMEM = 62 * MIB

f32 = jnp.float32
bf16 = jnp.bfloat16

UNIT = step_dual / bound_dual


def halves(table):
    high = table.astype(ml_dtypes.bfloat16)
    low = (table - high.astype(np.float64)).astype(ml_dtypes.bfloat16)
    return np.stack([high, low])


def cas(rows, columns, length):
    phase = (rows[:, None] * columns[None, :]) % length
    angle = phase * (2.0 * np.pi / length)
    return np.cos(angle) + np.sin(angle)


def z_table(length):
    index = np.arange(length)
    return halves(cas(index, index, length))


def x_tables(length):
    half, quarter = length // 2, length // 4
    place = np.arange(half)
    fourth = cas(4 * place[:quarter], place[:quarter], length)
    second = cas(4 * place[:quarter] + 2, place[:quarter], length)
    odd = cas(2 * place + 1, place, length)
    small = np.stack([halves(fourth), halves(second), halves(second.T)])
    return small, np.stack([halves(odd), halves(odd.T)])


def kx_rows(length):
    half, quarter = length // 2, length // 4
    return ((0, quarter, 4, 0), (quarter, quarter, 4, 2), (half, half, 2, 1))


def padded_to(length, unit):
    return -(-length // unit) * unit


def weights_kernel(nx, nz, levels, table_ref, code_ref, data, prior):
    heights, widths = code_ref.shape
    scale = 1.0 / (nx * nz)
    kz = lax.broadcasted_iota(jnp.int32, (heights, nz), 1)
    kz = jnp.minimum(kz, nz - kz)
    pick_z = jnp.where(kz == lax.broadcasted_iota(jnp.int32, (heights, nz), 0), 1.0, 0.0)
    pick_z = pick_z.astype(bf16)
    for base, count, step, least in kx_rows(nx):
        tile = min(256, count)
        for top in range(0, count, tile):
            kx = step * (top + lax.broadcasted_iota(jnp.int32, (tile, widths), 0)) + least
            kx = jnp.minimum(kx, nx - kx)
            pick_x = jnp.where(kx == lax.broadcasted_iota(jnp.int32, (tile, widths), 1), 1.0, 0.0)
            tall = lax.dot_general(
                pick_x.astype(bf16),
                code_ref[...],
                (((1,), (1,)), ((), ())),
                preferred_element_type=f32,
            )
            spread = jnp.dot(tall.astype(bf16), pick_z, preferred_element_type=f32)
            response = jnp.zeros_like(spread)
            for level in range(levels):
                response = jnp.where(spread == level + 1.0, table_ref[level], response)
            gain = scale / (response * response + 1.0)
            rows = slice(base + top, base + top + tile)
            prior[rows] = gain
            data[rows] = (UNIT * response) * gain


def make_weights(tf_table, tilt_index, wedge, nx, nz):
    levels = tf_table.shape[0]
    code = jnp.where(wedge > 0, tilt_index + 1, 0).T
    extra = [(0, padded_to(size, LANE) - size) for size in code.shape]
    code = jnp.pad(code, extra).astype(bf16)
    grid = jax.ShapeDtypeStruct((nx, nz), f32)
    vmem = pl.BlockSpec(memory_space=pltpu.VMEM)
    return pl.pallas_call(
        functools.partial(weights_kernel, nx, nz, levels),
        in_specs=[pl.BlockSpec(memory_space=pltpu.SMEM), vmem],
        out_specs=[vmem] * 2,
        out_shape=[grid] * 2,
        compiler_params=pltpu.CompilerParams(vmem_limit_bytes=MOST_VMEM),
        cost_estimate=pl.CostEstimate(
            flops=60 * nx * nz, bytes_accessed=12 * nx * nz, transcendentals=0
        ),
    )(tf_table, code)


def split(value):
    high = value.astype(bf16)
    return high, (value - high.astype(f32)).astype(bf16)


def dot3(a, b):
    dot = functools.partial(jnp.dot, preferred_element_type=f32)
    return dot(a[0], b[0]) + (dot(a[0], b[1]) + dot(a[1], b[0]))


def turn_kernel(ny, planes, cells, turned, staged, placed, semaphores):
    blocks = len(staged)
    steps = placed.shape[1] // planes
    rows = planes * ny
    incoming = [
        [
            pltpu.make_async_copy(
                cells.at[pl.ds(step * rows, rows), pl.ds(LANE * k, LANE)],
                staged[k].at[pl.ds(step * rows, rows), :],
                semaphores.at[0, step, k],
            )
            for k in range(blocks)
        ]
        for step in range(steps)
    ]
    outgoing = [
        pltpu.make_async_copy(
            placed.at[:, pl.ds(step * planes, planes), :],
            turned.at[:, pl.ds(step * planes, planes), :],
            semaphores.at[1, step, 0],
        )
        for step in range(steps)
    ]
    for step in range(steps):
        for copy in incoming[step]:
            copy.start()
    for step in range(steps):
        for copy in incoming[step]:
            copy.wait()
        for y in range(ny):
            for x in range(step * planes, (step + 1) * planes, SUB):
                for k in range(blocks):
                    placed[y, x : x + SUB, LANE * k : LANE * (k + 1)] = staged[k][
                        pl.ds(x * ny + y, SUB, stride=ny), :
                    ]
        outgoing[step].start()
    for copy in outgoing:
        copy.wait()


def turn(observed):
    slab, ny, nz = observed.shape
    planes = 2 * SUB if slab % (2 * SUB) == 0 else SUB
    anywhere = pl.BlockSpec(memory_space=pltpu.HBM)
    return pl.pallas_call(
        functools.partial(turn_kernel, ny, planes),
        in_specs=[anywhere],
        out_specs=anywhere,
        out_shape=jax.ShapeDtypeStruct((ny, slab, nz), f32),
        scratch_shapes=[
            [pltpu.VMEM((slab * ny, LANE), f32)] * (nz // LANE),
            pltpu.VMEM((ny, slab, nz), f32),
            pltpu.SemaphoreType.DMA((2, slab // planes, nz // LANE)),
        ],
        compiler_params=pltpu.CompilerParams(vmem_limit_bytes=MOST_VMEM),
        cost_estimate=pl.CostEstimate(
            flops=0, bytes_accessed=8 * slab * ny * nz, transcendentals=0
        ),
    )(observed.reshape(slab * ny, nz))


def window_tiles(width, nz):
    return width * nz // (SUB * LANE)


def filter_kernel(first, halo, slab, *refs):
    cells, ztab_far, small_far, odd_far, refs = refs[0], refs[1], refs[2], refs[3], refs[4:]
    if first:
        data_far, prior_far, windows_far, kept_far, refs = refs[0], refs[1], refs[2], refs[3], refs[4:]
    else:
        kept_far, prior_far, windows, refs = refs[0], refs[1], refs[2], refs[3:]
    ztab, small, odd, scale, other, high, low, padded, semaphores, refs = refs[:9] + (refs[9:],)
    if first:
        windows, window_semaphores, cells_near = refs
        cells_copy = pltpu.make_async_copy(cells, cells_near, semaphores.at[7])
        cells_copy.start()
        cells = cells_near
    devices, rows, _, nz = cells.shape
    nx = devices * slab
    half, quarter = nx // 2, nx // 4
    width = slab + 2 * halo
    blocks = nz // LANE
    arrivals = [
        pltpu.make_async_copy(ztab_far, ztab, semaphores.at[0]),
        pltpu.make_async_copy(small_far, small, semaphores.at[1]),
        pltpu.make_async_copy(odd_far.at[0], odd.at[0], semaphores.at[2]),
        pltpu.make_async_copy(prior_far, scale, semaphores.at[3]),
    ]
    if first:
        arrivals.append(pltpu.make_async_copy(data_far, other.at[0], semaphores.at[4]))
    last_arrival = pltpu.make_async_copy(odd_far.at[1], odd.at[1], semaphores.at[5])
    for copy in arrivals:
        copy.start()

    def table(ref, i, rows=slice(None)):
        return ref[i, 0, rows], ref[i, 1, rows]

    def store(spot, value):
        high[spot], low[spot] = split(value)

    def load(spot):
        return high[spot], low[spot]

    parts = [slice(i * quarter, (i + 1) * quarter) for i in range(4)]
    folds = [parts[0], parts[1], slice(half, nx)]
    for r in range(rows):
        if not first:
            kept_copy = pltpu.make_async_copy(kept_far.at[r], other.at[0], semaphores.at[4])
            kept_copy.start()
        if r == 0:
            last_arrival.start()
        if first and r == 0:
            cells_copy.wait()
        q = [
            cells[i * devices // 4 : (i + 1) * devices // 4, r].reshape(quarter, nz)
            for i in range(4)
        ]
        even = (q[0] + q[2], q[1] + q[3])
        folded = (even[0] + even[1], even[0] - even[1], q[0] - q[2], q[1] - q[3])
        if r == 0:
            arrivals[0].wait()
        ztable = (ztab[0], ztab[1])
        for spot, value in zip(parts, folded):
            store(spot, dot3(split(value), ztable))
        if r == 0:
            arrivals[1].wait()
        waves = [dot3(table(small, i), load(folds[i])) for i in range(2)]
        if r == 0:
            arrivals[2].wait()
        for i in range(2):
            waves.append(dot3(table(odd, 0, parts[i]), load(folds[2])))
        if r == 0:
            for copy in arrivals[3:]:
                copy.wait()
        if not first:
            kept_copy.wait()
        for spot, wave in zip(parts, waves):
            if first:
                seen = wave * other[0, spot]
                other[1, spot] = seen
                store(spot, seen + wave * (UNIT * scale[spot]))
            else:
                store(spot, other[0, spot] + wave * scale[spot])
        if first:
            kept_copy = pltpu.make_async_copy(other.at[1], kept_far.at[r], semaphores.at[6])
            kept_copy.start()
        after = (halo + nx) // SUB * SUB
        padded[:SUB] = jnp.zeros((SUB, nz), f32)
        padded[after : after + 2 * SUB] = jnp.zeros((2 * SUB, nz), f32)
        plus, minus = dot3(table(small, 0), load(folds[0])), dot3(table(small, 2), load(folds[1]))
        if r == 0:
            last_arrival.wait()
        leaving = []
        written, sent = set(), set()
        for i, e in enumerate((plus + minus, plus - minus)):
            o = dot3(table(odd, 1, parts[i]), load(folds[2]))
            for j, value in ((i, e + o), (i + 2, e - o)):
                place = halo + j * quarter
                padded[place : place + quarter] = dot3(split(value), ztable)
                written |= set(range(j * quarter, (j + 1) * quarter))
            for device in range(devices):
                needed = range(device * slab - halo, (device + 1) * slab + halo)
                if device in sent or not written.issuperset(x for x in needed if 0 <= x < nx):
                    continue
                sent.add(device)
                for g in range(width // SUB):
                    spot = device * slab + SUB * g
                    for k in range(blocks):
                        windows[device, r, g * blocks + k] = padded[
                            spot : spot + SUB, LANE * k : LANE * (k + 1)
                        ]
                rest = width % SUB
                spot = device * slab + width - rest
                for k in range(blocks if rest else 0):
                    tile, row = width // SUB * blocks + k * rest // SUB, k * rest % SUB
                    windows[device, r, tile, row : row + rest] = padded[
                        spot : spot + rest, LANE * k : LANE * (k + 1)
                    ]
                if first:
                    copy = pltpu.make_async_copy(
                        windows.at[device, r], windows_far.at[device, r], window_semaphores.at[device]
                    )
                    copy.start()
                    leaving.append(copy)
        if first:
            for copy in leaving:
                copy.wait()
            kept_copy.wait()


def run_filter(first, halo, cells, tables, far):
    devices, rows, slab, nz = cells.shape
    nx = devices * slab
    ztab, small, odd = tables
    vmem = pl.BlockSpec(memory_space=pltpu.VMEM)
    hbm = pl.BlockSpec(memory_space=pltpu.HBM)
    windows = (devices, rows, window_tiles(slab + 2 * halo, nz), SUB, LANE)
    out_shape, out_specs = [jax.ShapeDtypeStruct(windows, f32)], [hbm if first else vmem]
    if first:
        out_shape.append(jax.ShapeDtypeStruct((rows, nx, nz), f32))
        out_specs.append(hbm)
    scratch_shapes = [
        pltpu.VMEM(ztab.shape, bf16),
        pltpu.VMEM(small.shape, bf16),
        pltpu.VMEM(odd.shape, bf16),
        pltpu.VMEM((nx, nz), f32),
        pltpu.VMEM((2, nx, nz), f32),
        pltpu.VMEM((nx, nz), bf16),
        pltpu.VMEM((nx, nz), bf16),
        pltpu.VMEM((nx + 3 * SUB, nz), f32),
        pltpu.SemaphoreType.DMA((8,)),
    ]
    if first:
        scratch_shapes += [
            pltpu.VMEM(windows, f32),
            pltpu.SemaphoreType.DMA((devices,)),
            pltpu.VMEM(cells.shape, f32),
        ]
    return pl.pallas_call(
        functools.partial(filter_kernel, first, halo, slab),
        in_specs=[hbm if first else vmem] + [hbm] * (3 + len(far)),
        out_specs=out_specs,
        out_shape=out_shape,
        scratch_shapes=scratch_shapes,
        compiler_params=pltpu.CompilerParams(
            vmem_limit_bytes=MOST_VMEM if first else 32 * MIB
        ),
        cost_estimate=pl.CostEstimate(
            flops=6 * rows * nx * nz * (2 * nz + nx),
            bytes_accessed=8 * rows * nx * nz,
            transcendentals=0,
        ),
    )(cells, ztab, small, odd, *far)


def lane_sums(pieces):
    lane = lax.broadcasted_iota(jnp.int32, pieces[0].shape, 1)
    up = [pltpu.roll(piece, LANE - 1, 1) for piece in pieces]
    down = [pltpu.roll(piece, 1, 1) for piece in pieces]
    sums = []
    for k in range(len(pieces)):
        above = up[k + 1] if k + 1 < len(pieces) else 0.0
        below = down[k - 1] if k > 0 else 0.0
        sums.append(
            jnp.where(lane == LANE - 1, above, up[k]) + jnp.where(lane == 0, below, down[k])
        )
    return sums


def row_sums(groups):
    row = lax.broadcasted_iota(jnp.int32, groups[0].shape, 0)
    up = [pltpu.roll(group, SUB - 1, 0) for group in groups]
    down = [pltpu.roll(group, 1, 0) for group in groups]
    count = len(groups)
    return [
        jnp.where(row == SUB - 1, up[(g + 1) % count], up[g])
        + jnp.where(row == 0, down[g - 1], down[g])
        for g in range(count)
    ]


def passes_kernel(first, last, halo, slab, nx, start_ref, target, *refs):
    if first:
        duals_in, refs = None, refs
    else:
        duals_in, refs = refs[:3], refs[3:]
    if last:
        restored, refs = refs[0], refs[1:]
    else:
        current, duals_out, refs = refs[0], refs[1:4], refs[4:]
    lead, field, dual_x, dual_y, dual_z = refs[:5]
    turned = refs[5:-1] if last else ()
    ny, _, nz = field.shape
    width = slab + 2 * halo
    groups = padded_to(width, SUB) // SUB
    blocks = nz // LANE
    decay = 1.0 / (1.0 + step_dual * huber_eps / bound_dual)
    gain = step_dual * decay
    floor = 1.0 / (decay * decay)
    keep = 1.0 / (1.0 + step_primal)
    pull = step_primal * keep
    push = pull * gain / decay
    origin = start_ref[0] - halo

    def goal_of(y, g, k):
        if SUB * (g + 1) <= width:
            return target[y, g * blocks + k]
        rest = width % SUB
        tail = target[y, g * blocks + k * rest // SUB]
        shift = k * rest % SUB
        return pltpu.roll(tail, SUB - shift, 0) if shift else tail

    def masked(value, g):
        if SUB * g >= halo and SUB * (g + 1) <= width - halo:
            return value
        place = origin + SUB * g + lax.broadcasted_iota(jnp.int32, (SUB, LANE), 0)
        return jnp.where((place >= 0) & (place < nx), value, 0.0)

    def at(g, k):
        return pl.ds(SUB * g, SUB), pl.ds(LANE * k, LANE)

    empty = jnp.zeros(lead.shape[1:], f32)
    for plane in (0, ny + 1):
        lead[plane] = empty
        dual_y[plane] = empty

    @pl.loop(0, ny, unroll=UNROLL)
    def _(y):
        for g in range(groups):
            for k in range(blocks):
                lead[(y + 1,) + at(g, k)] = goal_of(y, g, k)

    for sweep in range(PASSES):
        final = sweep == PASSES - 1

        @pl.loop(0, ny, unroll=UNROLL)
        def _(y):
            here = [[lead[(y + 1,) + at(g, k)] for k in range(blocks)] for g in range(groups)]
            columns = [row_sums([here[g][k] for g in range(groups)]) for k in range(blocks)]
            for g in range(groups):
                along_z = lane_sums(here[g])
                for k in range(blocks):
                    spot = at(g, k)
                    twice = here[g][k] + here[g][k]
                    along_y = lead[(y,) + spot] + lead[(y + 2,) + spot]
                    raised = [columns[k][g] - twice, along_y - twice, along_z[k] - twice]
                    if sweep > 0:
                        before = [dual_x[(y,) + spot], dual_y[(y + 1,) + spot], dual_z[(y,) + spot]]
                    elif duals_in is not None:
                        before = [ref[(y,) + spot] for ref in duals_in]
                    else:
                        before = None
                    if before is not None:
                        raised = [old + new for old, new in zip(before, raised)]
                    total = (
                        raised[0] * raised[0] + raised[1] * raised[1] + raised[2] * raised[2]
                    )
                    shrink = lax.rsqrt(jnp.maximum(floor, total))
                    made = [raised[0] * masked(shrink, g), raised[1] * shrink, raised[2] * shrink]
                    dual_x[(y,) + spot] = made[0]
                    dual_y[(y + 1,) + spot] = made[1]
                    dual_z[(y,) + spot] = made[2]
                    if final and not last:
                        shift = halo - HALO_LAST
                        lo = max(0, shift - SUB * g)
                        hi = min(SUB, slab + 2 * HALO_LAST + shift - SUB * g)
                        if lo < hi:
                            rows = pl.ds(SUB * g + lo - shift, hi - lo)
                            for a in range(3):
                                duals_out[a][y, rows, spot[1]] = made[a][lo:hi]

        @pl.loop(0, ny, unroll=UNROLL)
        def _(y):
            wanted = range(groups)
            if final:
                wanted = [
                    g for g in wanted if SUB * (g + 1) > halo and SUB * g < width - halo
                ]
            near = [[dual_x[(y,) + at(g, k)] for k in range(blocks)] for g in range(groups)]
            columns = [row_sums([near[g][k] for g in range(groups)]) for k in range(blocks)]
            for g in wanted:
                here = [dual_z[(y,) + at(g, k)] for k in range(blocks)]
                along_z = lane_sums(here)
                for k in range(blocks):
                    spot = at(g, k)
                    along_y = dual_y[(y,) + spot] + dual_y[(y + 2,) + spot]
                    centre = near[g][k] + dual_y[(y + 1,) + spot] + here[k]
                    adjoint = columns[k][g] + along_y + along_z[k] - (centre + centre)
                    goal = goal_of(y, g, k)
                    if sweep == 0:
                        move = push * adjoint
                        updated = goal - move
                        ahead = updated - move
                    else:
                        old = field[(y,) + spot]
                        whole = UNIT if final and last else 1.0
                        updated = (keep / whole) * old + (pull / whole) * goal
                        updated = updated - (push / whole) * adjoint
                        ahead = updated + updated - old
                    if not final:
                        field[(y,) + spot] = updated
                        lead[(y + 1,) + spot] = masked(ahead, g)
                        continue
                    lo = max(0, halo - SUB * g)
                    hi = min(SUB, slab + halo - SUB * g)
                    x = SUB * g + lo - halo
                    if last:
                        turned[k][pl.ds(x * ny + y, hi - lo, stride=ny), :] = updated[lo:hi]
                    else:
                        current[y, pl.ds(x, hi - lo), spot[1]] = updated[lo:hi]

    copies = [
        pltpu.make_async_copy(
            block, restored.at[:, pl.ds(LANE * k, LANE)], refs[-1].at[k]
        )
        for k, block in enumerate(turned)
    ]
    for copy in copies:
        copy.start()
    for copy in copies:
        copy.wait()


def run_passes(first, last, halo, slab, nx, start, target, duals):
    ny = target.shape[0]
    nz = target.shape[1] * SUB * LANE // (slab + 2 * halo)
    width = padded_to(slab + 2 * halo, SUB)
    vmem = pl.BlockSpec(memory_space=pltpu.VMEM)
    if last:
        out_shape = jax.ShapeDtypeStruct((slab * ny, nz), f32)
        out_specs = pl.BlockSpec(memory_space=pltpu.HBM)
    else:
        kept = jax.ShapeDtypeStruct((ny, slab + 2 * HALO_LAST, nz), f32)
        out_shape = [jax.ShapeDtypeStruct((ny, slab, nz), f32), kept, kept, kept]
        out_specs = [vmem] * 4
    return pl.pallas_call(
        functools.partial(passes_kernel, first, last, halo, slab, nx),
        in_specs=[pl.BlockSpec(memory_space=pltpu.SMEM)] + [vmem] * (1 + len(duals)),
        out_specs=out_specs,
        out_shape=out_shape,
        scratch_shapes=[
            pltpu.VMEM((ny + 2, width, nz), f32),
            pltpu.VMEM((ny, width, nz), f32),
            pltpu.VMEM((ny, width, nz), f32),
            pltpu.VMEM((ny + 2, width, nz), f32),
            pltpu.VMEM((ny, width, nz), f32),
        ]
        + [pltpu.VMEM((slab * ny, LANE), f32)] * (nz // LANE if last else 0)
        + [pltpu.SemaphoreType.DMA((nz // LANE,))] * last,
        compiler_params=pltpu.CompilerParams(vmem_limit_bytes=40 * MIB),
        cost_estimate=pl.CostEstimate(
            flops=60 * PASSES * ny * width * nz,
            bytes_accessed=8 * 4 * ny * width * nz,
            transcendentals=PASSES * ny * width * nz,
        ),
    )(start, target, *duals)


def exchange(blocks):
    return lax.all_to_all(blocks, "gy", split_axis=0, concat_axis=0, tiled=True)


def local(observed, tf_table, tilt_index, wedge):
    slab, ny, nz = observed.shape
    devices = lax.axis_size("gy")
    rows = ny // devices
    nx = slab * devices
    start = (lax.axis_index("gy") * slab).astype(jnp.int32).reshape(1)
    tables = [jnp.asarray(table) for table in (z_table(nz),) + x_tables(nx)]
    cells = exchange(turn(observed).reshape(devices, rows, slab, nz))
    data, prior = make_weights(tf_table, tilt_index, wedge, nx, nz)
    duals = ()
    for outer in range(OUTER):
        first, last = outer == 0, outer == OUTER - 1
        halo = HALO_LAST if last else HALO_FIRST
        made = run_filter(first, halo, cells, tables, (data, prior) if first else (kept, prior))
        if first:
            kept = made[1]
        windows = exchange(made[0])
        target = windows.reshape((ny,) + windows.shape[2:])
        made = run_passes(first, last, halo, slab, nx, start, target, duals)
        if last:
            return made.reshape(slab, ny, nz)
        duals = tuple(made[1:])
        cells = exchange(made[0].reshape(devices, rows, slab, nz))


def solution(mesh):
    in_specs = (P(("groups", "gy"), None, None), P(), P(), P())
    out_specs = P(("groups", "gy"), None, None)
    return jax.shard_map(local, mesh=mesh, in_specs=in_specs, out_specs=out_specs, check_vma=False)
```

```python
import functools

import jax
import jax.numpy as jnp
import ml_dtypes
import numpy as np
from jax import lax
from jax.experimental import pallas as pl
from jax.experimental.pallas import tpu as pltpu
from jax.sharding import PartitionSpec as P

OUTER = 2
PASSES = 2

step_dual = 0.14
step_primal = 0.14
huber_eps = 0.05
bound_dual = 0.5

SUB = 8
LANE = 128
HALO_LAST = 2 * PASSES
HALO_FIRST = HALO_LAST + 2 * PASSES - 2
UNROLL = 8
COLUMN = 3
MIB = 1024 * 1024
MOST_VMEM = 61 * MIB

f32 = jnp.float32
bf16 = jnp.bfloat16

UNIT = step_dual / bound_dual


def halves(table):
    high = table.astype(ml_dtypes.bfloat16)
    low = (table - high.astype(np.float64)).astype(ml_dtypes.bfloat16)
    return np.stack([high, low])


def cas(rows, columns, length):
    phase = (rows[:, None] * columns[None, :]) % length
    angle = phase * (2.0 * np.pi / length)
    return np.cos(angle) + np.sin(angle)


def z_table(length):
    index = np.arange(length)
    return halves(cas(index, index, length))


def x_tables(length):
    half, quarter = length // 2, length // 4
    place = np.arange(half)
    fourth = cas(4 * place[:quarter], place[:quarter], length)
    second = cas(4 * place[:quarter] + 2, place[:quarter], length)
    odd = cas(2 * place + 1, place, length)
    small = np.stack([halves(fourth), halves(second), halves(second.T)])
    return small, np.stack([halves(odd), halves(odd.T)])


def kx_rows(length):
    half, quarter = length // 2, length // 4
    return ((0, quarter, 4, 0), (quarter, quarter, 4, 2), (half, half, 2, 1))


def padded_to(length, unit):
    return -(-length // unit) * unit


def weights_kernel(nx, nz, levels, table_ref, code_ref, data, prior):
    heights, widths = code_ref.shape
    scale = 1.0 / (nx * nz)
    kz = lax.broadcasted_iota(jnp.int32, (heights, nz), 1)
    kz = jnp.minimum(kz, nz - kz)
    pick_z = jnp.where(kz == lax.broadcasted_iota(jnp.int32, (heights, nz), 0), 1.0, 0.0)
    pick_z = pick_z.astype(bf16)
    for base, count, step, least in kx_rows(nx):
        tile = min(256, count)
        for top in range(0, count, tile):
            kx = step * (top + lax.broadcasted_iota(jnp.int32, (tile, widths), 0)) + least
            kx = jnp.minimum(kx, nx - kx)
            pick_x = jnp.where(kx == lax.broadcasted_iota(jnp.int32, (tile, widths), 1), 1.0, 0.0)
            tall = lax.dot_general(
                pick_x.astype(bf16),
                code_ref[...],
                (((1,), (1,)), ((), ())),
                preferred_element_type=f32,
            )
            spread = jnp.dot(tall.astype(bf16), pick_z, preferred_element_type=f32)
            response = jnp.zeros_like(spread)
            for level in range(levels):
                response = jnp.where(spread == level + 1.0, table_ref[level], response)
            gain = scale / (response * response + 1.0)
            rows = slice(base + top, base + top + tile)
            prior[rows] = gain
            data[rows] = (UNIT * response) * gain


def make_weights(tf_table, tilt_index, wedge, nx, nz):
    levels = tf_table.shape[0]
    code = jnp.where(wedge > 0, tilt_index + 1, 0).T
    extra = [(0, padded_to(size, LANE) - size) for size in code.shape]
    code = jnp.pad(code, extra).astype(bf16)
    grid = jax.ShapeDtypeStruct((nx, nz), f32)
    vmem = pl.BlockSpec(memory_space=pltpu.VMEM)
    return pl.pallas_call(
        functools.partial(weights_kernel, nx, nz, levels),
        in_specs=[pl.BlockSpec(memory_space=pltpu.SMEM), vmem],
        out_specs=[vmem] * 2,
        out_shape=[grid] * 2,
        compiler_params=pltpu.CompilerParams(vmem_limit_bytes=MOST_VMEM),
        cost_estimate=pl.CostEstimate(
            flops=60 * nx * nz, bytes_accessed=12 * nx * nz, transcendentals=0
        ),
    )(tf_table, code)


def split(value):
    high = value.astype(bf16)
    return high, (value - high.astype(f32)).astype(bf16)


def dot3(a, b):
    wide = jnp.concatenate([a[0], a[0], a[1]], axis=1)
    tall = jnp.concatenate([b[0], b[1], b[0]], axis=0)
    return jnp.dot(wide, tall, preferred_element_type=f32)


def turn_kernel(ny, planes, cells, turned, staged, placed, semaphores):
    blocks = len(staged)
    steps = placed.shape[1] // planes
    rows = planes * ny
    incoming = [
        [
            pltpu.make_async_copy(
                cells.at[pl.ds(step * rows, rows), pl.ds(LANE * k, LANE)],
                staged[k].at[pl.ds(step * rows, rows), :],
                semaphores.at[0, step, k],
            )
            for k in range(blocks)
        ]
        for step in range(steps)
    ]
    outgoing = [
        pltpu.make_async_copy(
            placed.at[:, pl.ds(step * planes, planes), :],
            turned.at[:, pl.ds(step * planes, planes), :],
            semaphores.at[1, step, 0],
        )
        for step in range(steps)
    ]
    for step in range(steps):
        for copy in incoming[step]:
            copy.start()
    for step in range(steps):
        for copy in incoming[step]:
            copy.wait()
        for y in range(ny):
            for x in range(step * planes, (step + 1) * planes, SUB):
                for k in range(blocks):
                    placed[y, x : x + SUB, LANE * k : LANE * (k + 1)] = staged[k][
                        pl.ds(x * ny + y, SUB, stride=ny), :
                    ]
        outgoing[step].start()
    for copy in outgoing:
        copy.wait()


def turn(observed):
    slab, ny, nz = observed.shape
    planes = 2 * SUB if slab % (2 * SUB) == 0 else SUB
    anywhere = pl.BlockSpec(memory_space=pltpu.HBM)
    return pl.pallas_call(
        functools.partial(turn_kernel, ny, planes),
        in_specs=[anywhere],
        out_specs=anywhere,
        out_shape=jax.ShapeDtypeStruct((ny, slab, nz), f32),
        scratch_shapes=[
            [pltpu.VMEM((slab * ny, LANE), f32)] * (nz // LANE),
            pltpu.VMEM((ny, slab, nz), f32),
            pltpu.SemaphoreType.DMA((2, slab // planes, nz // LANE)),
        ],
        compiler_params=pltpu.CompilerParams(vmem_limit_bytes=MOST_VMEM),
        cost_estimate=pl.CostEstimate(
            flops=0, bytes_accessed=8 * slab * ny * nz, transcendentals=0
        ),
    )(observed.reshape(slab * ny, nz))


def window_tiles(width, nz):
    return width * nz // (SUB * LANE)


def filter_kernel(first, halo, slab, *refs):
    cells, ztab_far, small_far, odd_far, refs = refs[0], refs[1], refs[2], refs[3], refs[4:]
    if first:
        data_far, prior_far, windows_far, kept_far, refs = refs[0], refs[1], refs[2], refs[3], refs[4:]
    else:
        kept_far, prior_far, windows, refs = refs[0], refs[1], refs[2], refs[3:]
    ztab, small, odd, scale, other, high, low, padded, semaphores, refs = refs[:9] + (refs[9:],)
    if first:
        windows, window_semaphores = refs
    devices, rows, _, nz = cells.shape
    nx = devices * slab
    half, quarter = nx // 2, nx // 4
    width = slab + 2 * halo
    blocks = nz // LANE
    arrivals = [
        pltpu.make_async_copy(ztab_far, ztab, semaphores.at[0]),
        pltpu.make_async_copy(small_far, small, semaphores.at[1]),
        pltpu.make_async_copy(odd_far.at[0], odd.at[0], semaphores.at[2]),
        pltpu.make_async_copy(prior_far, scale, semaphores.at[3]),
    ]
    if first:
        arrivals.append(pltpu.make_async_copy(data_far, other.at[0], semaphores.at[4]))
    last_arrival = pltpu.make_async_copy(odd_far.at[1], odd.at[1], semaphores.at[5])
    for copy in arrivals:
        copy.start()

    def table(ref, i, rows=slice(None)):
        return ref[i, 0, rows], ref[i, 1, rows]

    def store(spot, value):
        high[spot], low[spot] = split(value)

    def load(spot):
        return high[spot], low[spot]

    parts = [slice(i * quarter, (i + 1) * quarter) for i in range(4)]
    folds = [parts[0], parts[1], slice(half, nx)]
    for r in range(rows):
        if not first:
            kept_copy = pltpu.make_async_copy(kept_far.at[r], other.at[0], semaphores.at[4])
            kept_copy.start()
        if r == 0:
            last_arrival.start()
        q = [
            cells[i * devices // 4 : (i + 1) * devices // 4, r].reshape(quarter, nz)
            for i in range(4)
        ]
        even = (q[0] + q[2], q[1] + q[3])
        folded = (even[0] + even[1], even[0] - even[1], q[0] - q[2], q[1] - q[3])
        if r == 0:
            arrivals[0].wait()
        ztable = (ztab[0], ztab[1])
        for spot, value in zip(parts, folded):
            store(spot, dot3(split(value), ztable))
        if r == 0:
            arrivals[1].wait()
        waves = [dot3(table(small, i), load(folds[i])) for i in range(2)]
        if r == 0:
            arrivals[2].wait()
        for i in range(2):
            waves.append(dot3(table(odd, 0, parts[i]), load(folds[2])))
        if r == 0:
            for copy in arrivals[3:]:
                copy.wait()
        if not first:
            kept_copy.wait()
        for spot, wave in zip(parts, waves):
            if first:
                seen = wave * other[0, spot]
                other[1, spot] = seen
                store(spot, seen + wave * (UNIT * scale[spot]))
            else:
                store(spot, other[0, spot] + wave * scale[spot])
        if first:
            kept_copy = pltpu.make_async_copy(other.at[1], kept_far.at[r], semaphores.at[6])
            kept_copy.start()
        after = (halo + nx) // SUB * SUB
        padded[:SUB] = jnp.zeros((SUB, nz), f32)
        padded[after : after + 2 * SUB] = jnp.zeros((2 * SUB, nz), f32)
        plus, minus = dot3(table(small, 0), load(folds[0])), dot3(table(small, 2), load(folds[1]))
        if r == 0:
            last_arrival.wait()
        leaving = []
        written, sent = set(), set()
        for i, e in enumerate((plus + minus, plus - minus)):
            o = dot3(table(odd, 1, parts[i]), load(folds[2]))
            for j, value in ((i, e + o), (i + 2, e - o)):
                place = halo + j * quarter
                padded[place : place + quarter] = dot3(split(value), ztable)
                written |= set(range(j * quarter, (j + 1) * quarter))
            for device in range(devices):
                needed = range(device * slab - halo, (device + 1) * slab + halo)
                if device in sent or not written.issuperset(x for x in needed if 0 <= x < nx):
                    continue
                sent.add(device)
                for g in range(width // SUB):
                    spot = device * slab + SUB * g
                    for k in range(blocks):
                        windows[device, r, g * blocks + k] = padded[
                            spot : spot + SUB, LANE * k : LANE * (k + 1)
                        ]
                rest = width % SUB
                spot = device * slab + width - rest
                for k in range(blocks if rest else 0):
                    tile, row = width // SUB * blocks + k * rest // SUB, k * rest % SUB
                    windows[device, r, tile, row : row + rest] = padded[
                        spot : spot + rest, LANE * k : LANE * (k + 1)
                    ]
                if first:
                    copy = pltpu.make_async_copy(
                        windows.at[device, r], windows_far.at[device, r], window_semaphores.at[device]
                    )
                    copy.start()
                    leaving.append(copy)
        if first:
            for copy in leaving:
                copy.wait()
            kept_copy.wait()


def run_filter(first, halo, cells, tables, far):
    devices, rows, slab, nz = cells.shape
    nx = devices * slab
    ztab, small, odd = tables
    vmem = pl.BlockSpec(memory_space=pltpu.VMEM)
    hbm = pl.BlockSpec(memory_space=pltpu.HBM)
    windows = (devices, rows, window_tiles(slab + 2 * halo, nz), SUB, LANE)
    out_shape, out_specs = [jax.ShapeDtypeStruct(windows, f32)], [hbm if first else vmem]
    if first:
        out_shape.append(jax.ShapeDtypeStruct((rows, nx, nz), f32))
        out_specs.append(hbm)
    scratch_shapes = [
        pltpu.VMEM(ztab.shape, bf16),
        pltpu.VMEM(small.shape, bf16),
        pltpu.VMEM(odd.shape, bf16),
        pltpu.VMEM((nx, nz), f32),
        pltpu.VMEM((2, nx, nz), f32),
        pltpu.VMEM((nx, nz), bf16),
        pltpu.VMEM((nx, nz), bf16),
        pltpu.VMEM((nx + 3 * SUB, nz), f32),
        pltpu.SemaphoreType.DMA((7,)),
    ]
    if first:
        scratch_shapes += [
            pltpu.VMEM(windows, f32),
            pltpu.SemaphoreType.DMA((devices,)),
        ]
    return pl.pallas_call(
        functools.partial(filter_kernel, first, halo, slab),
        in_specs=[vmem] + [hbm] * (3 + len(far)),
        out_specs=out_specs,
        out_shape=out_shape,
        scratch_shapes=scratch_shapes,
        compiler_params=pltpu.CompilerParams(
            vmem_limit_bytes=MOST_VMEM if first else 32 * MIB
        ),
        cost_estimate=pl.CostEstimate(
            flops=6 * rows * nx * nz * (2 * nz + nx),
            bytes_accessed=8 * rows * nx * nz,
            transcendentals=0,
        ),
    )(cells, ztab, small, odd, *far)


def lane_sums(pieces):
    lane = lax.broadcasted_iota(jnp.int32, pieces[0].shape, 1)
    up = [pltpu.roll(piece, LANE - 1, 1) for piece in pieces]
    down = [pltpu.roll(piece, 1, 1) for piece in pieces]
    sums = []
    for k in range(len(pieces)):
        above = up[k + 1] if k + 1 < len(pieces) else 0.0
        below = down[k - 1] if k > 0 else 0.0
        sums.append(
            jnp.where(lane == LANE - 1, above, up[k]) + jnp.where(lane == 0, below, down[k])
        )
    return sums


def row_sums(groups):
    return inner_row_sums([groups[-1]] + groups + [groups[0]])


def inner_row_sums(groups):
    row = lax.broadcasted_iota(jnp.int32, groups[0].shape, 0)
    up = [pltpu.roll(group, SUB - 1, 0) for group in groups]
    down = [pltpu.roll(group, 1, 0) for group in groups]
    return [
        jnp.where(row == SUB - 1, up[g + 1], up[g]) + jnp.where(row == 0, down[g - 1], down[g])
        for g in range(1, len(groups) - 1)
    ]


def passes_kernel(first, last, halo, slab, nx, start_ref, target, *refs):
    if first:
        duals_in, refs = None, refs
    else:
        duals_in, refs = refs[:3], refs[3:]
    if last:
        restored, refs = refs[0], refs[1:]
    else:
        current, duals_out, refs = refs[0], refs[1:4], refs[4:]
    lead, field, dual_x, dual_y, dual_z = refs[:5]
    turned = refs[5:-1] if last else ()
    ny, _, nz = field.shape
    width = slab + 2 * halo
    groups = padded_to(width, SUB) // SUB
    blocks = nz // LANE
    decay = 1.0 / (1.0 + step_dual * huber_eps / bound_dual)
    gain = step_dual * decay
    floor = 1.0 / (decay * decay)
    keep = 1.0 / (1.0 + step_primal)
    pull = step_primal * keep
    push = pull * gain / decay
    origin = start_ref[0] - halo

    def goal_of(y, g, k):
        if SUB * (g + 1) <= width:
            return target[y, g * blocks + k]
        rest = width % SUB
        tail = target[y, g * blocks + k * rest // SUB]
        shift = k * rest % SUB
        return pltpu.roll(tail, SUB - shift, 0) if shift else tail

    def masked(value, g):
        if SUB * g >= halo and SUB * (g + 1) <= width - halo:
            return value
        place = origin + SUB * g + lax.broadcasted_iota(jnp.int32, (SUB, LANE), 0)
        return jnp.where((place >= 0) & (place < nx), value, 0.0)

    def at(g, k):
        return pl.ds(SUB * g, SUB), pl.ds(LANE * k, LANE)

    empty = jnp.zeros(lead.shape[1:], f32)
    for plane in (0, ny + 1):
        lead[plane] = empty
        dual_y[plane] = empty

    @pl.loop(0, ny, unroll=UNROLL)
    def _(y):
        for g in range(groups):
            for k in range(blocks):
                lead[(y + 1,) + at(g, k)] = goal_of(y, g, k)

    leaving = []
    for sweep in range(PASSES):
        final = sweep == PASSES - 1

        @pl.loop(0, ny, unroll=UNROLL)
        def _(y):
            here = [[lead[(y + 1,) + at(g, k)] for k in range(blocks)] for g in range(groups)]
            columns = [row_sums([here[g][k] for g in range(groups)]) for k in range(blocks)]
            for g in range(groups):
                along_z = lane_sums(here[g])
                for k in range(blocks):
                    spot = at(g, k)
                    twice = here[g][k] + here[g][k]
                    along_y = lead[(y,) + spot] + lead[(y + 2,) + spot]
                    raised = [columns[k][g] - twice, along_y - twice, along_z[k] - twice]
                    if sweep > 0:
                        before = [dual_x[(y,) + spot], dual_y[(y + 1,) + spot], dual_z[(y,) + spot]]
                    elif duals_in is not None:
                        before = [ref[(y,) + spot] for ref in duals_in]
                    else:
                        before = None
                    if before is not None:
                        raised = [old + new for old, new in zip(before, raised)]
                    total = (
                        raised[0] * raised[0] + raised[1] * raised[1] + raised[2] * raised[2]
                    )
                    shrink = lax.rsqrt(jnp.maximum(floor, total))
                    made = [raised[0] * masked(shrink, g), raised[1] * shrink, raised[2] * shrink]
                    dual_x[(y,) + spot] = made[0]
                    dual_y[(y + 1,) + spot] = made[1]
                    dual_z[(y,) + spot] = made[2]
                    if final and not last:
                        shift = halo - HALO_LAST
                        lo = max(0, shift - SUB * g)
                        hi = min(SUB, slab + 2 * HALO_LAST + shift - SUB * g)
                        if lo < hi:
                            rows = pl.ds(SUB * g + lo - shift, hi - lo)
                            for a in range(3):
                                duals_out[a][y, rows, spot[1]] = made[a][lo:hi]

        wanted = list(range(groups))
        if final:
            wanted = [g for g in wanted if SUB * (g + 1) > halo and SUB * g < width - halo]
        column = COLUMN if final and last else len(wanted)
        for some in [wanted[i : i + column] for i in range(0, len(wanted), column)]:

            @pl.loop(0, ny, unroll=UNROLL)
            def _(y):
                around = [some[0] - 1] + some + [some[-1] + 1]
                near = {
                    g: [dual_x[(y,) + at(g % groups, k)] for k in range(blocks)] for g in around
                }
                columns = [inner_row_sums([near[g][k] for g in around]) for k in range(blocks)]
                for place, g in enumerate(some):
                    here = [dual_z[(y,) + at(g, k)] for k in range(blocks)]
                    along_z = lane_sums(here)
                    for k in range(blocks):
                        spot = at(g, k)
                        along_y = dual_y[(y,) + spot] + dual_y[(y + 2,) + spot]
                        centre = near[g][k] + dual_y[(y + 1,) + spot] + here[k]
                        adjoint = columns[k][place] + along_y + along_z[k] - (centre + centre)
                        goal = goal_of(y, g, k)
                        if sweep == 0:
                            move = push * adjoint
                            updated = goal - move
                            ahead = updated - move
                        else:
                            old = field[(y,) + spot]
                            whole = UNIT if final and last else 1.0
                            updated = (keep / whole) * old + (pull / whole) * goal
                            updated = updated - (push / whole) * adjoint
                            ahead = updated + updated - old
                        if not final:
                            field[(y,) + spot] = updated
                            lead[(y + 1,) + spot] = masked(ahead, g)
                            continue
                        lo = max(0, halo - SUB * g)
                        hi = min(SUB, slab + halo - SUB * g)
                        x = SUB * g + lo - halo
                        if last:
                            turned[k][pl.ds(x * ny + y, hi - lo, stride=ny), :] = updated[lo:hi]
                        else:
                            current[y, pl.ds(x, hi - lo), spot[1]] = updated[lo:hi]

            if final and last:
                low = max(0, SUB * some[0] - halo) * ny
                high = min(slab, SUB * (some[-1] + 1) - halo) * ny
                for k, block in enumerate(turned):
                    copy = pltpu.make_async_copy(
                        block.at[pl.ds(low, high - low), :],
                        restored.at[pl.ds(low, high - low), pl.ds(LANE * k, LANE)],
                        refs[-1].at[len(leaving)],
                    )
                    copy.start()
                    leaving.append(copy)

    for copy in leaving:
        copy.wait()


def run_passes(first, last, halo, slab, nx, start, target, duals):
    ny = target.shape[0]
    nz = target.shape[1] * SUB * LANE // (slab + 2 * halo)
    width = padded_to(slab + 2 * halo, SUB)
    vmem = pl.BlockSpec(memory_space=pltpu.VMEM)
    if last:
        out_shape = jax.ShapeDtypeStruct((slab * ny, nz), f32)
        out_specs = pl.BlockSpec(memory_space=pltpu.HBM)
    else:
        kept = jax.ShapeDtypeStruct((ny, slab + 2 * HALO_LAST, nz), f32)
        out_shape = [jax.ShapeDtypeStruct((ny, slab, nz), f32), kept, kept, kept]
        out_specs = [vmem] * 4
    return pl.pallas_call(
        functools.partial(passes_kernel, first, last, halo, slab, nx),
        in_specs=[pl.BlockSpec(memory_space=pltpu.SMEM)] + [vmem] * (1 + len(duals)),
        out_specs=out_specs,
        out_shape=out_shape,
        scratch_shapes=[
            pltpu.VMEM((ny + 2, width, nz), f32),
            pltpu.VMEM((ny, width, nz), f32),
            pltpu.VMEM((ny, width, nz), f32),
            pltpu.VMEM((ny + 2, width, nz), f32),
            pltpu.VMEM((ny, width, nz), f32),
        ]
        + [pltpu.VMEM((slab * ny, LANE), f32)] * (nz // LANE if last else 0)
        + [pltpu.SemaphoreType.DMA((nz // LANE * width // SUB,))] * last,
        compiler_params=pltpu.CompilerParams(vmem_limit_bytes=40 * MIB),
        cost_estimate=pl.CostEstimate(
            flops=60 * PASSES * ny * width * nz,
            bytes_accessed=8 * 4 * ny * width * nz,
            transcendentals=PASSES * ny * width * nz,
        ),
    )(start, target, *duals)


def exchange(blocks):
    return lax.all_to_all(blocks, "gy", split_axis=0, concat_axis=0, tiled=True)


def local(observed, tf_table, tilt_index, wedge):
    slab, ny, nz = observed.shape
    devices = lax.axis_size("gy")
    rows = ny // devices
    nx = slab * devices
    start = (lax.axis_index("gy") * slab).astype(jnp.int32).reshape(1)
    tables = [jnp.asarray(table) for table in (z_table(nz),) + x_tables(nx)]
    cells = exchange(turn(observed).reshape(devices, rows, slab, nz))
    data, prior = make_weights(tf_table, tilt_index, wedge, nx, nz)
    duals = ()
    for outer in range(OUTER):
        first, last = outer == 0, outer == OUTER - 1
        halo = HALO_LAST if last else HALO_FIRST
        made = run_filter(first, halo, cells, tables, (data, prior) if first else (kept, prior))
        if first:
            kept = made[1]
        windows = exchange(made[0])
        target = windows.reshape((ny,) + windows.shape[2:])
        made = run_passes(first, last, halo, slab, nx, start, target, duals)
        if last:
            return made.reshape(slab, ny, nz)
        duals = tuple(made[1:])
        cells = exchange(made[0].reshape(devices, rows, slab, nz))


def solution(mesh):
    in_specs = (P(("groups", "gy"), None, None), P(), P(), P())
    out_specs = P(("groups", "gy"), None, None)
    return jax.shard_map(local, mesh=mesh, in_specs=in_specs, out_specs=out_specs, check_vma=False)
```

```python
import functools

import jax
import jax.numpy as jnp
import ml_dtypes
import numpy as np
from jax import lax
from jax.experimental import pallas as pl
from jax.experimental.pallas import tpu as pltpu
from jax.sharding import PartitionSpec as P

OUTER = 2
PASSES = 2

step_dual = 0.14
step_primal = 0.14
huber_eps = 0.05
bound_dual = 0.5

SUB = 8
LANE = 128
HALO_LAST = 2 * PASSES
HALO_FIRST = HALO_LAST + 2 * PASSES - 2
UNROLL = 8
COLUMN = 3
MIB = 1024 * 1024
MOST_VMEM = 61 * MIB

f32 = jnp.float32
bf16 = jnp.bfloat16

UNIT = step_dual / bound_dual


def halves(table):
    high = table.astype(ml_dtypes.bfloat16)
    low = (table - high.astype(np.float64)).astype(ml_dtypes.bfloat16)
    return np.stack([high, low])


def cas(rows, columns, length):
    phase = (rows[:, None] * columns[None, :]) % length
    angle = phase * (2.0 * np.pi / length)
    return np.cos(angle) + np.sin(angle)


def z_table(length):
    index = np.arange(length)
    return halves(cas(index, index, length))


def x_tables(length):
    half, quarter = length // 2, length // 4
    place = np.arange(half)
    fourth = cas(4 * place[:quarter], place[:quarter], length)
    second = cas(4 * place[:quarter] + 2, place[:quarter], length)
    odd = cas(2 * place + 1, place, length)
    small = np.stack([halves(fourth), halves(second), halves(second.T)])
    return small, np.stack([halves(odd), halves(odd.T)])


def kx_rows(length):
    half, quarter = length // 2, length // 4
    return ((0, quarter, 4, 0), (quarter, quarter, 4, 2), (half, half, 2, 1))


def padded_to(length, unit):
    return -(-length // unit) * unit


def weights_kernel(nx, nz, levels, table_ref, code_ref, weights):
    heights, widths = code_ref.shape
    scale = 1.0 / (nx * nz)
    kz = lax.broadcasted_iota(jnp.int32, (heights, nz), 1)
    kz = jnp.minimum(kz, nz - kz)
    pick_z = jnp.where(kz == lax.broadcasted_iota(jnp.int32, (heights, nz), 0), 1.0, 0.0)
    pick_z = pick_z.astype(bf16)
    for base, count, step, least in kx_rows(nx):
        tile = min(256, count)
        for top in range(0, count, tile):
            kx = step * (top + lax.broadcasted_iota(jnp.int32, (tile, widths), 0)) + least
            kx = jnp.minimum(kx, nx - kx)
            pick_x = jnp.where(kx == lax.broadcasted_iota(jnp.int32, (tile, widths), 1), 1.0, 0.0)
            tall = lax.dot_general(
                pick_x.astype(bf16),
                code_ref[...],
                (((1,), (1,)), ((), ())),
                preferred_element_type=f32,
            )
            spread = jnp.dot(tall.astype(bf16), pick_z, preferred_element_type=f32)
            response = jnp.zeros_like(spread)
            for level in range(levels):
                response = jnp.where(spread == level + 1.0, table_ref[level], response)
            gain = scale / (response * response + 1.0)
            rows = slice(base + top, base + top + tile)
            weights[0, rows] = (UNIT * response) * gain
            weights[1, rows] = gain


def make_weights(tf_table, tilt_index, wedge, nx, nz):
    levels = tf_table.shape[0]
    code = jnp.where(wedge > 0, tilt_index + 1, 0).T
    extra = [(0, padded_to(size, LANE) - size) for size in code.shape]
    code = jnp.pad(code, extra).astype(bf16)
    vmem = pl.BlockSpec(memory_space=pltpu.VMEM)
    return pl.pallas_call(
        functools.partial(weights_kernel, nx, nz, levels),
        in_specs=[pl.BlockSpec(memory_space=pltpu.SMEM), vmem],
        out_specs=vmem,
        out_shape=jax.ShapeDtypeStruct((2, nx, nz), f32),
        compiler_params=pltpu.CompilerParams(vmem_limit_bytes=16 * MIB),
        cost_estimate=pl.CostEstimate(
            flops=60000 * nx * nz, bytes_accessed=8 * nx * nz, transcendentals=0
        ),
    )(tf_table, code)


def split(value):
    high = value.astype(bf16)
    return high, (value - high.astype(f32)).astype(bf16)


def dot3(a, b):
    wide = jnp.concatenate([a[0], a[0], a[1]], axis=1)
    tall = jnp.concatenate([b[0], b[1], b[0]], axis=0)
    return jnp.dot(wide, tall, preferred_element_type=f32)


def turn_kernel(ny, planes, cells, turned, staged, placed, semaphores):
    blocks = len(staged)
    steps = placed.shape[1] // planes
    rows = planes * ny
    incoming = [
        [
            pltpu.make_async_copy(
                cells.at[pl.ds(step * rows, rows), pl.ds(LANE * k, LANE)],
                staged[k].at[pl.ds(step * rows, rows), :],
                semaphores.at[0, step, k],
            )
            for k in range(blocks)
        ]
        for step in range(steps)
    ]
    outgoing = [
        pltpu.make_async_copy(
            placed.at[:, pl.ds(step * planes, planes), :],
            turned.at[:, pl.ds(step * planes, planes), :],
            semaphores.at[1, step, 0],
        )
        for step in range(steps)
    ]
    for step in range(steps):
        for copy in incoming[step]:
            copy.start()
    for step in range(steps):
        for copy in incoming[step]:
            copy.wait()
        for y in range(ny):
            for x in range(step * planes, (step + 1) * planes, SUB):
                for k in range(blocks):
                    placed[y, x : x + SUB, LANE * k : LANE * (k + 1)] = staged[k][
                        pl.ds(x * ny + y, SUB, stride=ny), :
                    ]
        outgoing[step].start()
    for copy in outgoing:
        copy.wait()


def turn(observed):
    slab, ny, nz = observed.shape
    planes = 2 * SUB if slab % (2 * SUB) == 0 else SUB
    anywhere = pl.BlockSpec(memory_space=pltpu.HBM)
    return pl.pallas_call(
        functools.partial(turn_kernel, ny, planes),
        in_specs=[anywhere],
        out_specs=anywhere,
        out_shape=jax.ShapeDtypeStruct((ny, slab, nz), f32),
        scratch_shapes=[
            [pltpu.VMEM((slab * ny, LANE), f32)] * (nz // LANE),
            pltpu.VMEM((ny, slab, nz), f32),
            pltpu.SemaphoreType.DMA((2, slab // planes, nz // LANE)),
        ],
        compiler_params=pltpu.CompilerParams(vmem_limit_bytes=MOST_VMEM),
        cost_estimate=pl.CostEstimate(
            flops=0, bytes_accessed=8 * slab * ny * nz, transcendentals=0
        ),
    )(observed.reshape(slab * ny, nz))


def window_tiles(width, nz):
    return width * nz // (SUB * LANE)


def filter_kernel(first, halo, slab, *refs):
    cells, ztab, small, odd, weights, refs = refs[:5] + (refs[5:],)
    if first:
        windows, kept, high, low, padded = refs
    else:
        kept, windows, high, low, padded = refs
    devices, rows, _, nz = cells.shape
    nx = devices * slab
    half, quarter = nx // 2, nx // 4
    width = slab + 2 * halo
    blocks = nz // LANE
    ztable = (ztab[0], ztab[1])

    def table(ref, i, rows=slice(None)):
        return ref[i, 0, rows], ref[i, 1, rows]

    def store(spot, value):
        high[spot], low[spot] = split(value)

    def load(spot):
        return high[spot], low[spot]

    parts = [slice(i * quarter, (i + 1) * quarter) for i in range(4)]
    folds = [parts[0], parts[1], slice(half, nx)]
    for r in range(rows):
        q = [
            cells[i * devices // 4 : (i + 1) * devices // 4, r].reshape(quarter, nz)
            for i in range(4)
        ]
        even = (q[0] + q[2], q[1] + q[3])
        folded = (even[0] + even[1], even[0] - even[1], q[0] - q[2], q[1] - q[3])
        for spot, value in zip(parts, folded):
            store(spot, dot3(split(value), ztable))
        waves = [dot3(table(small, i), load(folds[i])) for i in range(2)]
        waves += [dot3(table(odd, 0, parts[i]), load(folds[2])) for i in range(2)]
        for spot, wave in zip(parts, waves):
            if first:
                seen = wave * weights[0, spot]
                kept[r, spot] = seen
                store(spot, seen + wave * (UNIT * weights[1, spot]))
            else:
                store(spot, kept[r, spot] + wave * weights[1, spot])
        after = (halo + nx) // SUB * SUB
        padded[:SUB] = jnp.zeros((SUB, nz), f32)
        padded[after : after + 2 * SUB] = jnp.zeros((2 * SUB, nz), f32)
        plus, minus = dot3(table(small, 0), load(folds[0])), dot3(table(small, 2), load(folds[1]))
        for i, e in enumerate((plus + minus, plus - minus)):
            o = dot3(table(odd, 1, parts[i]), load(folds[2]))
            for j, value in ((i, e + o), (i + 2, e - o)):
                place = halo + j * quarter
                padded[place : place + quarter] = dot3(split(value), ztable)
        for device in range(devices):
            for g in range(width // SUB):
                spot = device * slab + SUB * g
                for k in range(blocks):
                    windows[device, r, g * blocks + k] = padded[
                        spot : spot + SUB, LANE * k : LANE * (k + 1)
                    ]
            rest = width % SUB
            spot = device * slab + width - rest
            for k in range(blocks if rest else 0):
                tile, row = width // SUB * blocks + k * rest // SUB, k * rest % SUB
                windows[device, r, tile, row : row + rest] = padded[
                    spot : spot + rest, LANE * k : LANE * (k + 1)
                ]


def run_filter(first, halo, cells, tables, weights, kept):
    devices, rows, slab, nz = cells.shape
    nx = devices * slab
    vmem = pl.BlockSpec(memory_space=pltpu.VMEM)
    operands = [cells, *tables, weights, *kept]
    tiles = window_tiles(slab + 2 * halo, nz)
    out_shape = [jax.ShapeDtypeStruct((devices, rows, tiles, SUB, LANE), f32)]
    if first:
        out_shape.append(jax.ShapeDtypeStruct((rows, nx, nz), f32))
    return pl.pallas_call(
        functools.partial(filter_kernel, first, halo, slab),
        in_specs=[vmem] * len(operands),
        out_specs=[vmem] * len(out_shape),
        out_shape=out_shape,
        scratch_shapes=[
            pltpu.VMEM((nx, nz), bf16),
            pltpu.VMEM((nx, nz), bf16),
            pltpu.VMEM((nx + 3 * SUB, nz), f32),
        ],
        compiler_params=pltpu.CompilerParams(vmem_limit_bytes=24 * MIB),
        cost_estimate=pl.CostEstimate(
            flops=6 * rows * nx * nz * (2 * nz + nx),
            bytes_accessed=8 * rows * nx * nz,
            transcendentals=0,
        ),
    )(*operands)


def lane_sums(pieces):
    lane = lax.broadcasted_iota(jnp.int32, pieces[0].shape, 1)
    up = [pltpu.roll(piece, LANE - 1, 1) for piece in pieces]
    down = [pltpu.roll(piece, 1, 1) for piece in pieces]
    sums = []
    for k in range(len(pieces)):
        above = up[k + 1] if k + 1 < len(pieces) else 0.0
        below = down[k - 1] if k > 0 else 0.0
        sums.append(
            jnp.where(lane == LANE - 1, above, up[k]) + jnp.where(lane == 0, below, down[k])
        )
    return sums


def row_sums(groups):
    return inner_row_sums([groups[-1]] + groups + [groups[0]])


def inner_row_sums(groups):
    row = lax.broadcasted_iota(jnp.int32, groups[0].shape, 0)
    up = [pltpu.roll(group, SUB - 1, 0) for group in groups]
    down = [pltpu.roll(group, 1, 0) for group in groups]
    return [
        jnp.where(row == SUB - 1, up[g + 1], up[g]) + jnp.where(row == 0, down[g - 1], down[g])
        for g in range(1, len(groups) - 1)
    ]


def passes_kernel(first, last, halo, slab, nx, target, *refs):
    if first:
        duals_in, refs = None, refs
    else:
        duals_in, refs = refs[:3], refs[3:]
    if last:
        restored, refs = refs[0], refs[1:]
    else:
        current, duals_out, refs = refs[0], refs[1:4], refs[4:]
    lead, field, dual_x, dual_y, dual_z = refs[:5]
    turned = refs[5:-1] if last else ()
    ny, _, nz = field.shape
    width = slab + 2 * halo
    groups = padded_to(width, SUB) // SUB
    blocks = nz // LANE
    decay = 1.0 / (1.0 + step_dual * huber_eps / bound_dual)
    gain = step_dual * decay
    floor = 1.0 / (decay * decay)
    keep = 1.0 / (1.0 + step_primal)
    pull = step_primal * keep
    push = pull * gain / decay
    origin = lax.axis_index("gy") * slab - halo

    def goal_of(y, g, k):
        if SUB * (g + 1) <= width:
            return target[y, g * blocks + k]
        rest = width % SUB
        tail = target[y, g * blocks + k * rest // SUB]
        shift = k * rest % SUB
        return pltpu.roll(tail, SUB - shift, 0) if shift else tail

    def masked(value, g):
        if SUB * g >= halo and SUB * (g + 1) <= width - halo:
            return value
        place = origin + SUB * g + lax.broadcasted_iota(jnp.int32, (SUB, LANE), 0)
        return jnp.where((place >= 0) & (place < nx), value, 0.0)

    def at(g, k):
        return pl.ds(SUB * g, SUB), pl.ds(LANE * k, LANE)

    empty = jnp.zeros(lead.shape[1:], f32)
    for plane in (0, ny + 1):
        lead[plane] = empty
        dual_y[plane] = empty

    @pl.loop(0, ny, unroll=UNROLL)
    def _(y):
        for g in range(groups):
            for k in range(blocks):
                lead[(y + 1,) + at(g, k)] = goal_of(y, g, k)

    leaving = []
    for sweep in range(PASSES):
        final = sweep == PASSES - 1

        @pl.loop(0, ny, unroll=UNROLL)
        def _(y):
            here = [[lead[(y + 1,) + at(g, k)] for k in range(blocks)] for g in range(groups)]
            columns = [row_sums([here[g][k] for g in range(groups)]) for k in range(blocks)]
            for g in range(groups):
                along_z = lane_sums(here[g])
                for k in range(blocks):
                    spot = at(g, k)
                    twice = here[g][k] + here[g][k]
                    along_y = lead[(y,) + spot] + lead[(y + 2,) + spot]
                    raised = [columns[k][g] - twice, along_y - twice, along_z[k] - twice]
                    if sweep > 0:
                        before = [dual_x[(y,) + spot], dual_y[(y + 1,) + spot], dual_z[(y,) + spot]]
                    elif duals_in is not None:
                        before = [ref[(y,) + spot] for ref in duals_in]
                    else:
                        before = None
                    if before is not None:
                        raised = [old + new for old, new in zip(before, raised)]
                    total = (
                        raised[0] * raised[0] + raised[1] * raised[1] + raised[2] * raised[2]
                    )
                    shrink = lax.rsqrt(jnp.maximum(floor, total))
                    made = [raised[0] * masked(shrink, g), raised[1] * shrink, raised[2] * shrink]
                    dual_x[(y,) + spot] = made[0]
                    dual_y[(y + 1,) + spot] = made[1]
                    dual_z[(y,) + spot] = made[2]
                    if final and not last:
                        shift = halo - HALO_LAST
                        lo = max(0, shift - SUB * g)
                        hi = min(SUB, slab + 2 * HALO_LAST + shift - SUB * g)
                        if lo < hi:
                            rows = pl.ds(SUB * g + lo - shift, hi - lo)
                            for a in range(3):
                                duals_out[a][y, rows, spot[1]] = made[a][lo:hi]

        wanted = list(range(groups))
        if final:
            wanted = [g for g in wanted if SUB * (g + 1) > halo and SUB * g < width - halo]
        column = COLUMN if final and last else len(wanted)
        for some in [wanted[i : i + column] for i in range(0, len(wanted), column)]:

            @pl.loop(0, ny, unroll=UNROLL)
            def _(y):
                around = [some[0] - 1] + some + [some[-1] + 1]
                near = {
                    g: [dual_x[(y,) + at(g % groups, k)] for k in range(blocks)] for g in around
                }
                columns = [inner_row_sums([near[g][k] for g in around]) for k in range(blocks)]
                for place, g in enumerate(some):
                    here = [dual_z[(y,) + at(g, k)] for k in range(blocks)]
                    along_z = lane_sums(here)
                    for k in range(blocks):
                        spot = at(g, k)
                        along_y = dual_y[(y,) + spot] + dual_y[(y + 2,) + spot]
                        centre = near[g][k] + dual_y[(y + 1,) + spot] + here[k]
                        adjoint = columns[k][place] + along_y + along_z[k] - (centre + centre)
                        goal = goal_of(y, g, k)
                        if sweep == 0:
                            move = push * adjoint
                            updated = goal - move
                            ahead = updated - move
                        else:
                            old = field[(y,) + spot]
                            whole = UNIT if final and last else 1.0
                            updated = (keep / whole) * old + (pull / whole) * goal
                            updated = updated - (push / whole) * adjoint
                            ahead = updated + updated - old
                        if not final:
                            field[(y,) + spot] = updated
                            lead[(y + 1,) + spot] = masked(ahead, g)
                            continue
                        lo = max(0, halo - SUB * g)
                        hi = min(SUB, slab + halo - SUB * g)
                        x = SUB * g + lo - halo
                        if last:
                            turned[k][pl.ds(x * ny + y, hi - lo, stride=ny), :] = updated[lo:hi]
                        else:
                            current[y, pl.ds(x, hi - lo), spot[1]] = updated[lo:hi]

            if final and last:
                low = max(0, SUB * some[0] - halo) * ny
                high = min(slab, SUB * (some[-1] + 1) - halo) * ny
                for k, block in enumerate(turned):
                    copy = pltpu.make_async_copy(
                        block.at[pl.ds(low, high - low), :],
                        restored.at[pl.ds(low, high - low), pl.ds(LANE * k, LANE)],
                        refs[-1].at[len(leaving)],
                    )
                    copy.start()
                    leaving.append(copy)

    for copy in leaving:
        copy.wait()


def run_passes(first, last, halo, slab, nx, target, duals):
    ny = target.shape[0]
    nz = target.shape[1] * SUB * LANE // (slab + 2 * halo)
    width = padded_to(slab + 2 * halo, SUB)
    vmem = pl.BlockSpec(memory_space=pltpu.VMEM)
    if last:
        out_shape = jax.ShapeDtypeStruct((slab * ny, nz), f32)
        out_specs = pl.BlockSpec(memory_space=pltpu.HBM)
    else:
        kept = jax.ShapeDtypeStruct((ny, slab + 2 * HALO_LAST, nz), f32)
        out_shape = [jax.ShapeDtypeStruct((ny, slab, nz), f32), kept, kept, kept]
        out_specs = [vmem] * 4
    return pl.pallas_call(
        functools.partial(passes_kernel, first, last, halo, slab, nx),
        in_specs=[vmem] * (1 + len(duals)),
        out_specs=out_specs,
        out_shape=out_shape,
        scratch_shapes=[
            pltpu.VMEM((ny + 2, width, nz), f32),
            pltpu.VMEM((ny, width, nz), f32),
            pltpu.VMEM((ny, width, nz), f32),
            pltpu.VMEM((ny + 2, width, nz), f32),
            pltpu.VMEM((ny, width, nz), f32),
        ]
        + [pltpu.VMEM((slab * ny, LANE), f32)] * (nz // LANE if last else 0)
        + [pltpu.SemaphoreType.DMA((nz // LANE * width // SUB,))] * last,
        compiler_params=pltpu.CompilerParams(vmem_limit_bytes=40 * MIB),
        cost_estimate=pl.CostEstimate(
            flops=60 * PASSES * ny * width * nz,
            bytes_accessed=8 * 4 * ny * width * nz,
            transcendentals=PASSES * ny * width * nz,
        ),
    )(target, *duals)


def exchange(blocks):
    return lax.all_to_all(blocks, "gy", split_axis=0, concat_axis=0, tiled=True)


def local(observed, tf_table, tilt_index, wedge):
    slab, ny, nz = observed.shape
    devices = lax.axis_size("gy")
    rows = ny // devices
    nx = slab * devices
    tables = [jnp.asarray(table) for table in (z_table(nz),) + x_tables(nx)]
    cells = exchange(turn(observed).reshape(devices, rows, slab, nz))
    weights = make_weights(tf_table, tilt_index, wedge, nx, nz)
    duals, kept = (), ()
    for outer in range(OUTER):
        first, last = outer == 0, outer == OUTER - 1
        halo = HALO_LAST if last else HALO_FIRST
        made = run_filter(first, halo, cells, tables, weights, kept)
        kept = made[1:]
        windows = exchange(made[0])
        target = windows.reshape((ny,) + windows.shape[2:])
        made = run_passes(first, last, halo, slab, nx, target, duals)
        if last:
            return made.reshape(slab, ny, nz)
        duals = tuple(made[1:])
        cells = exchange(made[0].reshape(devices, rows, slab, nz))


def solution(mesh):
    in_specs = (P(("groups", "gy"), None, None), P(), P(), P())
    out_specs = P(("groups", "gy"), None, None)
    return jax.shard_map(local, mesh=mesh, in_specs=in_specs, out_specs=out_specs, check_vma=False)
```

```python
import functools

import jax
import jax.numpy as jnp
import ml_dtypes
import numpy as np
from jax import lax
from jax.experimental import pallas as pl
from jax.experimental.pallas import tpu as pltpu
from jax.sharding import PartitionSpec as P

OUTER = 2
PASSES = 2

step_dual = 0.14
step_primal = 0.14
huber_eps = 0.05
bound_dual = 0.5

SUB = 8
LANE = 128
HALO_LAST = 2 * PASSES
HALO_FIRST = HALO_LAST + 2 * PASSES - 2
UNROLL = 16
COLUMN = 3
MIB = 1024 * 1024
MOST_VMEM = 61 * MIB

f32 = jnp.float32
bf16 = jnp.bfloat16

UNIT = step_dual / bound_dual


def halves(table):
    high = table.astype(ml_dtypes.bfloat16)
    low = (table - high.astype(np.float64)).astype(ml_dtypes.bfloat16)
    return np.stack([high, low])


def cas(rows, columns, length):
    phase = (rows[:, None] * columns[None, :]) % length
    angle = phase * (2.0 * np.pi / length)
    return np.cos(angle) + np.sin(angle)


def z_table(length):
    index = np.arange(length)
    return halves(cas(index, index, length))


def x_tables(length):
    half, quarter = length // 2, length // 4
    place = np.arange(half)
    fourth = cas(4 * place[:quarter], place[:quarter], length)
    second = cas(4 * place[:quarter] + 2, place[:quarter], length)
    odd = cas(2 * place + 1, place, length)
    blocks = [fourth, second, second.T]
    for table in (odd, odd.T):
        for rows in (slice(0, quarter), slice(quarter, half)):
            blocks += [table[rows, :quarter], table[rows, quarter:]]
    return halves(np.stack(blocks))


def kx_rows(length):
    half, quarter = length // 2, length // 4
    return ((0, quarter, 4, 0), (quarter, quarter, 4, 2), (half, half, 2, 1))


def padded_to(length, unit):
    return -(-length // unit) * unit


def weights_kernel(nx, nz, levels, table_ref, code_ref, both_data, prior):
    heights, widths = code_ref.shape
    scale = 1.0 / (nx * nz)
    kz = lax.broadcasted_iota(jnp.int32, (heights, nz), 1)
    kz = jnp.minimum(kz, nz - kz)
    pick_z = jnp.where(kz == lax.broadcasted_iota(jnp.int32, (heights, nz), 0), 1.0, 0.0)
    pick_z = pick_z.astype(bf16)
    for base, count, step, least in kx_rows(nx):
        tile = min(256, count)
        for top in range(0, count, tile):
            kx = step * (top + lax.broadcasted_iota(jnp.int32, (tile, widths), 0)) + least
            kx = jnp.minimum(kx, nx - kx)
            pick_x = jnp.where(kx == lax.broadcasted_iota(jnp.int32, (tile, widths), 1), 1.0, 0.0)
            tall = lax.dot_general(
                pick_x.astype(bf16),
                code_ref[...],
                (((1,), (1,)), ((), ())),
                preferred_element_type=f32,
            )
            spread = jnp.dot(tall.astype(bf16), pick_z, preferred_element_type=f32)
            response = jnp.zeros_like(spread)
            for level in range(levels):
                response = jnp.where(spread == level + 1.0, table_ref[level], response)
            gain = scale / (response * response + 1.0)
            rows = slice(base + top, base + top + tile)
            prior[rows] = gain
            both_data[0, rows] = UNIT * (response * gain + gain)
            both_data[1, rows] = (UNIT * response) * gain


def make_weights(tf_table, tilt_index, wedge, nx, nz):
    levels = tf_table.shape[0]
    code = jnp.where(wedge > 0, tilt_index + 1, 0).T
    extra = [(0, padded_to(size, LANE) - size) for size in code.shape]
    code = jnp.pad(code, extra).astype(bf16)
    vmem = pl.BlockSpec(memory_space=pltpu.VMEM)
    return pl.pallas_call(
        functools.partial(weights_kernel, nx, nz, levels),
        in_specs=[pl.BlockSpec(memory_space=pltpu.SMEM), vmem],
        out_specs=[vmem] * 2,
        out_shape=[jax.ShapeDtypeStruct((2, nx, nz), f32), jax.ShapeDtypeStruct((nx, nz), f32)],
        compiler_params=pltpu.CompilerParams(vmem_limit_bytes=16 * MIB),
        cost_estimate=pl.CostEstimate(
            flops=60000 * nx * nz, bytes_accessed=8 * nx * nz, transcendentals=0
        ),
    )(tf_table, code)


def split(value):
    high = value.astype(bf16)
    return high, (value - high.astype(f32)).astype(bf16)


def dot3(a, b):
    wide = jnp.concatenate([a[0], a[0], a[1]], axis=1)
    tall = jnp.concatenate([b[0], b[1], b[0]], axis=0)
    return jnp.dot(wide, tall, preferred_element_type=f32)


def turn_kernel(ny, planes, cells, turned, staged, placed, semaphores):
    blocks = len(staged)
    steps = placed.shape[1] // planes
    rows = planes * ny
    incoming = [
        [
            pltpu.make_async_copy(
                cells.at[pl.ds(step * rows, rows), pl.ds(LANE * k, LANE)],
                staged[k].at[pl.ds(step * rows, rows), :],
                semaphores.at[0, step, k],
            )
            for k in range(blocks)
        ]
        for step in range(steps)
    ]
    outgoing = [
        pltpu.make_async_copy(
            placed.at[:, pl.ds(step * planes, planes), :],
            turned.at[:, pl.ds(step * planes, planes), :],
            semaphores.at[1, step, 0],
        )
        for step in range(steps)
    ]
    for step in range(steps):
        for copy in incoming[step]:
            copy.start()
    for step in range(steps):
        for copy in incoming[step]:
            copy.wait()
        for y in range(ny):
            for x in range(step * planes, (step + 1) * planes, SUB):
                for k in range(blocks):
                    placed[y, x : x + SUB, LANE * k : LANE * (k + 1)] = staged[k][
                        pl.ds(x * ny + y, SUB, stride=ny), :
                    ]
        outgoing[step].start()
    for copy in outgoing:
        copy.wait()


def turn(observed):
    slab, ny, nz = observed.shape
    planes = 2 * SUB if slab % (2 * SUB) == 0 else SUB
    anywhere = pl.BlockSpec(memory_space=pltpu.HBM)
    return pl.pallas_call(
        functools.partial(turn_kernel, ny, planes),
        in_specs=[anywhere],
        out_specs=anywhere,
        out_shape=jax.ShapeDtypeStruct((ny, slab, nz), f32),
        scratch_shapes=[
            [pltpu.VMEM((slab * ny, LANE), f32)] * (nz // LANE),
            pltpu.VMEM((ny, slab, nz), f32),
            pltpu.SemaphoreType.DMA((2, slab // planes, nz // LANE)),
        ],
        compiler_params=pltpu.CompilerParams(vmem_limit_bytes=MOST_VMEM),
        cost_estimate=pl.CostEstimate(
            flops=0, bytes_accessed=8 * slab * ny * nz, transcendentals=0
        ),
    )(observed.reshape(slab * ny, nz))


def window_tiles(width, nz):
    return width * nz // (SUB * LANE)


def filter_kernel(first, halo, slab, *refs):
    cells, ztab, xtab, weights, refs = refs[:4] + (refs[4:],)
    if first:
        windows, kept, high, low, padded = refs
    else:
        kept, windows, high, low, padded = refs
    devices, rows, _, nz = cells.shape
    nx = devices * slab
    half, quarter = nx // 2, nx // 4
    width = slab + 2 * halo
    blocks = nz // LANE
    ztable = (ztab[0], ztab[1])

    def table(*places):
        return [jnp.concatenate([xtab[part, i] for i in places], axis=1) for part in range(2)]

    def store(spot, value):
        high[spot], low[spot] = split(value)

    def load(spot):
        return high[spot], low[spot]

    parts = [slice(i * quarter, (i + 1) * quarter) for i in range(4)]
    folds = [parts[0], parts[1], slice(half, nx)]
    for r in range(rows):
        q = [
            cells[i * devices // 4 : (i + 1) * devices // 4, r].reshape(quarter, nz)
            for i in range(4)
        ]
        even = (q[0] + q[2], q[1] + q[3])
        folded = (even[0] + even[1], even[0] - even[1], q[0] - q[2], q[1] - q[3])
        for spot, value in zip(parts, folded):
            store(spot, dot3(split(value), ztable))
        waves = [dot3(table(i), load(folds[i])) for i in range(2)]
        waves += [dot3(table(3 + 2 * i, 4 + 2 * i), load(folds[2])) for i in range(2)]
        for spot, wave in zip(parts, waves):
            if first:
                kept[r, spot] = wave * weights[1, spot]
                store(spot, wave * weights[0, spot])
            else:
                store(spot, kept[r, spot] + wave * weights[spot])
        after = (halo + nx) // SUB * SUB
        padded[:SUB] = jnp.zeros((SUB, nz), f32)
        padded[after : after + 2 * SUB] = jnp.zeros((2 * SUB, nz), f32)
        plus, minus = dot3(table(0), load(folds[0])), dot3(table(2), load(folds[1]))
        for i, e in enumerate((plus + minus, plus - minus)):
            o = dot3(table(7 + 2 * i, 8 + 2 * i), load(folds[2]))
            for j, value in ((i, e + o), (i + 2, e - o)):
                place = halo + j * quarter
                padded[place : place + quarter] = dot3(split(value), ztable)
        for device in range(devices):
            for g in range(width // SUB):
                spot = device * slab + SUB * g
                for k in range(blocks):
                    windows[device, r, g * blocks + k] = padded[
                        spot : spot + SUB, LANE * k : LANE * (k + 1)
                    ]
            rest = width % SUB
            spot = device * slab + width - rest
            for k in range(blocks if rest else 0):
                tile, row = width // SUB * blocks + k * rest // SUB, k * rest % SUB
                windows[device, r, tile, row : row + rest] = padded[
                    spot : spot + rest, LANE * k : LANE * (k + 1)
                ]


def run_filter(first, halo, cells, tables, weights, kept):
    devices, rows, slab, nz = cells.shape
    nx = devices * slab
    vmem = pl.BlockSpec(memory_space=pltpu.VMEM)
    operands = [cells, *tables, weights, *kept]
    tiles = window_tiles(slab + 2 * halo, nz)
    out_shape = [jax.ShapeDtypeStruct((devices, rows, tiles, SUB, LANE), f32)]
    if first:
        out_shape.append(jax.ShapeDtypeStruct((rows, nx, nz), f32))
    return pl.pallas_call(
        functools.partial(filter_kernel, first, halo, slab),
        in_specs=[vmem] * len(operands),
        out_specs=[vmem] * len(out_shape),
        out_shape=out_shape,
        scratch_shapes=[
            pltpu.VMEM((nx, nz), bf16),
            pltpu.VMEM((nx, nz), bf16),
            pltpu.VMEM((nx + 3 * SUB, nz), f32),
        ],
        compiler_params=pltpu.CompilerParams(vmem_limit_bytes=24 * MIB),
        cost_estimate=pl.CostEstimate(
            flops=6 * rows * nx * nz * (2 * nz + nx),
            bytes_accessed=8 * rows * nx * nz,
            transcendentals=0,
        ),
    )(*operands)


def lane_sums(pieces):
    lane = lax.broadcasted_iota(jnp.int32, pieces[0].shape, 1)
    up = [pltpu.roll(piece, LANE - 1, 1) for piece in pieces]
    down = [pltpu.roll(piece, 1, 1) for piece in pieces]
    sums = []
    for k in range(len(pieces)):
        above = up[k + 1] if k + 1 < len(pieces) else 0.0
        below = down[k - 1] if k > 0 else 0.0
        sums.append(
            jnp.where(lane == LANE - 1, above, up[k]) + jnp.where(lane == 0, below, down[k])
        )
    return sums


def row_sums(groups):
    return inner_row_sums([groups[-1]] + groups + [groups[0]])


def inner_row_sums(groups):
    row = lax.broadcasted_iota(jnp.int32, groups[0].shape, 0)
    up = [pltpu.roll(group, SUB - 1, 0) for group in groups]
    down = [pltpu.roll(group, 1, 0) for group in groups]
    return [
        jnp.where(row == SUB - 1, up[g + 1], up[g]) + jnp.where(row == 0, down[g - 1], down[g])
        for g in range(1, len(groups) - 1)
    ]


def passes_kernel(first, last, halo, slab, nx, target, *refs):
    if first:
        duals_in, refs = None, refs
    else:
        duals_in, refs = refs[:3], refs[3:]
    if last:
        restored, dual_x, dual_y, dual_z, lead, field = refs[:1] + refs[-4:-1] + refs[1:3]
        turned, semaphores = refs[3:-4], refs[-1]
    else:
        current, dual_x, dual_y, dual_z, lead, field = refs
    ny, _, nz = field.shape
    width = slab + 2 * halo
    width_before = slab + 2 * HALO_FIRST
    groups = padded_to(width, SUB) // SUB
    blocks = nz // LANE
    decay = 1.0 / (1.0 + step_dual * huber_eps / bound_dual)
    gain = step_dual * decay
    floor = 1.0 / (decay * decay)
    keep = 1.0 / (1.0 + step_primal)
    pull = step_primal * keep
    push = pull * gain / decay
    origin = lax.axis_index("gy") * slab - halo

    def goal_of(y, g, k):
        if SUB * (g + 1) <= width:
            return target[y, g * blocks + k]
        rest = width % SUB
        tail = target[y, g * blocks + k * rest // SUB]
        shift = k * rest % SUB
        return pltpu.roll(tail, SUB - shift, 0) if shift else tail

    inside = {}
    for g in range(groups):
        if SUB * g < halo or SUB * (g + 1) > width - halo:
            place = origin + SUB * g + lax.broadcasted_iota(jnp.int32, (SUB, LANE), 0)
            inside[g] = jnp.where((place >= 0) & (place < nx), 1.0, 0.0)

    def masked(value, g):
        return value * inside[g] if g in inside else value

    def at(g, k):
        return pl.ds(SUB * g, SUB), pl.ds(LANE * k, LANE)

    empty = jnp.zeros(lead.shape[1:], f32)
    for plane in (0, ny + 1):
        lead[plane] = empty
        dual_y[plane] = empty

    @pl.loop(0, ny, unroll=UNROLL)
    def _(y):
        for g in range(groups):
            for k in range(blocks):
                lead[(y + 1,) + at(g, k)] = goal_of(y, g, k)

    leaving = []
    for sweep in range(PASSES):
        final = sweep == PASSES - 1

        @pl.loop(0, ny, unroll=UNROLL)
        def _(y):
            here = [[lead[(y + 1,) + at(g, k)] for k in range(blocks)] for g in range(groups)]
            columns = [row_sums([here[g][k] for g in range(groups)]) for k in range(blocks)]
            for g in range(groups):
                along_z = lane_sums(here[g])
                for k in range(blocks):
                    spot = at(g, k)
                    twice = here[g][k] + here[g][k]
                    along_y = lead[(y,) + spot] + lead[(y + 2,) + spot]
                    raised = [columns[k][g] - twice, along_y - twice, along_z[k] - twice]
                    if sweep > 0:
                        before = [dual_x[(y,) + spot], dual_y[(y + 1,) + spot], dual_z[(y,) + spot]]
                    elif duals_in is not None:
                        rows = pl.ds(SUB * g + (width_before - width) // 2, SUB)
                        before = [
                            ref[y + shift, rows, spot[1]] for ref, shift in zip(duals_in, (0, 1, 0))
                        ]
                    else:
                        before = None
                    if before is not None:
                        raised = [old + new for old, new in zip(before, raised)]
                    total = (
                        raised[0] * raised[0] + raised[1] * raised[1] + raised[2] * raised[2]
                    )
                    shrink = lax.rsqrt(jnp.maximum(floor, total))
                    made = [raised[0] * masked(shrink, g), raised[1] * shrink, raised[2] * shrink]
                    dual_x[(y,) + spot] = made[0]
                    dual_y[(y + 1,) + spot] = made[1]
                    dual_z[(y,) + spot] = made[2]

        wanted = list(range(groups))
        if final:
            wanted = [g for g in wanted if SUB * (g + 1) > halo and SUB * g < width - halo]
        column = COLUMN if final and last else len(wanted)
        for some in [wanted[i : i + column] for i in range(0, len(wanted), column)]:

            @pl.loop(0, ny, unroll=UNROLL)
            def _(y):
                around = [some[0] - 1] + some + [some[-1] + 1]
                near = {
                    g: [dual_x[(y,) + at(g % groups, k)] for k in range(blocks)] for g in around
                }
                columns = [inner_row_sums([near[g][k] for g in around]) for k in range(blocks)]
                for place, g in enumerate(some):
                    here = [dual_z[(y,) + at(g, k)] for k in range(blocks)]
                    along_z = lane_sums(here)
                    for k in range(blocks):
                        spot = at(g, k)
                        along_y = dual_y[(y,) + spot] + dual_y[(y + 2,) + spot]
                        centre = near[g][k] + dual_y[(y + 1,) + spot] + here[k]
                        adjoint = columns[k][place] + along_y + along_z[k] - (centre + centre)
                        goal = goal_of(y, g, k)
                        if sweep == 0:
                            move = push * adjoint
                            updated = goal - move
                            ahead = updated - move
                        else:
                            old = field[(y,) + spot]
                            whole = UNIT if final and last else 1.0
                            updated = (keep / whole) * old + (pull / whole) * goal
                            updated = updated - (push / whole) * adjoint
                            ahead = updated + updated - old
                        if not final:
                            field[(y,) + spot] = updated
                            lead[(y + 1,) + spot] = masked(ahead, g)
                            continue
                        lo = max(0, halo - SUB * g)
                        hi = min(SUB, slab + halo - SUB * g)
                        x = SUB * g + lo - halo
                        if last:
                            turned[k][pl.ds(x * ny + y, hi - lo, stride=ny), :] = updated[lo:hi]
                        else:
                            current[y, pl.ds(x, hi - lo), spot[1]] = updated[lo:hi]

            if final and last:
                low = max(0, SUB * some[0] - halo) * ny
                high = min(slab, SUB * (some[-1] + 1) - halo) * ny
                for k, block in enumerate(turned):
                    copy = pltpu.make_async_copy(
                        block.at[pl.ds(low, high - low), :],
                        restored.at[pl.ds(low, high - low), pl.ds(LANE * k, LANE)],
                        semaphores.at[len(leaving)],
                    )
                    copy.start()
                    leaving.append(copy)

    for copy in leaving:
        copy.wait()


def run_passes(first, last, halo, slab, nx, target, duals):
    ny = target.shape[0]
    nz = target.shape[1] * SUB * LANE // (slab + 2 * halo)
    width = padded_to(slab + 2 * halo, SUB)
    vmem = pl.BlockSpec(memory_space=pltpu.VMEM)
    dual_shapes = [(ny + framed, width, nz) for framed in (0, 2, 0)]
    scratch_shapes = [pltpu.VMEM((ny + 2, width, nz), f32), pltpu.VMEM((ny, width, nz), f32)]
    if last:
        out_shape = jax.ShapeDtypeStruct((slab * ny, nz), f32)
        out_specs = pl.BlockSpec(memory_space=pltpu.HBM)
        scratch_shapes += [pltpu.VMEM((slab * ny, LANE), f32)] * (nz // LANE)
        scratch_shapes += [pltpu.VMEM(shape, f32) for shape in dual_shapes]
        scratch_shapes.append(pltpu.SemaphoreType.DMA((nz // LANE * width // SUB,)))
    else:
        out_shape = [jax.ShapeDtypeStruct((ny, slab, nz), f32)]
        out_shape += [jax.ShapeDtypeStruct(shape, f32) for shape in dual_shapes]
        out_specs = [vmem] * 4
    return pl.pallas_call(
        functools.partial(passes_kernel, first, last, halo, slab, nx),
        in_specs=[vmem] * (1 + len(duals)),
        out_specs=out_specs,
        out_shape=out_shape,
        scratch_shapes=scratch_shapes,
        compiler_params=pltpu.CompilerParams(vmem_limit_bytes=40 * MIB),
        cost_estimate=pl.CostEstimate(
            flops=60 * PASSES * ny * width * nz,
            bytes_accessed=8 * 4 * ny * width * nz,
            transcendentals=PASSES * ny * width * nz,
        ),
    )(target, *duals)


def exchange(blocks):
    return lax.all_to_all(blocks, "gy", split_axis=0, concat_axis=0, tiled=True)


def local(observed, tf_table, tilt_index, wedge):
    slab, ny, nz = observed.shape
    devices = lax.axis_size("gy")
    rows = ny // devices
    nx = slab * devices
    tables = [jnp.asarray(table) for table in (z_table(nz), x_tables(nx))]
    cells = exchange(turn(observed).reshape(devices, rows, slab, nz))
    both_data, prior = make_weights(tf_table, tilt_index, wedge, nx, nz)
    duals, kept = (), ()
    for outer in range(OUTER):
        first, last = outer == 0, outer == OUTER - 1
        halo = HALO_LAST if last else HALO_FIRST
        made = run_filter(first, halo, cells, tables, both_data if first else prior, kept)
        kept = made[1:]
        windows = exchange(made[0])
        target = windows.reshape((ny,) + windows.shape[2:])
        made = run_passes(first, last, halo, slab, nx, target, duals)
        if last:
            return made.reshape(slab, ny, nz)
        duals = tuple(made[1:])
        cells = exchange(made[0].reshape(devices, rows, slab, nz))


def solution(mesh):
    in_specs = (P(("groups", "gy"), None, None), P(), P(), P())
    out_specs = P(("groups", "gy"), None, None)
    return jax.shard_map(local, mesh=mesh, in_specs=in_specs, out_specs=out_specs, check_vma=False)
```

```python
import functools

import jax
import jax.numpy as jnp
import ml_dtypes
import numpy as np
from jax import lax
from jax.experimental import pallas as pl
from jax.experimental.pallas import tpu as pltpu
from jax.sharding import PartitionSpec as P

OUTER = 2
PASSES = 2

step_dual = 0.14
step_primal = 0.14
huber_eps = 0.05
bound_dual = 0.5

SUB = 8
LANE = 128
HALO_LAST = 2 * PASSES
HALO_FIRST = HALO_LAST + 2 * PASSES - 2
UNROLL = 8
COLUMN = 3
MIB = 1024 * 1024
MOST_VMEM = 61 * MIB

f32 = jnp.float32
bf16 = jnp.bfloat16

UNIT = step_dual / bound_dual


def halves(table):
    high = table.astype(ml_dtypes.bfloat16)
    low = (table - high.astype(np.float64)).astype(ml_dtypes.bfloat16)
    return np.stack([high, low])


def cas(rows, columns, length):
    phase = (rows[:, None] * columns[None, :]) % length
    angle = phase * (2.0 * np.pi / length)
    return np.cos(angle) + np.sin(angle)


def z_table(length):
    index = np.arange(length)
    return halves(cas(index, index, length))


def x_tables(length):
    half, quarter = length // 2, length // 4
    place = np.arange(half)
    fourth = cas(4 * place[:quarter], place[:quarter], length)
    second = cas(4 * place[:quarter] + 2, 2 * place[:quarter] + 1, 2 * length)
    odd = cas(2 * place + 1, 2 * place + 1, 2 * length)
    blocks = [fourth, second]
    for rows in (slice(0, quarter), slice(quarter, half)):
        blocks += [odd[rows, :quarter], odd[rows, quarter:]]
    return halves(np.stack(blocks))


def kx_rows(length):
    half, quarter = length // 2, length // 4
    return ((0, quarter, 4, 0), (quarter, quarter, 4, 2), (half, half, 2, 1))


def padded_to(length, unit):
    return -(-length // unit) * unit


def response_kernel(nx, nz, levels, table_ref, code_ref, response):
    heights, widths = code_ref.shape
    kz = lax.broadcasted_iota(jnp.int32, (heights, nz), 1)
    kz = jnp.minimum(kz, nz - kz)
    pick_z = jnp.where(kz == lax.broadcasted_iota(jnp.int32, (heights, nz), 0), 1.0, 0.0)
    pick_z = pick_z.astype(bf16)
    for base, count, step, least in kx_rows(nx):
        tile = min(256, count)
        for top in range(0, count, tile):
            kx = step * (top + lax.broadcasted_iota(jnp.int32, (tile, widths), 0)) + least
            kx = jnp.minimum(kx, nx - kx)
            pick_x = jnp.where(kx == lax.broadcasted_iota(jnp.int32, (tile, widths), 1), 1.0, 0.0)
            tall = lax.dot_general(
                pick_x.astype(bf16),
                code_ref[...],
                (((1,), (1,)), ((), ())),
                preferred_element_type=f32,
            )
            spread = jnp.dot(tall.astype(bf16), pick_z, preferred_element_type=f32)
            value = jnp.zeros_like(spread)
            for level in range(levels):
                value = jnp.where(spread == level + 1.0, table_ref[level], value)
            response[base + top : base + top + tile] = value


def make_response(tf_table, tilt_index, wedge, nx, nz):
    levels = tf_table.shape[0]
    code = jnp.where(wedge > 0, tilt_index + 1, 0).T
    extra = [(0, padded_to(size, LANE) - size) for size in code.shape]
    code = jnp.pad(code, extra).astype(bf16)
    vmem = pl.BlockSpec(memory_space=pltpu.VMEM)
    return pl.pallas_call(
        functools.partial(response_kernel, nx, nz, levels),
        in_specs=[pl.BlockSpec(memory_space=pltpu.SMEM), vmem],
        out_specs=vmem,
        out_shape=jax.ShapeDtypeStruct((nx, nz), f32),
        compiler_params=pltpu.CompilerParams(vmem_limit_bytes=16 * MIB),
        cost_estimate=pl.CostEstimate(
            flops=60000 * nx * nz, bytes_accessed=4 * nx * nz, transcendentals=0
        ),
    )(tf_table, code)


def split(value):
    high = value.astype(bf16)
    return high, (value - high.astype(f32)).astype(bf16)


def dot3(a, b):
    wide = jnp.concatenate([a[0], a[0], a[1]], axis=1)
    tall = jnp.concatenate([b[0], b[1], b[0]], axis=0)
    return jnp.dot(wide, tall, preferred_element_type=f32)


def turn_kernel(ny, planes, cells, turned, staged, placed, semaphores):
    blocks = len(staged)
    steps = placed.shape[1] // planes
    rows = planes * ny
    incoming = [
        [
            pltpu.make_async_copy(
                cells.at[pl.ds(step * rows, rows), pl.ds(LANE * k, LANE)],
                staged[k].at[pl.ds(step * rows, rows), :],
                semaphores.at[0, step, k],
            )
            for k in range(blocks)
        ]
        for step in range(steps)
    ]
    outgoing = [
        pltpu.make_async_copy(
            placed.at[:, pl.ds(step * planes, planes), :],
            turned.at[:, pl.ds(step * planes, planes), :],
            semaphores.at[1, step, 0],
        )
        for step in range(steps)
    ]
    for step in range(steps):
        for copy in incoming[step]:
            copy.start()
    for step in range(steps):
        for copy in incoming[step]:
            copy.wait()
        for y in range(ny):
            for x in range(step * planes, (step + 1) * planes, SUB):
                for k in range(blocks):
                    placed[y, x : x + SUB, LANE * k : LANE * (k + 1)] = staged[k][
                        pl.ds(x * ny + y, SUB, stride=ny), :
                    ]
        outgoing[step].start()
    for copy in outgoing:
        copy.wait()


def turn(observed):
    slab, ny, nz = observed.shape
    planes = 2 * SUB if slab % (2 * SUB) == 0 else SUB
    anywhere = pl.BlockSpec(memory_space=pltpu.HBM)
    return pl.pallas_call(
        functools.partial(turn_kernel, ny, planes),
        in_specs=[anywhere],
        out_specs=anywhere,
        out_shape=jax.ShapeDtypeStruct((ny, slab, nz), f32),
        scratch_shapes=[
            [pltpu.VMEM((slab * ny, LANE), f32)] * (nz // LANE),
            pltpu.VMEM((ny, slab, nz), f32),
            pltpu.SemaphoreType.DMA((2, slab // planes, nz // LANE)),
        ],
        compiler_params=pltpu.CompilerParams(vmem_limit_bytes=MOST_VMEM),
        cost_estimate=pl.CostEstimate(
            flops=0, bytes_accessed=8 * slab * ny * nz, transcendentals=0
        ),
    )(observed.reshape(slab * ny, nz))


def window_tiles(width, nz):
    return width * nz // (SUB * LANE)


def filter_kernel(first, halo, slab, *refs):
    cells, ztab, xtab, weights, refs = refs[:4] + (refs[4:],)
    if first:
        windows, kept, prior, high, low, padded = refs
    else:
        kept, windows, high, low, padded = refs
    devices, rows, _, nz = cells.shape
    nx = devices * slab
    half, quarter = nx // 2, nx // 4
    width = slab + 2 * halo
    blocks = nz // LANE
    ztable = (ztab[0], ztab[1])

    def table(*places):
        return [jnp.concatenate([xtab[part, i] for i in places], axis=1) for part in range(2)]

    def store(spot, value):
        high[spot], low[spot] = split(value)

    def load(spot):
        return high[spot], low[spot]

    parts = [slice(i * quarter, (i + 1) * quarter) for i in range(4)]
    folds = [parts[0], parts[1], slice(half, nx)]
    for r in range(rows):
        q = [
            cells[i * devices // 4 : (i + 1) * devices // 4, r].reshape(quarter, nz)
            for i in range(4)
        ]
        even = (q[0] + q[2], q[1] + q[3])
        folded = (even[0] + even[1], even[0] - even[1], q[0] - q[2], q[1] - q[3])
        for spot, value in zip(parts, folded):
            store(spot, dot3(split(value), ztable))
        waves = [dot3(table(i), load(folds[i])) for i in range(2)]
        waves += [dot3(table(2 + 2 * i, 3 + 2 * i), load(folds[2])) for i in range(2)]
        for spot, wave in zip(parts, waves):
            if first:
                response = weights[spot]
                gain = (1.0 / (nx * nz)) / (response * response + 1.0)
                prior[spot] = gain
                wave = wave * (UNIT * gain)
                seen = wave * response
                kept[r, spot] = seen
                store(spot, seen + wave)
            else:
                store(spot, kept[r, spot] + wave * weights[spot])
        after = (halo + nx) // SUB * SUB
        padded[:SUB] = jnp.zeros((SUB, nz), f32)
        padded[after : after + 2 * SUB] = jnp.zeros((2 * SUB, nz), f32)
        plus, minus = dot3(table(0), load(folds[0])), dot3(table(1), load(folds[1]))
        for i, e in enumerate((plus + minus, plus - minus)):
            o = dot3(table(2 + 2 * i, 3 + 2 * i), load(folds[2]))
            for j, value in ((i, e + o), (i + 2, e - o)):
                place = halo + j * quarter
                padded[place : place + quarter] = dot3(split(value), ztable)
        for device in range(devices):
            for g in range(width // SUB):
                spot = device * slab + SUB * g
                for k in range(blocks):
                    windows[device, r, g * blocks + k] = padded[
                        spot : spot + SUB, LANE * k : LANE * (k + 1)
                    ]
            rest = width % SUB
            spot = device * slab + width - rest
            for k in range(blocks if rest else 0):
                tile, row = width // SUB * blocks + k * rest // SUB, k * rest % SUB
                windows[device, r, tile, row : row + rest] = padded[
                    spot : spot + rest, LANE * k : LANE * (k + 1)
                ]


def run_filter(first, halo, cells, tables, weights, kept):
    devices, rows, slab, nz = cells.shape
    nx = devices * slab
    vmem = pl.BlockSpec(memory_space=pltpu.VMEM)
    operands = [cells, *tables, weights, *kept]
    tiles = window_tiles(slab + 2 * halo, nz)
    out_shape = [jax.ShapeDtypeStruct((devices, rows, tiles, SUB, LANE), f32)]
    if first:
        out_shape += [
            jax.ShapeDtypeStruct((rows, nx, nz), f32),
            jax.ShapeDtypeStruct((nx, nz), f32),
        ]
    return pl.pallas_call(
        functools.partial(filter_kernel, first, halo, slab),
        in_specs=[vmem] * len(operands),
        out_specs=[vmem] * len(out_shape),
        out_shape=out_shape,
        scratch_shapes=[
            pltpu.VMEM((nx, nz), bf16),
            pltpu.VMEM((nx, nz), bf16),
            pltpu.VMEM((nx + 3 * SUB, nz), f32),
        ],
        compiler_params=pltpu.CompilerParams(vmem_limit_bytes=24 * MIB),
        cost_estimate=pl.CostEstimate(
            flops=6 * rows * nx * nz * (2 * nz + nx),
            bytes_accessed=8 * rows * nx * nz,
            transcendentals=0,
        ),
    )(*operands)


def lane_sums(pieces):
    lane = lax.broadcasted_iota(jnp.int32, pieces[0].shape, 1)
    up = [pltpu.roll(piece, LANE - 1, 1) for piece in pieces]
    down = [pltpu.roll(piece, 1, 1) for piece in pieces]
    sums = []
    for k in range(len(pieces)):
        above = up[k + 1] if k + 1 < len(pieces) else 0.0
        below = down[k - 1] if k > 0 else 0.0
        sums.append(
            jnp.where(lane == LANE - 1, above, up[k]) + jnp.where(lane == 0, below, down[k])
        )
    return sums


def row_sums(groups):
    return inner_row_sums([groups[-1]] + groups + [groups[0]])


def inner_row_sums(groups):
    row = lax.broadcasted_iota(jnp.int32, groups[0].shape, 0)
    up = [pltpu.roll(group, SUB - 1, 0) for group in groups]
    down = [pltpu.roll(group, 1, 0) for group in groups]
    return [
        jnp.where(row == SUB - 1, up[g + 1], up[g]) + jnp.where(row == 0, down[g - 1], down[g])
        for g in range(1, len(groups) - 1)
    ]


def passes_kernel(first, last, halo, slab, nx, target, *refs):
    if first:
        duals_in, refs = None, refs
    else:
        duals_in, refs = refs[:3], refs[3:]
    if last:
        restored, refs = refs[0], refs[1:]
    else:
        current, duals_out, refs = refs[0], refs[1:4], refs[4:]
    lead, field, dual_x, dual_y, dual_z = refs[:5]
    turned = refs[5:-1] if last else ()
    ny, _, nz = field.shape
    width = slab + 2 * halo
    groups = padded_to(width, SUB) // SUB
    blocks = nz // LANE
    decay = 1.0 / (1.0 + step_dual * huber_eps / bound_dual)
    gain = step_dual * decay
    floor = 1.0 / (decay * decay)
    keep = 1.0 / (1.0 + step_primal)
    pull = step_primal * keep
    push = pull * gain / decay
    origin = lax.axis_index("gy") * slab - halo

    def goal_of(y, g, k):
        if SUB * (g + 1) <= width:
            return target[y, g * blocks + k]
        rest = width % SUB
        tail = target[y, g * blocks + k * rest // SUB]
        shift = k * rest % SUB
        return pltpu.roll(tail, SUB - shift, 0) if shift else tail

    inside = {}
    for g in range(groups):
        if SUB * g < halo or SUB * (g + 1) > width - halo:
            place = origin + SUB * g + lax.broadcasted_iota(jnp.int32, (SUB, LANE), 0)
            inside[g] = jnp.where((place >= 0) & (place < nx), 1.0, 0.0)

    def masked(value, g):
        return value * inside[g] if g in inside else value

    def hand_on(which, y, g, k, value):
        shift = halo - HALO_LAST
        lo = max(0, shift - SUB * g)
        hi = min(SUB, slab + 2 * HALO_LAST + shift - SUB * g)
        if lo < hi:
            rows = pl.ds(SUB * g + lo - shift, hi - lo)
            duals_out[which][y, rows, pl.ds(LANE * k, LANE)] = value[lo:hi]

    centre_groups = [g for g in range(groups) if SUB * (g + 1) > halo and SUB * g < width - halo]

    def at(g, k):
        return pl.ds(SUB * g, SUB), pl.ds(LANE * k, LANE)

    empty = jnp.zeros(lead.shape[1:], f32)
    for plane in (0, ny + 1):
        lead[plane] = empty
        dual_y[plane] = empty

    @pl.loop(0, ny, unroll=UNROLL)
    def _(y):
        for g in range(groups):
            for k in range(blocks):
                lead[(y + 1,) + at(g, k)] = goal_of(y, g, k)

    leaving = []
    for sweep in range(PASSES):
        final = sweep == PASSES - 1

        @pl.loop(0, ny, unroll=UNROLL)
        def _(y):
            here = [[lead[(y + 1,) + at(g, k)] for k in range(blocks)] for g in range(groups)]
            columns = [row_sums([here[g][k] for g in range(groups)]) for k in range(blocks)]
            for g in range(groups):
                along_z = lane_sums(here[g])
                for k in range(blocks):
                    spot = at(g, k)
                    twice = here[g][k] + here[g][k]
                    along_y = lead[(y,) + spot] + lead[(y + 2,) + spot]
                    raised = [columns[k][g] - twice, along_y - twice, along_z[k] - twice]
                    if sweep > 0:
                        before = [dual_x[(y,) + spot], dual_y[(y + 1,) + spot], dual_z[(y,) + spot]]
                    elif duals_in is not None:
                        before = [ref[(y,) + spot] for ref in duals_in]
                    else:
                        before = None
                    if before is not None:
                        raised = [old + new for old, new in zip(before, raised)]
                    total = (
                        raised[0] * raised[0] + raised[1] * raised[1] + raised[2] * raised[2]
                    )
                    shrink = lax.rsqrt(jnp.maximum(floor, total))
                    made = [raised[0] * masked(shrink, g), raised[1] * shrink, raised[2] * shrink]
                    dual_x[(y,) + spot] = made[0]
                    dual_y[(y + 1,) + spot] = made[1]
                    dual_z[(y,) + spot] = made[2]
                    if final and not last:
                        for a in (0,) if g in centre_groups else (0, 1, 2):
                            hand_on(a, y, g, k, made[a])

        wanted = centre_groups if final else list(range(groups))
        column = COLUMN if final and last else len(wanted)
        for some in [wanted[i : i + column] for i in range(0, len(wanted), column)]:

            @pl.loop(0, ny, unroll=UNROLL)
            def _(y):
                around = [some[0] - 1] + some + [some[-1] + 1]
                near = {
                    g: [dual_x[(y,) + at(g % groups, k)] for k in range(blocks)] for g in around
                }
                columns = [inner_row_sums([near[g][k] for g in around]) for k in range(blocks)]
                for place, g in enumerate(some):
                    here = [dual_z[(y,) + at(g, k)] for k in range(blocks)]
                    along_z = lane_sums(here)
                    for k in range(blocks):
                        spot = at(g, k)
                        along_y = dual_y[(y,) + spot] + dual_y[(y + 2,) + spot]
                        middle = dual_y[(y + 1,) + spot]
                        if final and not last:
                            hand_on(1, y, g, k, middle)
                            hand_on(2, y, g, k, here[k])
                        centre = near[g][k] + middle + here[k]
                        adjoint = columns[k][place] + along_y + along_z[k] - (centre + centre)
                        goal = goal_of(y, g, k)
                        if sweep == 0:
                            move = push * adjoint
                            updated = goal - move
                            ahead = updated - move
                        else:
                            old = field[(y,) + spot]
                            whole = UNIT if final and last else 1.0
                            updated = (keep / whole) * old + (pull / whole) * goal
                            updated = updated - (push / whole) * adjoint
                            ahead = updated + updated - old
                        if not final:
                            field[(y,) + spot] = updated
                            lead[(y + 1,) + spot] = masked(ahead, g)
                            continue
                        lo = max(0, halo - SUB * g)
                        hi = min(SUB, slab + halo - SUB * g)
                        x = SUB * g + lo - halo
                        if last:
                            turned[k][pl.ds(x * ny + y, hi - lo, stride=ny), :] = updated[lo:hi]
                        else:
                            current[y, pl.ds(x, hi - lo), spot[1]] = updated[lo:hi]

            if final and last:
                low = max(0, SUB * some[0] - halo) * ny
                high = min(slab, SUB * (some[-1] + 1) - halo) * ny
                for k, block in enumerate(turned):
                    copy = pltpu.make_async_copy(
                        block.at[pl.ds(low, high - low), :],
                        restored.at[pl.ds(low, high - low), pl.ds(LANE * k, LANE)],
                        refs[-1].at[len(leaving)],
                    )
                    copy.start()
                    leaving.append(copy)

    for copy in leaving:
        copy.wait()


def run_passes(first, last, halo, slab, nx, target, duals):
    ny = target.shape[0]
    nz = target.shape[1] * SUB * LANE // (slab + 2 * halo)
    width = padded_to(slab + 2 * halo, SUB)
    vmem = pl.BlockSpec(memory_space=pltpu.VMEM)
    if last:
        out_shape = jax.ShapeDtypeStruct((slab * ny, nz), f32)
        out_specs = pl.BlockSpec(memory_space=pltpu.HBM)
    else:
        kept = jax.ShapeDtypeStruct((ny, slab + 2 * HALO_LAST, nz), f32)
        out_shape = [jax.ShapeDtypeStruct((ny, slab, nz), f32), kept, kept, kept]
        out_specs = [vmem] * 4
    return pl.pallas_call(
        functools.partial(passes_kernel, first, last, halo, slab, nx),
        in_specs=[vmem] * (1 + len(duals)),
        out_specs=out_specs,
        out_shape=out_shape,
        scratch_shapes=[
            pltpu.VMEM((ny + 2, width, nz), f32),
            pltpu.VMEM((ny, width, nz), f32),
            pltpu.VMEM((ny, width, nz), f32),
            pltpu.VMEM((ny + 2, width, nz), f32),
            pltpu.VMEM((ny, width, nz), f32),
        ]
        + [pltpu.VMEM((slab * ny, LANE), f32)] * (nz // LANE if last else 0)
        + [pltpu.SemaphoreType.DMA((nz // LANE * width // SUB,))] * last,
        compiler_params=pltpu.CompilerParams(vmem_limit_bytes=40 * MIB),
        cost_estimate=pl.CostEstimate(
            flops=60 * PASSES * ny * width * nz,
            bytes_accessed=8 * 4 * ny * width * nz,
            transcendentals=PASSES * ny * width * nz,
        ),
    )(target, *duals)


def exchange(blocks):
    return lax.all_to_all(blocks, "gy", split_axis=0, concat_axis=0, tiled=True)


def local(observed, tf_table, tilt_index, wedge):
    slab, ny, nz = observed.shape
    devices = lax.axis_size("gy")
    rows = ny // devices
    nx = slab * devices
    tables = [jnp.asarray(table) for table in (z_table(nz), x_tables(nx))]
    cells = exchange(turn(observed).reshape(devices, rows, slab, nz))
    weights = make_response(tf_table, tilt_index, wedge, nx, nz)
    duals, kept = (), ()
    for outer in range(OUTER):
        first, last = outer == 0, outer == OUTER - 1
        halo = HALO_LAST if last else HALO_FIRST
        made = run_filter(first, halo, cells, tables, weights, kept)
        if first:
            kept, weights = (made[1],), made[2]
        windows = exchange(made[0])
        target = windows.reshape((ny,) + windows.shape[2:])
        made = run_passes(first, last, halo, slab, nx, target, duals)
        if last:
            return made.reshape(slab, ny, nz)
        duals = tuple(made[1:])
        cells = exchange(made[0].reshape(devices, rows, slab, nz))


def solution(mesh):
    in_specs = (P(("groups", "gy"), None, None), P(), P(), P())
    out_specs = P(("groups", "gy"), None, None)
    return jax.shard_map(local, mesh=mesh, in_specs=in_specs, out_specs=out_specs, check_vma=False)
```

```python
import functools

import jax
import jax.numpy as jnp
import ml_dtypes
import numpy as np
from jax import lax
from jax.experimental import pallas as pl
from jax.experimental.pallas import tpu as pltpu
from jax.sharding import PartitionSpec as P

OUTER = 2
PASSES = 2

step_dual = 0.14
step_primal = 0.14
huber_eps = 0.05
bound_dual = 0.5

SUB = 8
LANE = 128
HALO_LAST = 2 * PASSES
HALO_FIRST = HALO_LAST + 2 * PASSES - 2
UNROLL = 16
COLUMN = 4
MIB = 1024 * 1024
MOST_VMEM = 61 * MIB

f32 = jnp.float32
bf16 = jnp.bfloat16

UNIT = step_dual / bound_dual


def halves(table):
    high = table.astype(ml_dtypes.bfloat16)
    low = (table - high.astype(np.float64)).astype(ml_dtypes.bfloat16)
    return np.stack([high, low])


def cas(rows, columns, length):
    phase = (rows[:, None] * columns[None, :]) % length
    angle = phase * (2.0 * np.pi / length)
    return np.cos(angle) + np.sin(angle)


def z_table(length):
    index = np.arange(length)
    return halves(cas(index, index, length))


def x_tables(length):
    half, quarter = length // 2, length // 4
    place = np.arange(half)
    fourth = cas(4 * place[:quarter], place[:quarter], length)
    second = cas(4 * place[:quarter] + 2, 2 * place[:quarter] + 1, 2 * length)
    odd = cas(2 * place + 1, 2 * place + 1, 2 * length)
    blocks = [fourth, second]
    for rows in (slice(0, quarter), slice(quarter, half)):
        blocks += [odd[rows, :quarter], odd[rows, quarter:]]
    return halves(np.stack(blocks))


def kx_rows(length):
    half, quarter = length // 2, length // 4
    return ((0, quarter, 4, 0), (quarter, quarter, 4, 2), (half, half, 2, 1))


def padded_to(length, unit):
    return -(-length // unit) * unit


def response_kernel(nx, nz, levels, table_ref, code_ref, response):
    heights, widths = code_ref.shape
    kz = lax.broadcasted_iota(jnp.int32, (heights, nz), 1)
    kz = jnp.minimum(kz, nz - kz)
    pick_z = jnp.where(kz == lax.broadcasted_iota(jnp.int32, (heights, nz), 0), 1.0, 0.0)
    pick_z = pick_z.astype(bf16)
    for base, count, step, least in kx_rows(nx):
        tile = min(256, count)
        for top in range(0, count, tile):
            kx = step * (top + lax.broadcasted_iota(jnp.int32, (tile, widths), 0)) + least
            kx = jnp.minimum(kx, nx - kx)
            pick_x = jnp.where(kx == lax.broadcasted_iota(jnp.int32, (tile, widths), 1), 1.0, 0.0)
            tall = lax.dot_general(
                pick_x.astype(bf16),
                code_ref[...],
                (((1,), (1,)), ((), ())),
                preferred_element_type=f32,
            )
            spread = jnp.dot(tall.astype(bf16), pick_z, preferred_element_type=f32)
            value = jnp.zeros_like(spread)
            for level in range(levels):
                value = jnp.where(spread == level + 1.0, table_ref[level], value)
            response[base + top : base + top + tile] = value


def make_response(tf_table, tilt_index, wedge, nx, nz):
    levels = tf_table.shape[0]
    code = jnp.where(wedge > 0, tilt_index + 1, 0).T
    extra = [(0, padded_to(size, LANE) - size) for size in code.shape]
    code = jnp.pad(code, extra).astype(bf16)
    vmem = pl.BlockSpec(memory_space=pltpu.VMEM)
    return pl.pallas_call(
        functools.partial(response_kernel, nx, nz, levels),
        in_specs=[pl.BlockSpec(memory_space=pltpu.SMEM), vmem],
        out_specs=vmem,
        out_shape=jax.ShapeDtypeStruct((nx, nz), f32),
        compiler_params=pltpu.CompilerParams(vmem_limit_bytes=16 * MIB),
        cost_estimate=pl.CostEstimate(
            flops=60000 * nx * nz, bytes_accessed=4 * nx * nz, transcendentals=0
        ),
    )(tf_table, code)


def split(value):
    high = value.astype(bf16)
    return high, (value - high.astype(f32)).astype(bf16)


def dot3(a, b):
    wide = jnp.concatenate([a[0], a[0], a[1]], axis=1)
    tall = jnp.concatenate([b[0], b[1], b[0]], axis=0)
    return jnp.dot(wide, tall, preferred_element_type=f32)


def turn_kernel(ny, planes, cells, turned, staged, placed, semaphores):
    blocks = len(staged)
    steps = placed.shape[1] // planes
    rows = planes * ny
    incoming = [
        [
            pltpu.make_async_copy(
                cells.at[pl.ds(step * rows, rows), pl.ds(LANE * k, LANE)],
                staged[k].at[pl.ds(step * rows, rows), :],
                semaphores.at[0, step, k],
            )
            for k in range(blocks)
        ]
        for step in range(steps)
    ]
    outgoing = [
        pltpu.make_async_copy(
            placed.at[:, pl.ds(step * planes, planes), :],
            turned.at[:, pl.ds(step * planes, planes), :],
            semaphores.at[1, step, 0],
        )
        for step in range(steps)
    ]
    for step in range(steps):
        for copy in incoming[step]:
            copy.start()
    for step in range(steps):
        for copy in incoming[step]:
            copy.wait()
        for y in range(ny):
            for x in range(step * planes, (step + 1) * planes, SUB):
                for k in range(blocks):
                    placed[y, x : x + SUB, LANE * k : LANE * (k + 1)] = staged[k][
                        pl.ds(x * ny + y, SUB, stride=ny), :
                    ]
        outgoing[step].start()
    for copy in outgoing:
        copy.wait()


def turn(observed):
    slab, ny, nz = observed.shape
    planes = 2 * SUB if slab % (2 * SUB) == 0 else SUB
    anywhere = pl.BlockSpec(memory_space=pltpu.HBM)
    return pl.pallas_call(
        functools.partial(turn_kernel, ny, planes),
        in_specs=[anywhere],
        out_specs=anywhere,
        out_shape=jax.ShapeDtypeStruct((ny, slab, nz), f32),
        scratch_shapes=[
            [pltpu.VMEM((slab * ny, LANE), f32)] * (nz // LANE),
            pltpu.VMEM((ny, slab, nz), f32),
            pltpu.SemaphoreType.DMA((2, slab // planes, nz // LANE)),
        ],
        compiler_params=pltpu.CompilerParams(vmem_limit_bytes=MOST_VMEM),
        cost_estimate=pl.CostEstimate(
            flops=0, bytes_accessed=8 * slab * ny * nz, transcendentals=0
        ),
    )(observed.reshape(slab * ny, nz))


def window_tiles(width, nz):
    return width * nz // (SUB * LANE)


def filter_kernel(first, halo, slab, *refs):
    cells, weights, xtab, refs = refs[:3] + (refs[3:],)
    devices, rows, _, nz = cells.shape
    nx = devices * slab
    half, quarter = nx // 2, nx // 4
    width = slab + 2 * halo
    blocks = nz // LANE
    if quarter == nz:
        ztable = (xtab[0, 0], xtab[1, 0])
    else:
        ztable, refs = (refs[0][0], refs[0][1]), refs[1:]
    if first:
        windows, kept, prior, high, low, padded = refs
    else:
        kept, windows, high, low, padded = refs

    def table(*places):
        return [jnp.concatenate([xtab[part, i] for i in places], axis=1) for part in range(2)]

    def store(spot, value):
        high[spot], low[spot] = split(value)

    def load(spot):
        return high[spot], low[spot]

    parts = [slice(i * quarter, (i + 1) * quarter) for i in range(4)]
    folds = [parts[0], parts[1], slice(half, nx)]
    for r in range(rows):
        q = [
            cells[i * devices // 4 : (i + 1) * devices // 4, r].reshape(quarter, nz)
            for i in range(4)
        ]
        even = (q[0] + q[2], q[1] + q[3])
        folded = (even[0] + even[1], even[0] - even[1], q[0] - q[2], q[1] - q[3])
        for spot, value in zip(parts, folded):
            store(spot, dot3(split(value), ztable))
        waves = [dot3(table(i), load(folds[i])) for i in range(2)]
        waves += [dot3(table(2 + 2 * i, 3 + 2 * i), load(folds[2])) for i in range(2)]
        for spot, wave in zip(parts, waves):
            if first:
                response = weights[spot]
                gain = (1.0 / (nx * nz)) / (response * response + 1.0)
                prior[spot] = gain
                wave = wave * (UNIT * gain)
                seen = wave * response
                kept[r, spot] = seen
                store(spot, seen + wave)
            else:
                store(spot, kept[r, spot] + wave * weights[spot])
        after = (halo + nx) // SUB * SUB
        padded[:SUB] = jnp.zeros((SUB, nz), f32)
        padded[after : after + 2 * SUB] = jnp.zeros((2 * SUB, nz), f32)
        plus, minus = dot3(table(0), load(folds[0])), dot3(table(1), load(folds[1]))
        for i, e in enumerate((plus + minus, plus - minus)):
            o = dot3(table(2 + 2 * i, 3 + 2 * i), load(folds[2]))
            for j, value in ((i, e + o), (i + 2, e - o)):
                place = halo + j * quarter
                padded[place : place + quarter] = dot3(split(value), ztable)
        for device in range(devices):
            for g in range(width // SUB):
                spot = device * slab + SUB * g
                for k in range(blocks):
                    windows[device, r, g * blocks + k] = padded[
                        spot : spot + SUB, LANE * k : LANE * (k + 1)
                    ]
            rest = width % SUB
            spot = device * slab + width - rest
            for k in range(blocks if rest else 0):
                tile, row = width // SUB * blocks + k * rest // SUB, k * rest % SUB
                windows[device, r, tile, row : row + rest] = padded[
                    spot : spot + rest, LANE * k : LANE * (k + 1)
                ]


def run_filter(first, halo, cells, tables, weights, kept):
    devices, rows, slab, nz = cells.shape
    nx = devices * slab
    vmem = pl.BlockSpec(memory_space=pltpu.VMEM)
    operands = [cells, weights, *tables, *kept]
    tiles = window_tiles(slab + 2 * halo, nz)
    out_shape = [jax.ShapeDtypeStruct((devices, rows, tiles, SUB, LANE), f32)]
    if first:
        out_shape += [
            jax.ShapeDtypeStruct((rows, nx, nz), f32),
            jax.ShapeDtypeStruct((nx, nz), f32),
        ]
    return pl.pallas_call(
        functools.partial(filter_kernel, first, halo, slab),
        in_specs=[vmem] * len(operands),
        out_specs=[vmem] * len(out_shape),
        out_shape=out_shape,
        scratch_shapes=[
            pltpu.VMEM((nx, nz), bf16),
            pltpu.VMEM((nx, nz), bf16),
            pltpu.VMEM((nx + 3 * SUB, nz), f32),
        ],
        compiler_params=pltpu.CompilerParams(vmem_limit_bytes=24 * MIB),
        cost_estimate=pl.CostEstimate(
            flops=6 * rows * nx * nz * (2 * nz + nx),
            bytes_accessed=8 * rows * nx * nz,
            transcendentals=0,
        ),
    )(*operands)


def lane_sums(pieces):
    lane = lax.broadcasted_iota(jnp.int32, pieces[0].shape, 1)
    up = [pltpu.roll(piece, LANE - 1, 1) for piece in pieces]
    down = [pltpu.roll(piece, 1, 1) for piece in pieces]
    sums = []
    for k in range(len(pieces)):
        above = up[k + 1] if k + 1 < len(pieces) else 0.0
        below = down[k - 1] if k > 0 else 0.0
        sums.append(
            jnp.where(lane == LANE - 1, above, up[k]) + jnp.where(lane == 0, below, down[k])
        )
    return sums


def row_sums(groups):
    return inner_row_sums([groups[-1]] + groups + [groups[0]])


def inner_row_sums(groups):
    row = lax.broadcasted_iota(jnp.int32, groups[0].shape, 0)
    up = [pltpu.roll(group, SUB - 1, 0) for group in groups]
    down = [pltpu.roll(group, 1, 0) for group in groups]
    return [
        jnp.where(row == SUB - 1, up[g + 1], up[g]) + jnp.where(row == 0, down[g - 1], down[g])
        for g in range(1, len(groups) - 1)
    ]


def passes_kernel(first, last, halo, slab, nx, target, *refs):
    if first:
        duals_in, refs = None, refs
    else:
        duals_in, refs = refs[:3], refs[3:]
    if last:
        restored, refs = refs[0], refs[1:]
    else:
        current, duals_out, refs = refs[0], refs[1:4], refs[4:]
    lead, field, dual_x, dual_y, dual_z = refs[:5]
    turned = refs[5:-1] if last else ()
    ny, _, nz = field.shape
    width = slab + 2 * halo
    groups = padded_to(width, SUB) // SUB
    blocks = nz // LANE
    decay = 1.0 / (1.0 + step_dual * huber_eps / bound_dual)
    gain = step_dual * decay
    floor = 1.0 / (decay * decay)
    keep = 1.0 / (1.0 + step_primal)
    pull = step_primal * keep
    push = pull * gain / decay
    origin = lax.axis_index("gy") * slab - halo

    def goal_of(y, g, k):
        if SUB * (g + 1) <= width:
            return target[y, g * blocks + k]
        rest = width % SUB
        tail = target[y, g * blocks + k * rest // SUB]
        shift = k * rest % SUB
        return pltpu.roll(tail, SUB - shift, 0) if shift else tail

    inside = {}
    for g in range(groups):
        if SUB * g < halo or SUB * (g + 1) > width - halo:
            place = origin + SUB * g + lax.broadcasted_iota(jnp.int32, (SUB, LANE), 0)
            inside[g] = jnp.where((place >= 0) & (place < nx), 1.0, 0.0)

    def masked(value, g):
        return value * inside[g] if g in inside else value

    def hand_on(which, y, g, k, value):
        shift = halo - HALO_LAST
        lo = max(0, shift - SUB * g)
        hi = min(SUB, slab + 2 * HALO_LAST + shift - SUB * g)
        if lo < hi:
            rows = pl.ds(SUB * g + lo - shift, hi - lo)
            duals_out[which][y, rows, pl.ds(LANE * k, LANE)] = value[lo:hi]

    centre_groups = [g for g in range(groups) if SUB * (g + 1) > halo and SUB * g < width - halo]

    def at(g, k):
        return pl.ds(SUB * g, SUB), pl.ds(LANE * k, LANE)

    empty = jnp.zeros(lead.shape[1:], f32)
    for plane in (0, ny + 1):
        lead[plane] = empty
        dual_y[plane] = empty

    @pl.loop(0, ny, unroll=UNROLL)
    def _(y):
        for g in range(groups):
            for k in range(blocks):
                lead[(y + 1,) + at(g, k)] = goal_of(y, g, k)

    leaving = []
    for sweep in range(PASSES):
        final = sweep == PASSES - 1

        @pl.loop(0, ny, unroll=UNROLL)
        def _(y):
            here = [[lead[(y + 1,) + at(g, k)] for k in range(blocks)] for g in range(groups)]
            columns = [row_sums([here[g][k] for g in range(groups)]) for k in range(blocks)]
            for g in range(groups):
                along_z = lane_sums(here[g])
                for k in range(blocks):
                    spot = at(g, k)
                    twice = here[g][k] + here[g][k]
                    along_y = lead[(y,) + spot] + lead[(y + 2,) + spot]
                    raised = [columns[k][g] - twice, along_y - twice, along_z[k] - twice]
                    if sweep > 0:
                        before = [dual_x[(y,) + spot], dual_y[(y + 1,) + spot], dual_z[(y,) + spot]]
                    elif duals_in is not None:
                        before = [ref[(y,) + spot] for ref in duals_in]
                    else:
                        before = None
                    if before is not None:
                        raised = [old + new for old, new in zip(before, raised)]
                    total = (
                        raised[0] * raised[0] + raised[1] * raised[1] + raised[2] * raised[2]
                    )
                    shrink = lax.rsqrt(jnp.maximum(floor, total))
                    made = [raised[0] * masked(shrink, g), raised[1] * shrink, raised[2] * shrink]
                    dual_x[(y,) + spot] = made[0]
                    dual_y[(y + 1,) + spot] = made[1]
                    dual_z[(y,) + spot] = made[2]
                    if final and not last:
                        for a in (0,) if g in centre_groups else (0, 1, 2):
                            hand_on(a, y, g, k, made[a])

        wanted = centre_groups if final else list(range(groups))
        column = COLUMN if final and last else len(wanted)
        for some in [wanted[i : i + column] for i in range(0, len(wanted), column)]:

            @pl.loop(0, ny, unroll=UNROLL)
            def _(y):
                around = [some[0] - 1] + some + [some[-1] + 1]
                near = {
                    g: [dual_x[(y,) + at(g % groups, k)] for k in range(blocks)] for g in around
                }
                columns = [inner_row_sums([near[g][k] for g in around]) for k in range(blocks)]
                for place, g in enumerate(some):
                    here = [dual_z[(y,) + at(g, k)] for k in range(blocks)]
                    along_z = lane_sums(here)
                    for k in range(blocks):
                        spot = at(g, k)
                        along_y = dual_y[(y,) + spot] + dual_y[(y + 2,) + spot]
                        middle = dual_y[(y + 1,) + spot]
                        if final and not last:
                            hand_on(1, y, g, k, middle)
                            hand_on(2, y, g, k, here[k])
                        centre = near[g][k] + middle + here[k]
                        adjoint = columns[k][place] + along_y + along_z[k] - (centre + centre)
                        goal = goal_of(y, g, k)
                        if sweep == 0:
                            move = push * adjoint
                            updated = goal - move
                            ahead = updated - move
                        else:
                            old = field[(y,) + spot]
                            whole = UNIT if final and last else 1.0
                            updated = (keep / whole) * old + (pull / whole) * goal
                            updated = updated - (push / whole) * adjoint
                            ahead = updated + updated - old
                        if not final:
                            field[(y,) + spot] = updated
                            lead[(y + 1,) + spot] = masked(ahead, g)
                            continue
                        lo = max(0, halo - SUB * g)
                        hi = min(SUB, slab + halo - SUB * g)
                        x = SUB * g + lo - halo
                        if last:
                            turned[k][pl.ds(x * ny + y, hi - lo, stride=ny), :] = updated[lo:hi]
                        else:
                            current[y, pl.ds(x, hi - lo), spot[1]] = updated[lo:hi]

            if final and last:
                low = max(0, SUB * some[0] - halo) * ny
                high = min(slab, SUB * (some[-1] + 1) - halo) * ny
                for k, block in enumerate(turned):
                    copy = pltpu.make_async_copy(
                        block.at[pl.ds(low, high - low), :],
                        restored.at[pl.ds(low, high - low), pl.ds(LANE * k, LANE)],
                        refs[-1].at[len(leaving)],
                    )
                    copy.start()
                    leaving.append(copy)

    for copy in leaving:
        copy.wait()


def run_passes(first, last, halo, slab, nx, target, duals):
    ny = target.shape[0]
    nz = target.shape[1] * SUB * LANE // (slab + 2 * halo)
    width = padded_to(slab + 2 * halo, SUB)
    vmem = pl.BlockSpec(memory_space=pltpu.VMEM)
    if last:
        out_shape = jax.ShapeDtypeStruct((slab * ny, nz), f32)
        out_specs = pl.BlockSpec(memory_space=pltpu.HBM)
    else:
        kept = jax.ShapeDtypeStruct((ny, slab + 2 * HALO_LAST, nz), f32)
        out_shape = [jax.ShapeDtypeStruct((ny, slab, nz), f32), kept, kept, kept]
        out_specs = [vmem] * 4
    return pl.pallas_call(
        functools.partial(passes_kernel, first, last, halo, slab, nx),
        in_specs=[vmem] * (1 + len(duals)),
        out_specs=out_specs,
        out_shape=out_shape,
        scratch_shapes=[
            pltpu.VMEM((ny + 2, width, nz), f32),
            pltpu.VMEM((ny, width, nz), f32),
            pltpu.VMEM((ny, width, nz), f32),
            pltpu.VMEM((ny + 2, width, nz), f32),
            pltpu.VMEM((ny, width, nz), f32),
        ]
        + [pltpu.VMEM((slab * ny, LANE), f32)] * (nz // LANE if last else 0)
        + [pltpu.SemaphoreType.DMA((nz // LANE * width // SUB,))] * last,
        compiler_params=pltpu.CompilerParams(vmem_limit_bytes=40 * MIB),
        cost_estimate=pl.CostEstimate(
            flops=60 * PASSES * ny * width * nz,
            bytes_accessed=8 * 4 * ny * width * nz,
            transcendentals=PASSES * ny * width * nz,
        ),
    )(target, *duals)


def exchange(blocks):
    return lax.all_to_all(blocks, "gy", split_axis=0, concat_axis=0, tiled=True)


def local(observed, tf_table, tilt_index, wedge):
    slab, ny, nz = observed.shape
    devices = lax.axis_size("gy")
    rows = ny // devices
    nx = slab * devices
    tables = [jnp.asarray(x_tables(nx))]
    if nx != 4 * nz:
        tables.append(jnp.asarray(z_table(nz)))
    cells = exchange(turn(observed).reshape(devices, rows, slab, nz))
    weights = make_response(tf_table, tilt_index, wedge, nx, nz)
    duals, kept = (), ()
    for outer in range(OUTER):
        first, last = outer == 0, outer == OUTER - 1
        halo = HALO_LAST if last else HALO_FIRST
        made = run_filter(first, halo, cells, tables, weights, kept)
        if first:
            kept, weights = (made[1],), made[2]
        windows = exchange(made[0])
        target = windows.reshape((ny,) + windows.shape[2:])
        made = run_passes(first, last, halo, slab, nx, target, duals)
        if last:
            return made.reshape(slab, ny, nz)
        duals = tuple(made[1:])
        cells = exchange(made[0].reshape(devices, rows, slab, nz))


def solution(mesh):
    in_specs = (P(("groups", "gy"), None, None), P(), P(), P())
    out_specs = P(("groups", "gy"), None, None)
    return jax.shard_map(local, mesh=mesh, in_specs=in_specs, out_specs=out_specs, check_vma=False)
```

```python
import functools

import jax
import jax.numpy as jnp
import ml_dtypes
import numpy as np
from jax import lax
from jax.experimental import pallas as pl
from jax.experimental.pallas import tpu as pltpu
from jax.sharding import PartitionSpec as P

OUTER = 2
PASSES = 2

step_dual = 0.14
step_primal = 0.14
huber_eps = 0.05
bound_dual = 0.5

SUB = 8
LANE = 128
HALO_LAST = 2 * PASSES
HALO_FIRST = HALO_LAST + 2 * PASSES - 2
UNROLL = 16
COLUMN = 4
MIB = 1024 * 1024
MOST_VMEM = 61 * MIB

f32 = jnp.float32
bf16 = jnp.bfloat16

UNIT = step_dual / bound_dual


def halves(table):
    high = table.astype(ml_dtypes.bfloat16)
    low = (table - high.astype(np.float64)).astype(ml_dtypes.bfloat16)
    return np.stack([high, low])


def cas(rows, columns, length):
    phase = (rows[:, None] * columns[None, :]) % length
    angle = phase * (2.0 * np.pi / length)
    return np.cos(angle) + np.sin(angle)


def z_table(length):
    index = np.arange(length)
    return halves(cas(index, index, length))


def x_tables(length):
    half, quarter = length // 2, length // 4
    place = np.arange(half)
    fourth = cas(4 * place[:quarter], place[:quarter], length)
    second = cas(4 * place[:quarter] + 2, 2 * place[:quarter] + 1, 2 * length)
    odd = cas(2 * place + 1, 2 * place + 1, 2 * length)
    blocks = [fourth, second]
    for rows in (slice(0, quarter), slice(quarter, half)):
        blocks += [odd[rows, :quarter], odd[rows, quarter:]]
    return halves(np.stack(blocks))


def kx_rows(length):
    half, quarter = length // 2, length // 4
    return ((0, quarter, 4, 0), (quarter, quarter, 4, 2), (half, half, 2, 1))


def padded_to(length, unit):
    return -(-length // unit) * unit


def response_kernel(nx, nz, levels, table_ref, code_ref, response):
    heights, widths = code_ref.shape
    kz = lax.broadcasted_iota(jnp.int32, (heights, nz), 1)
    kz = jnp.minimum(kz, nz - kz)
    pick_z = jnp.where(kz == lax.broadcasted_iota(jnp.int32, (heights, nz), 0), 1.0, 0.0)
    pick_z = pick_z.astype(bf16)
    for base, count, step, least in kx_rows(nx):
        tile = min(256, count)
        for top in range(0, count, tile):
            kx = step * (top + lax.broadcasted_iota(jnp.int32, (tile, widths), 0)) + least
            kx = jnp.minimum(kx, nx - kx)
            pick_x = jnp.where(kx == lax.broadcasted_iota(jnp.int32, (tile, widths), 1), 1.0, 0.0)
            tall = lax.dot_general(
                pick_x.astype(bf16),
                code_ref[...],
                (((1,), (1,)), ((), ())),
                preferred_element_type=f32,
            )
            spread = jnp.dot(tall.astype(bf16), pick_z, preferred_element_type=f32)
            value = jnp.zeros_like(spread)
            for level in range(levels):
                value = jnp.where(spread == level + 1.0, table_ref[level], value)
            response[base + top : base + top + tile] = value


def make_response(tf_table, tilt_index, wedge, nx, nz):
    levels = tf_table.shape[0]
    code = jnp.where(wedge > 0, tilt_index + 1, 0).T
    extra = [(0, padded_to(size, LANE) - size) for size in code.shape]
    code = jnp.pad(code, extra).astype(bf16)
    vmem = pl.BlockSpec(memory_space=pltpu.VMEM)
    return pl.pallas_call(
        functools.partial(response_kernel, nx, nz, levels),
        in_specs=[pl.BlockSpec(memory_space=pltpu.SMEM), vmem],
        out_specs=vmem,
        out_shape=jax.ShapeDtypeStruct((nx, nz), f32),
        compiler_params=pltpu.CompilerParams(vmem_limit_bytes=16 * MIB),
        cost_estimate=pl.CostEstimate(
            flops=60000 * nx * nz, bytes_accessed=4 * nx * nz, transcendentals=0
        ),
    )(tf_table, code)


def split(value):
    high = value.astype(bf16)
    return high, (value - high.astype(f32)).astype(bf16)


def dot3(a, b):
    wide = jnp.concatenate([a[0], a[0], a[1]], axis=1)
    tall = jnp.concatenate([b[0], b[1], b[0]], axis=0)
    return jnp.dot(wide, tall, preferred_element_type=f32)


def turn_kernel(ny, planes, cells, turned, staged, placed, semaphores):
    blocks = len(staged)
    steps = placed.shape[1] // planes
    rows = planes * ny
    incoming = [
        [
            pltpu.make_async_copy(
                cells.at[pl.ds(step * rows, rows), pl.ds(LANE * k, LANE)],
                staged[k].at[pl.ds(step * rows, rows), :],
                semaphores.at[0, step, k],
            )
            for k in range(blocks)
        ]
        for step in range(steps)
    ]
    outgoing = [
        pltpu.make_async_copy(
            placed.at[:, pl.ds(step * planes, planes), :],
            turned.at[:, pl.ds(step * planes, planes), :],
            semaphores.at[1, step, 0],
        )
        for step in range(steps)
    ]
    for step in range(steps):
        for copy in incoming[step]:
            copy.start()
    for step in range(steps):
        for copy in incoming[step]:
            copy.wait()
        for y in range(ny):
            for x in range(step * planes, (step + 1) * planes, SUB):
                for k in range(blocks):
                    placed[y, x : x + SUB, LANE * k : LANE * (k + 1)] = staged[k][
                        pl.ds(x * ny + y, SUB, stride=ny), :
                    ]
        outgoing[step].start()
    for copy in outgoing:
        copy.wait()


def turn(observed):
    slab, ny, nz = observed.shape
    planes = SUB
    anywhere = pl.BlockSpec(memory_space=pltpu.HBM)
    return pl.pallas_call(
        functools.partial(turn_kernel, ny, planes),
        in_specs=[anywhere],
        out_specs=anywhere,
        out_shape=jax.ShapeDtypeStruct((ny, slab, nz), f32),
        scratch_shapes=[
            [pltpu.VMEM((slab * ny, LANE), f32)] * (nz // LANE),
            pltpu.VMEM((ny, slab, nz), f32),
            pltpu.SemaphoreType.DMA((2, slab // planes, nz // LANE)),
        ],
        compiler_params=pltpu.CompilerParams(vmem_limit_bytes=MOST_VMEM),
        cost_estimate=pl.CostEstimate(
            flops=0, bytes_accessed=8 * slab * ny * nz, transcendentals=0
        ),
    )(observed.reshape(slab * ny, nz))


def window_tiles(width, nz):
    return width * nz // (SUB * LANE)


def filter_kernel(first, opens, closes, halo, slab, *refs):
    if opens:
        cells, refs = refs[0], refs[1:]
        devices, rows, _, nz = cells.shape
    else:
        arrived, refs = refs[0], refs[1:]
        rows, nz = arrived.shape[0], arrived.shape[2]
        devices = arrived.shape[1] // slab
    nx = devices * slab
    if closes:
        weights, refs = refs[0], refs[1:]
    xtab, refs = refs[0], refs[1:]
    half, quarter = nx // 2, nx // 4
    width = slab + 2 * halo
    blocks = nz // LANE
    if quarter == nz:
        ztable = (xtab[0, 0], xtab[1, 0])
    else:
        ztable, refs = (refs[0][0], refs[0][1]), refs[1:]
    if not closes:
        leaving, high, low, padded = refs
    elif first:
        windows, kept, prior, high, low, padded = refs
    else:
        kept, windows, high, low, padded = refs

    def table(*places):
        return [jnp.concatenate([xtab[part, i] for i in places], axis=1) for part in range(2)]

    def store(spot, value):
        high[spot], low[spot] = split(value)

    def load(spot):
        return high[spot], low[spot]

    parts = [slice(i * quarter, (i + 1) * quarter) for i in range(4)]
    folds = [parts[0], parts[1], slice(half, nx)]
    for r in range(rows):
        if opens:
            q = [
                cells[i * devices // 4 : (i + 1) * devices // 4, r].reshape(quarter, nz)
                for i in range(4)
            ]
            even = (q[0] + q[2], q[1] + q[3])
            folded = (even[0] + even[1], even[0] - even[1], q[0] - q[2], q[1] - q[3])
            for spot, value in zip(parts, folded):
                store(spot, dot3(split(value), ztable))
            waves = [dot3(table(i), load(folds[i])) for i in range(2)]
            waves += [dot3(table(2 + 2 * i, 3 + 2 * i), load(folds[2])) for i in range(2)]
        else:
            waves = [arrived[r, spot] for spot in parts]
        if not closes:
            for spot, wave in zip(parts, waves):
                leaving[r, spot] = wave
            continue
        for spot, wave in zip(parts, waves):
            if first:
                response = weights[spot]
                gain = (1.0 / (nx * nz)) / (response * response + 1.0)
                prior[spot] = gain
                wave = wave * (UNIT * gain)
                seen = wave * response
                kept[r, spot] = seen
                store(spot, seen + wave)
            else:
                store(spot, kept[r, spot] + wave * weights[spot])
        after = (halo + nx) // SUB * SUB
        padded[:SUB] = jnp.zeros((SUB, nz), f32)
        padded[after : after + 2 * SUB] = jnp.zeros((2 * SUB, nz), f32)
        plus, minus = dot3(table(0), load(folds[0])), dot3(table(1), load(folds[1]))
        for i, e in enumerate((plus + minus, plus - minus)):
            o = dot3(table(2 + 2 * i, 3 + 2 * i), load(folds[2]))
            for j, value in ((i, e + o), (i + 2, e - o)):
                place = halo + j * quarter
                padded[place : place + quarter] = dot3(split(value), ztable)
        for device in range(devices):
            for g in range(width // SUB):
                spot = device * slab + SUB * g
                for k in range(blocks):
                    windows[device, r, g * blocks + k] = padded[
                        spot : spot + SUB, LANE * k : LANE * (k + 1)
                    ]
            rest = width % SUB
            spot = device * slab + width - rest
            for k in range(blocks if rest else 0):
                tile, row = width // SUB * blocks + k * rest // SUB, k * rest % SUB
                windows[device, r, tile, row : row + rest] = padded[
                    spot : spot + rest, LANE * k : LANE * (k + 1)
                ]


def run_filter(first, opens, closes, halo, slab, source, weights, tables, kept):
    if opens:
        devices, rows, _, nz = source.shape
    else:
        devices, rows, nz = source.shape[1] // slab, source.shape[0], source.shape[2]
    nx = devices * slab
    vmem = pl.BlockSpec(memory_space=pltpu.VMEM)
    waves = jax.ShapeDtypeStruct((rows, nx, nz), f32)
    tiles = window_tiles(slab + 2 * halo, nz)
    if closes:
        operands = [source, weights, *tables, *kept]
        out_shape = [jax.ShapeDtypeStruct((devices, rows, tiles, SUB, LANE), f32)]
        if first:
            out_shape += [waves, jax.ShapeDtypeStruct((nx, nz), f32)]
    else:
        operands, out_shape = [source, *tables], [waves]
    share = (opens + closes) / 2
    return pl.pallas_call(
        functools.partial(filter_kernel, first, opens, closes, halo, slab),
        in_specs=[vmem] * len(operands),
        out_specs=[vmem] * len(out_shape),
        out_shape=out_shape,
        scratch_shapes=[
            pltpu.VMEM((nx, nz), bf16),
            pltpu.VMEM((nx, nz), bf16),
            pltpu.VMEM((nx + 3 * SUB, nz), f32),
        ],
        compiler_params=pltpu.CompilerParams(vmem_limit_bytes=24 * MIB),
        cost_estimate=pl.CostEstimate(
            flops=int(share * 6 * rows * nx * nz * (2 * nz + nx)),
            bytes_accessed=8 * rows * nx * nz,
            transcendentals=0,
        ),
    )(*operands)


def lane_sums(pieces):
    lane = lax.broadcasted_iota(jnp.int32, pieces[0].shape, 1)
    up = [pltpu.roll(piece, LANE - 1, 1) for piece in pieces]
    down = [pltpu.roll(piece, 1, 1) for piece in pieces]
    sums = []
    for k in range(len(pieces)):
        above = up[k + 1] if k + 1 < len(pieces) else 0.0
        below = down[k - 1] if k > 0 else 0.0
        sums.append(
            jnp.where(lane == LANE - 1, above, up[k]) + jnp.where(lane == 0, below, down[k])
        )
    return sums


def row_sums(groups):
    return inner_row_sums([groups[-1]] + groups + [groups[0]])


def inner_row_sums(groups):
    row = lax.broadcasted_iota(jnp.int32, groups[0].shape, 0)
    up = [pltpu.roll(group, SUB - 1, 0) for group in groups]
    down = [pltpu.roll(group, 1, 0) for group in groups]
    return [
        jnp.where(row == SUB - 1, up[g + 1], up[g]) + jnp.where(row == 0, down[g - 1], down[g])
        for g in range(1, len(groups) - 1)
    ]


def each_plane(count):
    def run(body):
        if count <= UNROLL:
            for y in range(count):
                body(y)
        else:
            pl.loop(0, count, unroll=UNROLL)(body)

    return run


def passes_kernel(first, last, halo, slab, nx, target, *refs):
    if first:
        duals_in, refs = None, refs
    else:
        duals_in, refs = refs[:3], refs[3:]
    if last:
        restored, refs = refs[0], refs[1:]
    else:
        current, duals_out, refs = refs[0], refs[1:4], refs[4:]
    lead, field, dual_x, dual_y, dual_z = refs[:5]
    turned = refs[5:-1] if last else ()
    ny, _, nz = field.shape
    width = slab + 2 * halo
    groups = padded_to(width, SUB) // SUB
    blocks = nz // LANE
    decay = 1.0 / (1.0 + step_dual * huber_eps / bound_dual)
    gain = step_dual * decay
    floor = 1.0 / (decay * decay)
    keep = 1.0 / (1.0 + step_primal)
    pull = step_primal * keep
    push = pull * gain / decay
    origin = lax.axis_index("gy") * slab - halo

    def goal_of(y, g, k):
        if SUB * (g + 1) <= width:
            return target[y, g * blocks + k]
        rest = width % SUB
        tail = target[y, g * blocks + k * rest // SUB]
        shift = k * rest % SUB
        return pltpu.roll(tail, SUB - shift, 0) if shift else tail

    inside = {}
    for g in range(groups):
        if SUB * g < halo or SUB * (g + 1) > width - halo:
            place = origin + SUB * g + lax.broadcasted_iota(jnp.int32, (SUB, LANE), 0)
            inside[g] = jnp.where((place >= 0) & (place < nx), 1.0, 0.0)

    def masked(value, g):
        return value * inside[g] if g in inside else value

    def hand_on(which, y, g, k, value):
        shift = halo - HALO_LAST
        lo = max(0, shift - SUB * g)
        hi = min(SUB, slab + 2 * HALO_LAST + shift - SUB * g)
        if lo < hi:
            rows = pl.ds(SUB * g + lo - shift, hi - lo)
            duals_out[which][y, rows, pl.ds(LANE * k, LANE)] = value[lo:hi]

    centre_groups = [g for g in range(groups) if SUB * (g + 1) > halo and SUB * g < width - halo]

    def at(g, k):
        return pl.ds(SUB * g, SUB), pl.ds(LANE * k, LANE)

    empty = jnp.zeros(lead.shape[1:], f32)
    for plane in (0, ny + 1):
        lead[plane] = empty
        dual_y[plane] = empty

    written_out = ny <= UNROLL
    if not written_out:

        @each_plane(ny)
        def _(y):
            for g in range(groups):
                for k in range(blocks):
                    lead[(y + 1,) + at(g, k)] = goal_of(y, g, k)

    def lead_of(sweep, y, g, k):
        if sweep == 0 and written_out:
            return goal_of(y, g, k) if 0 <= y < ny else jnp.zeros((SUB, LANE), f32)
        return lead[(y + 1,) + at(g, k)]

    leaving = []
    for sweep in range(PASSES):
        final = sweep == PASSES - 1

        @each_plane(ny)
        def _(y):
            here = [[lead_of(sweep, y, g, k) for k in range(blocks)] for g in range(groups)]
            columns = [row_sums([here[g][k] for g in range(groups)]) for k in range(blocks)]
            for g in range(groups):
                along_z = lane_sums(here[g])
                for k in range(blocks):
                    spot = at(g, k)
                    twice = here[g][k] + here[g][k]
                    along_y = lead_of(sweep, y - 1, g, k) + lead_of(sweep, y + 1, g, k)
                    raised = [columns[k][g] - twice, along_y - twice, along_z[k] - twice]
                    if sweep > 0:
                        before = [dual_x[(y,) + spot], dual_y[(y + 1,) + spot], dual_z[(y,) + spot]]
                    elif duals_in is not None:
                        before = [ref[(y,) + spot] for ref in duals_in]
                    else:
                        before = None
                    if before is not None:
                        raised = [old + new for old, new in zip(before, raised)]
                    total = (
                        raised[0] * raised[0] + raised[1] * raised[1] + raised[2] * raised[2]
                    )
                    shrink = lax.rsqrt(jnp.maximum(floor, total))
                    made = [raised[0] * masked(shrink, g), raised[1] * shrink, raised[2] * shrink]
                    dual_x[(y,) + spot] = made[0]
                    dual_y[(y + 1,) + spot] = made[1]
                    dual_z[(y,) + spot] = made[2]
                    if final and not last:
                        for a in (0,) if g in centre_groups else (0, 1, 2):
                            hand_on(a, y, g, k, made[a])

        wanted = centre_groups if final else list(range(groups))
        column = COLUMN if final and last else len(wanted)
        for some in [wanted[i : i + column] for i in range(0, len(wanted), column)]:

            @each_plane(ny)
            def _(y):
                around = [some[0] - 1] + some + [some[-1] + 1]
                near = {
                    g: [dual_x[(y,) + at(g % groups, k)] for k in range(blocks)] for g in around
                }
                columns = [inner_row_sums([near[g][k] for g in around]) for k in range(blocks)]
                for place, g in enumerate(some):
                    here = [dual_z[(y,) + at(g, k)] for k in range(blocks)]
                    along_z = lane_sums(here)
                    for k in range(blocks):
                        spot = at(g, k)
                        along_y = dual_y[(y,) + spot] + dual_y[(y + 2,) + spot]
                        middle = dual_y[(y + 1,) + spot]
                        if final and not last:
                            hand_on(1, y, g, k, middle)
                            hand_on(2, y, g, k, here[k])
                        centre = near[g][k] + middle + here[k]
                        adjoint = columns[k][place] + along_y + along_z[k] - (centre + centre)
                        goal = goal_of(y, g, k)
                        if sweep == 0:
                            move = push * adjoint
                            updated = goal - move
                            ahead = updated - move
                        else:
                            old = field[(y,) + spot]
                            whole = UNIT if final and last else 1.0
                            updated = (keep / whole) * old + (pull / whole) * goal
                            updated = updated - (push / whole) * adjoint
                            ahead = updated + updated - old
                        if not final:
                            field[(y,) + spot] = updated
                            lead[(y + 1,) + spot] = masked(ahead, g)
                            continue
                        lo = max(0, halo - SUB * g)
                        hi = min(SUB, slab + halo - SUB * g)
                        x = SUB * g + lo - halo
                        if last:
                            turned[k][pl.ds(x * ny + y, hi - lo, stride=ny), :] = updated[lo:hi]
                        else:
                            current[y, pl.ds(x, hi - lo), spot[1]] = updated[lo:hi]

            if final and last:
                low = max(0, SUB * some[0] - halo) * ny
                high = min(slab, SUB * (some[-1] + 1) - halo) * ny
                for k, block in enumerate(turned):
                    copy = pltpu.make_async_copy(
                        block.at[pl.ds(low, high - low), :],
                        restored.at[pl.ds(low, high - low), pl.ds(LANE * k, LANE)],
                        refs[-1].at[len(leaving)],
                    )
                    copy.start()
                    leaving.append(copy)

    for copy in leaving:
        copy.wait()


def run_passes(first, last, halo, slab, nx, target, duals):
    ny = target.shape[0]
    nz = target.shape[1] * SUB * LANE // (slab + 2 * halo)
    width = padded_to(slab + 2 * halo, SUB)
    vmem = pl.BlockSpec(memory_space=pltpu.VMEM)
    if last:
        out_shape = jax.ShapeDtypeStruct((slab * ny, nz), f32)
        out_specs = pl.BlockSpec(memory_space=pltpu.HBM)
    else:
        kept = jax.ShapeDtypeStruct((ny, slab + 2 * HALO_LAST, nz), f32)
        out_shape = [jax.ShapeDtypeStruct((ny, slab, nz), f32), kept, kept, kept]
        out_specs = [vmem] * 4
    return pl.pallas_call(
        functools.partial(passes_kernel, first, last, halo, slab, nx),
        in_specs=[vmem] * (1 + len(duals)),
        out_specs=out_specs,
        out_shape=out_shape,
        scratch_shapes=[
            pltpu.VMEM((ny + 2, width, nz), f32),
            pltpu.VMEM((ny, width, nz), f32),
            pltpu.VMEM((ny, width, nz), f32),
            pltpu.VMEM((ny + 2, width, nz), f32),
            pltpu.VMEM((ny, width, nz), f32),
        ]
        + [pltpu.VMEM((slab * ny, LANE), f32)] * (nz // LANE if last else 0)
        + [pltpu.SemaphoreType.DMA((nz // LANE * width // SUB,))] * last,
        compiler_params=pltpu.CompilerParams(vmem_limit_bytes=40 * MIB),
        cost_estimate=pl.CostEstimate(
            flops=60 * PASSES * ny * width * nz,
            bytes_accessed=8 * 4 * ny * width * nz,
            transcendentals=PASSES * ny * width * nz,
        ),
    )(target, *duals)


def exchange(blocks):
    return lax.all_to_all(blocks, "gy", split_axis=0, concat_axis=0, tiled=True)


def local(observed, tf_table, tilt_index, wedge):
    slab, ny, nz = observed.shape
    devices = lax.axis_size("gy")
    rows = ny // devices
    nx = slab * devices
    tables = [jnp.asarray(x_tables(nx))]
    if nx != 4 * nz:
        tables.append(jnp.asarray(z_table(nz)))
    cells = exchange(turn(observed).reshape(devices, rows, slab, nz))
    weights = make_response(tf_table, tilt_index, wedge, nx, nz)
    duals, kept = (), ()
    for outer in range(OUTER):
        first, last = outer == 0, outer == OUTER - 1
        halo = HALO_LAST if last else HALO_FIRST
        if first:
            (cells,) = run_filter(True, True, False, halo, slab, cells, None, tables, kept)
        made = run_filter(first, not first, True, halo, slab, cells, weights, tables, kept)
        if first:
            kept, weights = (made[1],), made[2]
        windows = exchange(made[0])
        target = windows.reshape((ny,) + windows.shape[2:])
        made = run_passes(first, last, halo, slab, nx, target, duals)
        if last:
            return made.reshape(slab, ny, nz)
        duals = tuple(made[1:])
        cells = exchange(made[0].reshape(devices, rows, slab, nz))


def solution(mesh):
    in_specs = (P(("groups", "gy"), None, None), P(), P(), P())
    out_specs = P(("groups", "gy"), None, None)
    return jax.shard_map(local, mesh=mesh, in_specs=in_specs, out_specs=out_specs, check_vma=False)
```

```python
import functools

import jax
import jax.numpy as jnp
import ml_dtypes
import numpy as np
from jax import lax
from jax.experimental import pallas as pl
from jax.experimental.pallas import tpu as pltpu
from jax.sharding import PartitionSpec as P

OUTER = 2
PASSES = 2

step_dual = 0.14
step_primal = 0.14
huber_eps = 0.05
bound_dual = 0.5

SUB = 8
LANE = 128
HALO_LAST = 2 * PASSES
HALO_FIRST = HALO_LAST + 2 * PASSES - 2
UNROLL = 16
COLUMN = 4
MIB = 1024 * 1024
MOST_VMEM = 61 * MIB

f32 = jnp.float32
bf16 = jnp.bfloat16

UNIT = step_dual / bound_dual


def halves(table):
    high = table.astype(ml_dtypes.bfloat16)
    low = (table - high.astype(np.float64)).astype(ml_dtypes.bfloat16)
    return np.stack([high, low])


def cas(rows, columns, length):
    phase = (rows[:, None] * columns[None, :]) % length
    angle = phase * (2.0 * np.pi / length)
    return np.cos(angle) + np.sin(angle)


def z_table(length):
    index = np.arange(length)
    return halves(cas(index, index, length))


def x_tables(length):
    half, quarter = length // 2, length // 4
    place = np.arange(half)
    fourth = cas(4 * place[:quarter], place[:quarter], length)
    second = cas(4 * place[:quarter] + 2, 2 * place[:quarter] + 1, 2 * length)
    odd = cas(2 * place + 1, 2 * place + 1, 2 * length)
    blocks = [fourth, second]
    for rows in (slice(0, quarter), slice(quarter, half)):
        blocks += [odd[rows, :quarter], odd[rows, quarter:]]
    return halves(np.stack(blocks))


def kx_rows(length):
    half, quarter = length // 2, length // 4
    return ((0, quarter, 4, 0), (quarter, quarter, 4, 2), (half, half, 2, 1))


def padded_to(length, unit):
    return -(-length // unit) * unit


def response_kernel(nx, nz, levels, table_ref, code_ref, response):
    heights, widths = code_ref.shape
    kz = lax.broadcasted_iota(jnp.int32, (heights, nz), 1)
    kz = jnp.minimum(kz, nz - kz)
    pick_z = jnp.where(kz == lax.broadcasted_iota(jnp.int32, (heights, nz), 0), 1.0, 0.0)
    pick_z = pick_z.astype(bf16)
    for base, count, step, least in kx_rows(nx):
        tile = min(256, count)
        for top in range(0, count, tile):
            kx = step * (top + lax.broadcasted_iota(jnp.int32, (tile, widths), 0)) + least
            kx = jnp.minimum(kx, nx - kx)
            pick_x = jnp.where(kx == lax.broadcasted_iota(jnp.int32, (tile, widths), 1), 1.0, 0.0)
            tall = lax.dot_general(
                pick_x.astype(bf16),
                code_ref[...],
                (((1,), (1,)), ((), ())),
                preferred_element_type=f32,
            )
            spread = jnp.dot(tall.astype(bf16), pick_z, preferred_element_type=f32)
            value = jnp.zeros_like(spread)
            for level in range(levels):
                value = jnp.where(spread == level + 1.0, table_ref[level], value)
            response[base + top : base + top + tile] = value


def make_response(tf_table, tilt_index, wedge, nx, nz):
    levels = tf_table.shape[0]
    code = jnp.where(wedge > 0, tilt_index + 1, 0).T
    extra = [(0, padded_to(size, LANE) - size) for size in code.shape]
    code = jnp.pad(code, extra).astype(bf16)
    vmem = pl.BlockSpec(memory_space=pltpu.VMEM)
    return pl.pallas_call(
        functools.partial(response_kernel, nx, nz, levels),
        in_specs=[pl.BlockSpec(memory_space=pltpu.SMEM), vmem],
        out_specs=vmem,
        out_shape=jax.ShapeDtypeStruct((nx, nz), f32),
        compiler_params=pltpu.CompilerParams(vmem_limit_bytes=16 * MIB),
        cost_estimate=pl.CostEstimate(
            flops=60000 * nx * nz, bytes_accessed=4 * nx * nz, transcendentals=0
        ),
    )(tf_table, code)


def split(value):
    high = value.astype(bf16)
    return high, (value - high.astype(f32)).astype(bf16)


def dot3(a, b):
    wide = jnp.concatenate([a[0], a[0], a[1]], axis=1)
    tall = jnp.concatenate([b[0], b[1], b[0]], axis=0)
    return jnp.dot(wide, tall, preferred_element_type=f32)


def turn_kernel(ny, planes, cells, turned, staged, placed, semaphores):
    blocks = len(staged)
    steps = placed.shape[1] // planes
    rows = planes * ny
    incoming = [
        [
            pltpu.make_async_copy(
                cells.at[pl.ds(step * rows, rows), pl.ds(LANE * k, LANE)],
                staged[k].at[pl.ds(step * rows, rows), :],
                semaphores.at[0, step, k],
            )
            for k in range(blocks)
        ]
        for step in range(steps)
    ]
    outgoing = [
        pltpu.make_async_copy(
            placed.at[:, pl.ds(step * planes, planes), :],
            turned.at[:, pl.ds(step * planes, planes), :],
            semaphores.at[1, step, 0],
        )
        for step in range(steps)
    ]
    for step in range(steps):
        for copy in incoming[step]:
            copy.start()
    for step in range(steps):
        for copy in incoming[step]:
            copy.wait()
        for x in range(step * planes, (step + 1) * planes, SUB):
            for k in range(blocks):
                block = staged[k][x * ny : (x + SUB) * ny].reshape(SUB, ny, LANE)
                placed[:, x : x + SUB, LANE * k : LANE * (k + 1)] = jnp.swapaxes(block, 0, 1)
        outgoing[step].start()
    for copy in outgoing:
        copy.wait()


def turn(observed):
    slab, ny, nz = observed.shape
    planes = SUB
    anywhere = pl.BlockSpec(memory_space=pltpu.HBM)
    return pl.pallas_call(
        functools.partial(turn_kernel, ny, planes),
        in_specs=[anywhere],
        out_specs=anywhere,
        out_shape=jax.ShapeDtypeStruct((ny, slab, nz), f32),
        scratch_shapes=[
            [pltpu.VMEM((slab * ny, LANE), f32)] * (nz // LANE),
            pltpu.VMEM((ny, slab, nz), f32),
            pltpu.SemaphoreType.DMA((2, slab // planes, nz // LANE)),
        ],
        compiler_params=pltpu.CompilerParams(vmem_limit_bytes=MOST_VMEM),
        cost_estimate=pl.CostEstimate(
            flops=0, bytes_accessed=8 * slab * ny * nz, transcendentals=0
        ),
    )(observed.reshape(slab * ny, nz))


def window_tiles(width, nz):
    return width * nz // (SUB * LANE)


def filter_kernel(first, opens, closes, halo, slab, *refs):
    if opens:
        cells, refs = refs[0], refs[1:]
        devices, rows, _, nz = cells.shape
    else:
        arrived, refs = refs[0], refs[1:]
        rows, nz = arrived.shape[0], arrived.shape[2]
        devices = arrived.shape[1] // slab
    nx = devices * slab
    if closes:
        weights, refs = refs[0], refs[1:]
    xtab, refs = refs[0], refs[1:]
    half, quarter = nx // 2, nx // 4
    width = slab + 2 * halo
    blocks = nz // LANE
    if quarter == nz:
        ztable = (xtab[0, 0], xtab[1, 0])
    else:
        ztable, refs = (refs[0][0], refs[0][1]), refs[1:]
    if not closes:
        leaving, high, low, padded = refs
    elif first:
        windows, kept, prior, high, low, padded = refs
    else:
        kept, windows, high, low, padded = refs

    def table(*places):
        return [jnp.concatenate([xtab[part, i] for i in places], axis=1) for part in range(2)]

    def store(spot, value):
        high[spot], low[spot] = split(value)

    def load(spot):
        return high[spot], low[spot]

    parts = [slice(i * quarter, (i + 1) * quarter) for i in range(4)]
    folds = [parts[0], parts[1], slice(half, nx)]
    for r in range(rows):
        if opens:
            q = [
                cells[i * devices // 4 : (i + 1) * devices // 4, r].reshape(quarter, nz)
                for i in range(4)
            ]
            even = (q[0] + q[2], q[1] + q[3])
            folded = (even[0] + even[1], even[0] - even[1], q[0] - q[2], q[1] - q[3])
            for spot, value in zip(parts, folded):
                store(spot, dot3(split(value), ztable))
            waves = [dot3(table(i), load(folds[i])) for i in range(2)]
            waves += [dot3(table(2 + 2 * i, 3 + 2 * i), load(folds[2])) for i in range(2)]
        else:
            waves = [arrived[r, spot] for spot in parts]
        if not closes:
            for spot, wave in zip(parts, waves):
                leaving[r, spot] = wave
            continue
        for spot, wave in zip(parts, waves):
            if first:
                response = weights[spot]
                gain = (1.0 / (nx * nz)) / (response * response + 1.0)
                prior[spot] = gain
                wave = wave * (UNIT * gain)
                seen = wave * response
                kept[r, spot] = seen
                store(spot, seen + wave)
            else:
                store(spot, kept[r, spot] + wave * weights[spot])
        after = (halo + nx) // SUB * SUB
        padded[:SUB] = jnp.zeros((SUB, nz), f32)
        padded[after : after + 2 * SUB] = jnp.zeros((2 * SUB, nz), f32)
        plus, minus = dot3(table(0), load(folds[0])), dot3(table(1), load(folds[1]))
        for i, e in enumerate((plus + minus, plus - minus)):
            o = dot3(table(2 + 2 * i, 3 + 2 * i), load(folds[2]))
            for j, value in ((i, e + o), (i + 2, e - o)):
                place = halo + j * quarter
                padded[place : place + quarter] = dot3(split(value), ztable)
        for device in range(devices):
            for g in range(width // SUB):
                spot = device * slab + SUB * g
                for k in range(blocks):
                    windows[device, r, g * blocks + k] = padded[
                        spot : spot + SUB, LANE * k : LANE * (k + 1)
                    ]
            rest = width % SUB
            spot = device * slab + width - rest
            for k in range(blocks if rest else 0):
                tile, row = width // SUB * blocks + k * rest // SUB, k * rest % SUB
                windows[device, r, tile, row : row + rest] = padded[
                    spot : spot + rest, LANE * k : LANE * (k + 1)
                ]


def run_filter(first, opens, closes, halo, slab, source, weights, tables, kept):
    if opens:
        devices, rows, _, nz = source.shape
    else:
        devices, rows, nz = source.shape[1] // slab, source.shape[0], source.shape[2]
    nx = devices * slab
    vmem = pl.BlockSpec(memory_space=pltpu.VMEM)
    waves = jax.ShapeDtypeStruct((rows, nx, nz), f32)
    tiles = window_tiles(slab + 2 * halo, nz)
    if closes:
        operands = [source, weights, *tables, *kept]
        out_shape = [jax.ShapeDtypeStruct((devices, rows, tiles, SUB, LANE), f32)]
        if first:
            out_shape += [waves, jax.ShapeDtypeStruct((nx, nz), f32)]
    else:
        operands, out_shape = [source, *tables], [waves]
    share = (opens + closes) / 2
    return pl.pallas_call(
        functools.partial(filter_kernel, first, opens, closes, halo, slab),
        in_specs=[vmem] * len(operands),
        out_specs=[vmem] * len(out_shape),
        out_shape=out_shape,
        scratch_shapes=[
            pltpu.VMEM((nx, nz), bf16),
            pltpu.VMEM((nx, nz), bf16),
            pltpu.VMEM((nx + 3 * SUB, nz), f32),
        ],
        compiler_params=pltpu.CompilerParams(vmem_limit_bytes=24 * MIB),
        cost_estimate=pl.CostEstimate(
            flops=int(share * 6 * rows * nx * nz * (2 * nz + nx)),
            bytes_accessed=8 * rows * nx * nz,
            transcendentals=0,
        ),
    )(*operands)


def lane_sums(pieces):
    lane = lax.broadcasted_iota(jnp.int32, pieces[0].shape, 1)
    up = [pltpu.roll(piece, LANE - 1, 1) for piece in pieces]
    down = [pltpu.roll(piece, 1, 1) for piece in pieces]
    sums = []
    for k in range(len(pieces)):
        above = up[k + 1] if k + 1 < len(pieces) else 0.0
        below = down[k - 1] if k > 0 else 0.0
        sums.append(
            jnp.where(lane == LANE - 1, above, up[k]) + jnp.where(lane == 0, below, down[k])
        )
    return sums


def row_sums(groups):
    return inner_row_sums([groups[-1]] + groups + [groups[0]])


def inner_row_sums(groups):
    row = lax.broadcasted_iota(jnp.int32, groups[0].shape, 0)
    up = [pltpu.roll(group, SUB - 1, 0) for group in groups]
    down = [pltpu.roll(group, 1, 0) for group in groups]
    return [
        jnp.where(row == SUB - 1, up[g + 1], up[g]) + jnp.where(row == 0, down[g - 1], down[g])
        for g in range(1, len(groups) - 1)
    ]


def each_plane(count):
    def run(body):
        if count <= UNROLL:
            for y in range(count):
                body(y)
        else:
            pl.loop(0, count, unroll=UNROLL)(body)

    return run


def passes_kernel(first, last, halo, slab, nx, target, *refs):
    if first:
        duals_in, refs = None, refs
    else:
        duals_in, refs = refs[:3], refs[3:]
    if last:
        restored, refs = refs[0], refs[1:]
    else:
        current, duals_out, refs = refs[0], refs[1:4], refs[4:]
    lead, field, dual_x, dual_y, dual_z = refs[:5]
    if last:
        placed, turned, semaphores = refs[5:]
    ny, _, nz = field.shape
    width = slab + 2 * halo
    groups = padded_to(width, SUB) // SUB
    blocks = nz // LANE
    decay = 1.0 / (1.0 + step_dual * huber_eps / bound_dual)
    gain = step_dual * decay
    floor = 1.0 / (decay * decay)
    keep = 1.0 / (1.0 + step_primal)
    pull = step_primal * keep
    push = pull * gain / decay
    origin = lax.axis_index("gy") * slab - halo

    def goal_of(y, g, k):
        if SUB * (g + 1) <= width:
            return target[y, g * blocks + k]
        rest = width % SUB
        tail = target[y, g * blocks + k * rest // SUB]
        shift = k * rest % SUB
        return pltpu.roll(tail, SUB - shift, 0) if shift else tail

    inside = {}
    for g in range(groups):
        if SUB * g < halo or SUB * (g + 1) > width - halo:
            place = origin + SUB * g + lax.broadcasted_iota(jnp.int32, (SUB, LANE), 0)
            inside[g] = jnp.where((place >= 0) & (place < nx), 1.0, 0.0)

    def masked(value, g):
        return value * inside[g] if g in inside else value

    def hand_on(which, y, g, k, value):
        shift = halo - HALO_LAST
        lo = max(0, shift - SUB * g)
        hi = min(SUB, slab + 2 * HALO_LAST + shift - SUB * g)
        if lo < hi:
            rows = pl.ds(SUB * g + lo - shift, hi - lo)
            duals_out[which][y, rows, pl.ds(LANE * k, LANE)] = value[lo:hi]

    centre_groups = [g for g in range(groups) if SUB * (g + 1) > halo and SUB * g < width - halo]

    def at(g, k):
        return pl.ds(SUB * g, SUB), pl.ds(LANE * k, LANE)

    empty = jnp.zeros(lead.shape[1:], f32)
    for plane in (0, ny + 1):
        lead[plane] = empty
        dual_y[plane] = empty

    written_out = ny <= UNROLL
    if not written_out:

        @each_plane(ny)
        def _(y):
            for g in range(groups):
                for k in range(blocks):
                    lead[(y + 1,) + at(g, k)] = goal_of(y, g, k)

    def lead_of(sweep, y, g, k):
        if sweep == 0 and written_out:
            return goal_of(y, g, k) if 0 <= y < ny else jnp.zeros((SUB, LANE), f32)
        return lead[(y + 1,) + at(g, k)]

    leaving, gone = [], 0
    for sweep in range(PASSES):
        final = sweep == PASSES - 1

        @each_plane(ny)
        def _(y):
            here = [[lead_of(sweep, y, g, k) for k in range(blocks)] for g in range(groups)]
            columns = [row_sums([here[g][k] for g in range(groups)]) for k in range(blocks)]
            for g in range(groups):
                along_z = lane_sums(here[g])
                for k in range(blocks):
                    spot = at(g, k)
                    twice = here[g][k] + here[g][k]
                    along_y = lead_of(sweep, y - 1, g, k) + lead_of(sweep, y + 1, g, k)
                    raised = [columns[k][g] - twice, along_y - twice, along_z[k] - twice]
                    if sweep > 0:
                        before = [dual_x[(y,) + spot], dual_y[(y + 1,) + spot], dual_z[(y,) + spot]]
                    elif duals_in is not None:
                        before = [ref[(y,) + spot] for ref in duals_in]
                    else:
                        before = None
                    if before is not None:
                        raised = [old + new for old, new in zip(before, raised)]
                    total = (
                        raised[0] * raised[0] + raised[1] * raised[1] + raised[2] * raised[2]
                    )
                    shrink = lax.rsqrt(jnp.maximum(floor, total))
                    made = [raised[0] * masked(shrink, g), raised[1] * shrink, raised[2] * shrink]
                    dual_x[(y,) + spot] = made[0]
                    dual_y[(y + 1,) + spot] = made[1]
                    dual_z[(y,) + spot] = made[2]
                    if final and not last:
                        for a in (0,) if g in centre_groups else (0, 1, 2):
                            hand_on(a, y, g, k, made[a])

        wanted = centre_groups if final else list(range(groups))
        column = COLUMN if final and last else len(wanted)
        for some in [wanted[i : i + column] for i in range(0, len(wanted), column)]:

            @each_plane(ny)
            def _(y):
                around = [some[0] - 1] + some + [some[-1] + 1]
                near = {
                    g: [dual_x[(y,) + at(g % groups, k)] for k in range(blocks)] for g in around
                }
                columns = [inner_row_sums([near[g][k] for g in around]) for k in range(blocks)]
                for place, g in enumerate(some):
                    here = [dual_z[(y,) + at(g, k)] for k in range(blocks)]
                    along_z = lane_sums(here)
                    for k in range(blocks):
                        spot = at(g, k)
                        along_y = dual_y[(y,) + spot] + dual_y[(y + 2,) + spot]
                        middle = dual_y[(y + 1,) + spot]
                        if final and not last:
                            hand_on(1, y, g, k, middle)
                            hand_on(2, y, g, k, here[k])
                        centre = near[g][k] + middle + here[k]
                        adjoint = columns[k][place] + along_y + along_z[k] - (centre + centre)
                        goal = goal_of(y, g, k)
                        if sweep == 0:
                            move = push * adjoint
                            updated = goal - move
                            ahead = updated - move
                        else:
                            old = field[(y,) + spot]
                            whole = UNIT if final and last else 1.0
                            updated = (keep / whole) * old + (pull / whole) * goal
                            updated = updated - (push / whole) * adjoint
                            ahead = updated + updated - old
                        if not final:
                            field[(y,) + spot] = updated
                            lead[(y + 1,) + spot] = masked(ahead, g)
                            continue
                        lo = max(0, halo - SUB * g)
                        hi = min(SUB, slab + halo - SUB * g)
                        x = SUB * g + lo - halo
                        if last:
                            placed[y, pl.ds(x, hi - lo), spot[1]] = updated[lo:hi]
                        else:
                            current[y, pl.ds(x, hi - lo), spot[1]] = updated[lo:hi]

            if final and last:
                ready = min(slab, SUB * (some[-1] + 1) - halo) // SUB * SUB
                for x in range(gone, ready, SUB):
                    for k in range(blocks):
                        lanes = pl.ds(LANE * k, LANE)
                        block = jnp.swapaxes(placed[:, pl.ds(x, SUB), lanes], 0, 1)
                        turned[pl.ds(x * ny, SUB * ny), lanes] = block.reshape(SUB * ny, LANE)
                if ready > gone:
                    rows = pl.ds(gone * ny, (ready - gone) * ny)
                    copy = pltpu.make_async_copy(
                        turned.at[rows, :], restored.at[rows, :], semaphores.at[len(leaving)]
                    )
                    copy.start()
                    leaving.append(copy)
                gone = ready

    for copy in leaving:
        copy.wait()


def run_passes(first, last, halo, slab, nx, target, duals):
    ny = target.shape[0]
    nz = target.shape[1] * SUB * LANE // (slab + 2 * halo)
    width = padded_to(slab + 2 * halo, SUB)
    vmem = pl.BlockSpec(memory_space=pltpu.VMEM)
    if last:
        out_shape = jax.ShapeDtypeStruct((slab * ny, nz), f32)
        out_specs = pl.BlockSpec(memory_space=pltpu.HBM)
    else:
        kept = jax.ShapeDtypeStruct((ny, slab + 2 * HALO_LAST, nz), f32)
        out_shape = [jax.ShapeDtypeStruct((ny, slab, nz), f32), kept, kept, kept]
        out_specs = [vmem] * 4
    return pl.pallas_call(
        functools.partial(passes_kernel, first, last, halo, slab, nx),
        in_specs=[vmem] * (1 + len(duals)),
        out_specs=out_specs,
        out_shape=out_shape,
        scratch_shapes=[
            pltpu.VMEM((ny + 2, width, nz), f32),
            pltpu.VMEM((ny, width, nz), f32),
            pltpu.VMEM((ny, width, nz), f32),
            pltpu.VMEM((ny + 2, width, nz), f32),
            pltpu.VMEM((ny, width, nz), f32),
        ]
        + [
            pltpu.VMEM((ny, slab, nz), f32),
            pltpu.VMEM((slab * ny, nz), f32),
            pltpu.SemaphoreType.DMA((width // SUB,)),
        ]
        * last,
        compiler_params=pltpu.CompilerParams(vmem_limit_bytes=40 * MIB),
        cost_estimate=pl.CostEstimate(
            flops=60 * PASSES * ny * width * nz,
            bytes_accessed=8 * 4 * ny * width * nz,
            transcendentals=PASSES * ny * width * nz,
        ),
    )(target, *duals)


def exchange(blocks):
    return lax.all_to_all(blocks, "gy", split_axis=0, concat_axis=0, tiled=True)


def local(observed, tf_table, tilt_index, wedge):
    slab, ny, nz = observed.shape
    devices = lax.axis_size("gy")
    rows = ny // devices
    nx = slab * devices
    tables = [jnp.asarray(x_tables(nx))]
    if nx != 4 * nz:
        tables.append(jnp.asarray(z_table(nz)))
    cells = exchange(turn(observed).reshape(devices, rows, slab, nz))
    weights = make_response(tf_table, tilt_index, wedge, nx, nz)
    duals, kept = (), ()
    for outer in range(OUTER):
        first, last = outer == 0, outer == OUTER - 1
        halo = HALO_LAST if last else HALO_FIRST
        if first:
            (cells,) = run_filter(True, True, False, halo, slab, cells, None, tables, kept)
        made = run_filter(first, not first, True, halo, slab, cells, weights, tables, kept)
        if first:
            kept, weights = (made[1],), made[2]
        windows = exchange(made[0])
        target = windows.reshape((ny,) + windows.shape[2:])
        made = run_passes(first, last, halo, slab, nx, target, duals)
        if last:
            return made.reshape(slab, ny, nz)
        duals = tuple(made[1:])
        cells = exchange(made[0].reshape(devices, rows, slab, nz))


def solution(mesh):
    in_specs = (P(("groups", "gy"), None, None), P(), P(), P())
    out_specs = P(("groups", "gy"), None, None)
    return jax.shard_map(local, mesh=mesh, in_specs=in_specs, out_specs=out_specs, check_vma=False)
```

```python
import functools

import jax
import jax.numpy as jnp
import ml_dtypes
import numpy as np
from jax import lax
from jax.experimental import pallas as pl
from jax.experimental.pallas import tpu as pltpu
from jax.sharding import PartitionSpec as P

OUTER = 2
PASSES = 2

step_dual = 0.14
step_primal = 0.14
huber_eps = 0.05
bound_dual = 0.5

SUB = 8
LANE = 128
HALO_LAST = 2 * PASSES
HALO_FIRST = HALO_LAST + 2 * PASSES - 2
UNROLL = 16
COLUMN = 4
MIB = 1024 * 1024
MOST_VMEM = 61 * MIB

f32 = jnp.float32
bf16 = jnp.bfloat16

UNIT = step_dual / bound_dual


def halves(table):
    high = table.astype(ml_dtypes.bfloat16)
    low = (table - high.astype(np.float64)).astype(ml_dtypes.bfloat16)
    return np.stack([high, low])


def cas(rows, columns, length):
    phase = (rows[:, None] * columns[None, :]) % length
    angle = phase * (2.0 * np.pi / length)
    return np.cos(angle) + np.sin(angle)


def z_table(length):
    index = np.arange(length)
    return halves(cas(index, index, length))


def x_tables(length):
    half, quarter = length // 2, length // 4
    place = np.arange(half)
    fourth = cas(4 * place[:quarter], place[:quarter], length)
    second = cas(4 * place[:quarter] + 2, 2 * place[:quarter] + 1, 2 * length)
    odd = cas(2 * place + 1, 2 * place + 1, 2 * length)
    blocks = [fourth, second]
    for rows in (slice(0, quarter), slice(quarter, half)):
        blocks += [odd[rows, :quarter], odd[rows, quarter:]]
    return halves(np.stack(blocks))


def kx_rows(length):
    half, quarter = length // 2, length // 4
    return ((0, quarter, 4, 0), (quarter, quarter, 4, 2), (half, half, 2, 1))


def padded_to(length, unit):
    return -(-length // unit) * unit


def response_kernel(nx, nz, levels, table_ref, code_ref, response):
    heights, widths = code_ref.shape
    kz = lax.broadcasted_iota(jnp.int32, (heights, nz), 1)
    kz = jnp.minimum(kz, nz - kz)
    pick_z = jnp.where(kz == lax.broadcasted_iota(jnp.int32, (heights, nz), 0), 1.0, 0.0)
    pick_z = pick_z.astype(bf16)
    for base, count, step, least in kx_rows(nx):
        tile = min(256, count)
        for top in range(0, count, tile):
            kx = step * (top + lax.broadcasted_iota(jnp.int32, (tile, widths), 0)) + least
            kx = jnp.minimum(kx, nx - kx)
            pick_x = jnp.where(kx == lax.broadcasted_iota(jnp.int32, (tile, widths), 1), 1.0, 0.0)
            tall = lax.dot_general(
                pick_x.astype(bf16),
                code_ref[...],
                (((1,), (1,)), ((), ())),
                preferred_element_type=f32,
            )
            spread = jnp.dot(tall.astype(bf16), pick_z, preferred_element_type=f32)
            value = jnp.zeros_like(spread)
            for level in range(levels):
                value = jnp.where(spread == level + 1.0, table_ref[level], value)
            response[base + top : base + top + tile] = value


def make_response(tf_table, tilt_index, wedge, nx, nz):
    levels = tf_table.shape[0]
    code = jnp.where(wedge > 0, tilt_index + 1, 0).T
    extra = [(0, padded_to(size, LANE) - size) for size in code.shape]
    code = jnp.pad(code, extra).astype(bf16)
    vmem = pl.BlockSpec(memory_space=pltpu.VMEM)
    return pl.pallas_call(
        functools.partial(response_kernel, nx, nz, levels),
        in_specs=[pl.BlockSpec(memory_space=pltpu.SMEM), vmem],
        out_specs=vmem,
        out_shape=jax.ShapeDtypeStruct((nx, nz), f32),
        compiler_params=pltpu.CompilerParams(vmem_limit_bytes=16 * MIB),
        cost_estimate=pl.CostEstimate(
            flops=60000 * nx * nz, bytes_accessed=4 * nx * nz, transcendentals=0
        ),
    )(tf_table, code)


def split(value):
    high = value.astype(bf16)
    return high, (value - high.astype(f32)).astype(bf16)


def dot3(a, b):
    wide = jnp.concatenate([a[0], a[0], a[1]], axis=1)
    tall = jnp.concatenate([b[0], b[1], b[0]], axis=0)
    return jnp.dot(wide, tall, preferred_element_type=f32)


def turn_kernel(ny, planes, cells, turned, staged, placed, semaphores):
    slab, nz = placed.shape[1:]
    steps = slab // planes
    rows = planes * ny
    incoming = [
        pltpu.make_async_copy(
            cells.at[pl.ds(step * rows, rows), :],
            staged.at[pl.ds(step * rows, rows), :],
            semaphores.at[0, step],
        )
        for step in range(steps)
    ]
    outgoing = [
        pltpu.make_async_copy(
            placed.at[:, pl.ds(step * planes, planes), :],
            turned.at[:, pl.ds(step * planes, planes), :],
            semaphores.at[1, step],
        )
        for step in range(steps)
    ]
    for copy in incoming:
        copy.start()
    for step in range(steps):
        incoming[step].wait()
        for x in range(step * planes, (step + 1) * planes, SUB):
            for lane in range(0, nz, LANE):
                block = staged[x * ny : (x + SUB) * ny, lane : lane + LANE]
                block = jnp.swapaxes(block.reshape(SUB, ny, LANE), 0, 1)
                placed[:, x : x + SUB, lane : lane + LANE] = block
        outgoing[step].start()
    for copy in outgoing:
        copy.wait()


def turn(observed):
    slab, ny, nz = observed.shape
    planes = 2 * SUB if slab % (2 * SUB) == 0 else SUB
    anywhere = pl.BlockSpec(memory_space=pltpu.HBM)
    return pl.pallas_call(
        functools.partial(turn_kernel, ny, planes),
        in_specs=[anywhere],
        out_specs=anywhere,
        out_shape=jax.ShapeDtypeStruct((ny, slab, nz), f32),
        scratch_shapes=[
            pltpu.VMEM((slab * ny, nz), f32),
            pltpu.VMEM((ny, slab, nz), f32),
            pltpu.SemaphoreType.DMA((2, slab // planes)),
        ],
        compiler_params=pltpu.CompilerParams(vmem_limit_bytes=MOST_VMEM),
        cost_estimate=pl.CostEstimate(
            flops=0, bytes_accessed=8 * slab * ny * nz, transcendentals=0
        ),
    )(observed.reshape(slab * ny, nz))


def window_tiles(width, nz):
    return width * nz // (SUB * LANE)


def filter_kernel(first, opens, closes, halo, slab, *refs):
    if opens:
        cells, refs = refs[0], refs[1:]
        devices, rows, _, nz = cells.shape
    else:
        arrived, refs = refs[0], refs[1:]
        rows, nz = arrived.shape[0], arrived.shape[2]
        devices = arrived.shape[1] // slab
    nx = devices * slab
    if closes:
        weights, refs = refs[0], refs[1:]
    xtab, refs = refs[0], refs[1:]
    half, quarter = nx // 2, nx // 4
    width = slab + 2 * halo
    blocks = nz // LANE
    if quarter == nz:
        ztable = (xtab[0, 0], xtab[1, 0])
    else:
        ztable, refs = (refs[0][0], refs[0][1]), refs[1:]
    if not closes:
        leaving, high, low, padded = refs
    elif first:
        windows, kept, prior, high, low, padded = refs
    else:
        kept, windows, high, low, padded = refs

    def table(*places):
        return [jnp.concatenate([xtab[part, i] for i in places], axis=1) for part in range(2)]

    def store(spot, value):
        high[spot], low[spot] = split(value)

    def load(spot):
        return high[spot], low[spot]

    parts = [slice(i * quarter, (i + 1) * quarter) for i in range(4)]
    folds = [parts[0], parts[1], slice(half, nx)]
    for r in range(rows):
        if opens:
            q = [
                cells[i * devices // 4 : (i + 1) * devices // 4, r].reshape(quarter, nz)
                for i in range(4)
            ]
            even = (q[0] + q[2], q[1] + q[3])
            folded = (even[0] + even[1], even[0] - even[1], q[0] - q[2], q[1] - q[3])
            for spot, value in zip(parts, folded):
                store(spot, dot3(split(value), ztable))
            waves = [dot3(table(i), load(folds[i])) for i in range(2)]
            waves += [dot3(table(2 + 2 * i, 3 + 2 * i), load(folds[2])) for i in range(2)]
        else:
            waves = [arrived[r, spot] for spot in parts]
        if not closes:
            for spot, wave in zip(parts, waves):
                leaving[r, spot] = wave
            continue
        for spot, wave in zip(parts, waves):
            if first:
                response = weights[spot]
                gain = (1.0 / (nx * nz)) / (response * response + 1.0)
                prior[spot] = gain
                wave = wave * (UNIT * gain)
                seen = wave * response
                kept[r, spot] = seen
                store(spot, seen + wave)
            else:
                store(spot, kept[r, spot] + wave * weights[spot])
        after = (halo + nx) // SUB * SUB
        padded[:SUB] = jnp.zeros((SUB, nz), f32)
        padded[after : after + 2 * SUB] = jnp.zeros((2 * SUB, nz), f32)
        plus, minus = dot3(table(0), load(folds[0])), dot3(table(1), load(folds[1]))
        for i, e in enumerate((plus + minus, plus - minus)):
            o = dot3(table(2 + 2 * i, 3 + 2 * i), load(folds[2]))
            for j, value in ((i, e + o), (i + 2, e - o)):
                place = halo + j * quarter
                padded[place : place + quarter] = dot3(split(value), ztable)
        for device in range(devices):
            for g in range(width // SUB):
                spot = device * slab + SUB * g
                for k in range(blocks):
                    windows[device, r, g * blocks + k] = padded[
                        spot : spot + SUB, LANE * k : LANE * (k + 1)
                    ]
            rest = width % SUB
            spot = device * slab + width - rest
            for k in range(blocks if rest else 0):
                tile, row = width // SUB * blocks + k * rest // SUB, k * rest % SUB
                windows[device, r, tile, row : row + rest] = padded[
                    spot : spot + rest, LANE * k : LANE * (k + 1)
                ]


def run_filter(first, opens, closes, halo, slab, source, weights, tables, kept):
    if opens:
        devices, rows, _, nz = source.shape
    else:
        devices, rows, nz = source.shape[1] // slab, source.shape[0], source.shape[2]
    nx = devices * slab
    vmem = pl.BlockSpec(memory_space=pltpu.VMEM)
    waves = jax.ShapeDtypeStruct((rows, nx, nz), f32)
    tiles = window_tiles(slab + 2 * halo, nz)
    if closes:
        operands = [source, weights, *tables, *kept]
        out_shape = [jax.ShapeDtypeStruct((devices, rows, tiles, SUB, LANE), f32)]
        if first:
            out_shape += [waves, jax.ShapeDtypeStruct((nx, nz), f32)]
    else:
        operands, out_shape = [source, *tables], [waves]
    share = (opens + closes) / 2
    return pl.pallas_call(
        functools.partial(filter_kernel, first, opens, closes, halo, slab),
        in_specs=[vmem] * len(operands),
        out_specs=[vmem] * len(out_shape),
        out_shape=out_shape,
        scratch_shapes=[
            pltpu.VMEM((nx, nz), bf16),
            pltpu.VMEM((nx, nz), bf16),
            pltpu.VMEM((nx + 3 * SUB, nz), f32),
        ],
        compiler_params=pltpu.CompilerParams(vmem_limit_bytes=24 * MIB),
        cost_estimate=pl.CostEstimate(
            flops=int(share * 6 * rows * nx * nz * (2 * nz + nx)),
            bytes_accessed=8 * rows * nx * nz,
            transcendentals=0,
        ),
    )(*operands)


def lane_sums(pieces):
    lane = lax.broadcasted_iota(jnp.int32, pieces[0].shape, 1)
    up = [pltpu.roll(piece, LANE - 1, 1) for piece in pieces]
    down = [pltpu.roll(piece, 1, 1) for piece in pieces]
    sums = []
    for k in range(len(pieces)):
        above = up[k + 1] if k + 1 < len(pieces) else 0.0
        below = down[k - 1] if k > 0 else 0.0
        sums.append(
            jnp.where(lane == LANE - 1, above, up[k]) + jnp.where(lane == 0, below, down[k])
        )
    return sums


def row_sums(groups):
    return inner_row_sums([groups[-1]] + groups + [groups[0]])


def inner_row_sums(groups):
    row = lax.broadcasted_iota(jnp.int32, groups[0].shape, 0)
    up = [pltpu.roll(group, SUB - 1, 0) for group in groups]
    down = [pltpu.roll(group, 1, 0) for group in groups]
    return [
        jnp.where(row == SUB - 1, up[g + 1], up[g]) + jnp.where(row == 0, down[g - 1], down[g])
        for g in range(1, len(groups) - 1)
    ]


def each_plane(count):
    def run(body):
        if count <= UNROLL:
            for y in range(count):
                body(y)
        else:
            pl.loop(0, count, unroll=UNROLL)(body)

    return run


def passes_kernel(first, last, halo, slab, nx, target, *refs):
    if first:
        duals_in, refs = None, refs
    else:
        duals_in, refs = refs[:3], refs[3:]
    if last:
        restored, refs = refs[0], refs[1:]
    else:
        current, duals_out, refs = refs[0], refs[1:4], refs[4:]
    lead, field, dual_x, dual_y, dual_z = refs[:5]
    if last:
        placed, turned, semaphores = refs[5:]
    ny, _, nz = field.shape
    width = slab + 2 * halo
    groups = padded_to(width, SUB) // SUB
    blocks = nz // LANE
    decay = 1.0 / (1.0 + step_dual * huber_eps / bound_dual)
    gain = step_dual * decay
    floor = 1.0 / (decay * decay)
    keep = 1.0 / (1.0 + step_primal)
    pull = step_primal * keep
    push = pull * gain / decay
    origin = lax.axis_index("gy") * slab - halo

    def goal_of(y, g, k):
        if SUB * (g + 1) <= width:
            return target[y, g * blocks + k]
        rest = width % SUB
        tail = target[y, g * blocks + k * rest // SUB]
        shift = k * rest % SUB
        return pltpu.roll(tail, SUB - shift, 0) if shift else tail

    inside = {}
    for g in range(groups):
        if SUB * g < halo or SUB * (g + 1) > width - halo:
            place = origin + SUB * g + lax.broadcasted_iota(jnp.int32, (SUB, LANE), 0)
            inside[g] = jnp.where((place >= 0) & (place < nx), 1.0, 0.0)

    def masked(value, g):
        return value * inside[g] if g in inside else value

    def hand_on(which, y, g, k, value):
        shift = halo - HALO_LAST
        lo = max(0, shift - SUB * g)
        hi = min(SUB, slab + 2 * HALO_LAST + shift - SUB * g)
        if lo < hi:
            rows = pl.ds(SUB * g + lo - shift, hi - lo)
            duals_out[which][y, rows, pl.ds(LANE * k, LANE)] = value[lo:hi]

    centre_groups = [g for g in range(groups) if SUB * (g + 1) > halo and SUB * g < width - halo]

    def at(g, k):
        return pl.ds(SUB * g, SUB), pl.ds(LANE * k, LANE)

    empty = jnp.zeros(lead.shape[1:], f32)
    for plane in (0, ny + 1):
        lead[plane] = empty
        dual_y[plane] = empty

    written_out = ny <= UNROLL
    if not written_out:

        @each_plane(ny)
        def _(y):
            for g in range(groups):
                for k in range(blocks):
                    lead[(y + 1,) + at(g, k)] = goal_of(y, g, k)

    def lead_of(sweep, y, g, k):
        if sweep == 0 and written_out:
            return goal_of(y, g, k) if 0 <= y < ny else jnp.zeros((SUB, LANE), f32)
        return lead[(y + 1,) + at(g, k)]

    leaving, gone = [], 0
    for sweep in range(PASSES):
        final = sweep == PASSES - 1

        @each_plane(ny)
        def _(y):
            here = [[lead_of(sweep, y, g, k) for k in range(blocks)] for g in range(groups)]
            columns = [row_sums([here[g][k] for g in range(groups)]) for k in range(blocks)]
            for g in range(groups):
                along_z = lane_sums(here[g])
                for k in range(blocks):
                    spot = at(g, k)
                    twice = here[g][k] + here[g][k]
                    along_y = lead_of(sweep, y - 1, g, k) + lead_of(sweep, y + 1, g, k)
                    raised = [columns[k][g] - twice, along_y - twice, along_z[k] - twice]
                    if sweep > 0:
                        before = [dual_x[(y,) + spot], dual_y[(y + 1,) + spot], dual_z[(y,) + spot]]
                    elif duals_in is not None:
                        before = [ref[(y,) + spot] for ref in duals_in]
                    else:
                        before = None
                    if before is not None:
                        raised = [old + new for old, new in zip(before, raised)]
                    total = (
                        raised[0] * raised[0] + raised[1] * raised[1] + raised[2] * raised[2]
                    )
                    shrink = lax.rsqrt(jnp.maximum(floor, total))
                    made = [raised[0] * masked(shrink, g), raised[1] * shrink, raised[2] * shrink]
                    dual_x[(y,) + spot] = made[0]
                    dual_y[(y + 1,) + spot] = made[1]
                    dual_z[(y,) + spot] = made[2]
                    if final and not last:
                        for a in (0,) if g in centre_groups else (0, 1, 2):
                            hand_on(a, y, g, k, made[a])

        wanted = centre_groups if final else list(range(groups))
        column = COLUMN if final and last else len(wanted)
        for some in [wanted[i : i + column] for i in range(0, len(wanted), column)]:

            @each_plane(ny)
            def _(y):
                around = [some[0] - 1] + some + [some[-1] + 1]
                near = {
                    g: [dual_x[(y,) + at(g % groups, k)] for k in range(blocks)] for g in around
                }
                columns = [inner_row_sums([near[g][k] for g in around]) for k in range(blocks)]
                for place, g in enumerate(some):
                    here = [dual_z[(y,) + at(g, k)] for k in range(blocks)]
                    along_z = lane_sums(here)
                    for k in range(blocks):
                        spot = at(g, k)
                        along_y = dual_y[(y,) + spot] + dual_y[(y + 2,) + spot]
                        middle = dual_y[(y + 1,) + spot]
                        if final and not last:
                            hand_on(1, y, g, k, middle)
                            hand_on(2, y, g, k, here[k])
                        centre = near[g][k] + middle + here[k]
                        adjoint = columns[k][place] + along_y + along_z[k] - (centre + centre)
                        goal = goal_of(y, g, k)
                        if sweep == 0:
                            move = push * adjoint
                            updated = goal - move
                            ahead = updated - move
                        else:
                            old = field[(y,) + spot]
                            whole = UNIT if final and last else 1.0
                            updated = (keep / whole) * old + (pull / whole) * goal
                            updated = updated - (push / whole) * adjoint
                            ahead = updated + updated - old
                        if not final:
                            field[(y,) + spot] = updated
                            lead[(y + 1,) + spot] = masked(ahead, g)
                            continue
                        lo = max(0, halo - SUB * g)
                        hi = min(SUB, slab + halo - SUB * g)
                        x = SUB * g + lo - halo
                        if last:
                            placed[y, pl.ds(x, hi - lo), spot[1]] = updated[lo:hi]
                        else:
                            current[y, pl.ds(x, hi - lo), spot[1]] = updated[lo:hi]

            if final and last:
                ready = min(slab, SUB * (some[-1] + 1) - halo) // SUB * SUB
                for x in range(gone, ready, SUB):
                    for k in range(blocks):
                        lanes = pl.ds(LANE * k, LANE)
                        block = jnp.swapaxes(placed[:, pl.ds(x, SUB), lanes], 0, 1)
                        turned[pl.ds(x * ny, SUB * ny), lanes] = block.reshape(SUB * ny, LANE)
                if ready > gone:
                    rows = pl.ds(gone * ny, (ready - gone) * ny)
                    copy = pltpu.make_async_copy(
                        turned.at[rows, :], restored.at[rows, :], semaphores.at[len(leaving)]
                    )
                    copy.start()
                    leaving.append(copy)
                gone = ready

    for copy in leaving:
        copy.wait()


def run_passes(first, last, halo, slab, nx, target, duals):
    ny = target.shape[0]
    nz = target.shape[1] * SUB * LANE // (slab + 2 * halo)
    width = padded_to(slab + 2 * halo, SUB)
    vmem = pl.BlockSpec(memory_space=pltpu.VMEM)
    if last:
        out_shape = jax.ShapeDtypeStruct((slab * ny, nz), f32)
        out_specs = pl.BlockSpec(memory_space=pltpu.HBM)
    else:
        kept = jax.ShapeDtypeStruct((ny, slab + 2 * HALO_LAST, nz), f32)
        out_shape = [jax.ShapeDtypeStruct((ny, slab, nz), f32), kept, kept, kept]
        out_specs = [vmem] * 4
    return pl.pallas_call(
        functools.partial(passes_kernel, first, last, halo, slab, nx),
        in_specs=[vmem] * (1 + len(duals)),
        out_specs=out_specs,
        out_shape=out_shape,
        scratch_shapes=[
            pltpu.VMEM((ny + 2, width, nz), f32),
            pltpu.VMEM((ny, width, nz), f32),
            pltpu.VMEM((ny, width, nz), f32),
            pltpu.VMEM((ny + 2, width, nz), f32),
            pltpu.VMEM((ny, width, nz), f32),
        ]
        + [
            pltpu.VMEM((ny, slab, nz), f32),
            pltpu.VMEM((slab * ny, nz), f32),
            pltpu.SemaphoreType.DMA((width // SUB,)),
        ]
        * last,
        compiler_params=pltpu.CompilerParams(vmem_limit_bytes=40 * MIB),
        cost_estimate=pl.CostEstimate(
            flops=60 * PASSES * ny * width * nz,
            bytes_accessed=8 * 4 * ny * width * nz,
            transcendentals=PASSES * ny * width * nz,
        ),
    )(target, *duals)


def exchange(blocks):
    return lax.all_to_all(blocks, "gy", split_axis=0, concat_axis=0, tiled=True)


def local(observed, tf_table, tilt_index, wedge):
    slab, ny, nz = observed.shape
    devices = lax.axis_size("gy")
    rows = ny // devices
    nx = slab * devices
    tables = [jnp.asarray(x_tables(nx))]
    if nx != 4 * nz:
        tables.append(jnp.asarray(z_table(nz)))
    cells = exchange(turn(observed).reshape(devices, rows, slab, nz))
    weights = make_response(tf_table, tilt_index, wedge, nx, nz)
    duals, kept = (), ()
    for outer in range(OUTER):
        first, last = outer == 0, outer == OUTER - 1
        halo = HALO_LAST if last else HALO_FIRST
        if first:
            (cells,) = run_filter(True, True, False, halo, slab, cells, None, tables, kept)
        made = run_filter(first, not first, True, halo, slab, cells, weights, tables, kept)
        if first:
            kept, weights = (made[1],), made[2]
        windows = exchange(made[0])
        target = windows.reshape((ny,) + windows.shape[2:])
        made = run_passes(first, last, halo, slab, nx, target, duals)
        if last:
            return made.reshape(slab, ny, nz)
        duals = tuple(made[1:])
        cells = exchange(made[0].reshape(devices, rows, slab, nz))


def solution(mesh):
    in_specs = (P(("groups", "gy"), None, None), P(), P(), P())
    out_specs = P(("groups", "gy"), None, None)
    return jax.shard_map(local, mesh=mesh, in_specs=in_specs, out_specs=out_specs, check_vma=False)
```
